32 devices in a mesh: tm: 4 (over z), height: 8 (over y, x, core).
Axes of the slice: x: 2, y: 2, z: 4, core: 2. Of those that a mesh axis runs over, the one named last changes fastest.
Arguments:
- tokens: bfloat16 [8, 16, 64, 1536], P('tm', 'height'), may hold values from -6 to 6
- norm_gain: float32 [1536], replicated, may hold values from 0.5 to 1.5
- in_weight: bfloat16 [1536, 3072], replicated, may hold values from -0.15625 to 0.15625
- bc_weight: bfloat16 [1536, 512], replicated, may hold values from -0.15625 to 0.15625
- dt_weight: bfloat16 [1536, 48], replicated, may hold values from -0.15625 to 0.15625
- dt_bias: float32 [48], replicated, may hold values from -1 to 1
- decay_rate: float32 [2, 24], replicated, may hold values from 0.0006510417 to 0.05
- out_gain: float32 [1536], replicated, may hold values from 0.5 to 1.5
- out_weight: bfloat16 [1536, 1536], replicated, may hold values from -0.15625 to 0.15625
Outputs:
- mixed: bfloat16 [8, 16, 64, 1536], P('tm', 'height')
The draws below stay inside these ranges and needn't reach their ends.
All inputs are finite; a program needn't handle non-finite values.
Results may differ from the reference program's by a relative error of at most 0.02.
Values may be sent and summed in bfloat16 or wider, within the bound.
No kernel may reach another device: no remote copies, remote signals or barrier semaphores. Data moves between devices by JAX's collectives and lax.ppermute only.
A program may use at most 192 MiB of HBM per device.

```python
import math
import jax
import jax.numpy as jnp
from jax import lax

D = 1536
HEADS = 24
HEAD_DIM = 64
STATE = 128
W = 64
INNER = 1536
FRAMES = 8
ROWS = 16


def steps_of(own_key, extent, split, low, top_value):
    loudness = 1.0
    for dim, parts in split:
        draws = jax.random.uniform(jax.random.fold_in(jax.random.fold_in(own_key, 6), dim), (parts,), jnp.float32, low / len(split), top_value / len(split))
        loudness = loudness * jnp.repeat(jnp.exp(draws), extent[dim] // parts).reshape((-1,) + (1,) * (len(extent) - 1 - dim))
    return loudness


def scatter_about(stream_key, shape, scale, bound, split=(), held_as=jnp.bfloat16):
    values = jax.random.normal(stream_key, shape, jnp.float32) * scale
    if len(split) > 0:
        values = steps_of(stream_key, shape, split, -0.22, 0.18) * values
    return jnp.clip(values, min=-bound, max=bound).astype(held_as)


def setup_inputs(seed: int = 0) -> dict:
    key_list = jax.random.split(jax.random.key(seed), 10)
    tokens = scatter_about(key_list[0], (FRAMES, ROWS, W, D), 1.0, 6.0, ((0, 4), (1, 8)))
    norm_gain = jnp.clip(1.0 + 0.1 * jax.random.normal(key_list[1], (D,), jnp.float32), 0.5, 1.5)
    in_weight = scatter_about(key_list[2], (D, 2 * INNER), D ** -0.5, 0.15625)
    bc_weight = scatter_about(key_list[3], (D, 4 * STATE), D ** -0.5, 0.15625)
    dt_weight = scatter_about(key_list[4], (D, 2 * HEADS), D ** -0.5, 0.15625)
    dt_bias = jnp.clip(jax.random.uniform(key_list[5], (2 * HEADS,), jnp.float32, -1.0, 1.0), -1.0, 1.0)
    decay_rate = jnp.clip(jnp.exp(jax.random.uniform(key_list[6], (2, HEADS), jnp.float32, math.log(0.0006510417), math.log(0.05))), 0.0006510417, 0.05)
    out_gain = jnp.clip(1.0 + 0.1 * jax.random.normal(key_list[7], (INNER,), jnp.float32), 0.5, 1.5)
    out_weight = scatter_about(key_list[8], (INNER, D), INNER ** -0.5, 0.15625)
    return dict(tokens=tokens, norm_gain=norm_gain, in_weight=in_weight, bc_weight=bc_weight, dt_weight=dt_weight, dt_bias=dt_bias, decay_rate=decay_rate, out_gain=out_gain, out_weight=out_weight)


PRECISE = lax.Precision.HIGH
EPSILON = 1e-05

def stored(values):
    return lax.optimization_barrier(values.astype(jnp.bfloat16))

def rms_scale(values, scaling):
    mean_square = lax.optimization_barrier(jnp.mean(values * values, axis=-1, keepdims=True))
    return values * lax.rsqrt(mean_square + EPSILON) * scaling

def block_step(carried, pieces):
    inputs, b_proj, c_proj, dt_values, log_decay = pieces
    running = jnp.cumsum(log_decay, axis=0)
    length = inputs.shape[0]
    causal = jnp.arange(length)[:, None] >= jnp.arange(length)[None, :]
    spread = running[:, None, :] - running[None, :, :]
    decays = jnp.exp(jnp.where(causal[:, :, None], spread, -jnp.inf))
    scores = jnp.dot(c_proj.astype(jnp.bfloat16), b_proj.astype(jnp.bfloat16).T, preferred_element_type=jnp.float32)
    weights = scores[:, :, None] * decays * dt_values[None, :, :]
    within = jnp.einsum('ijh,jhp->ihp', weights, inputs, precision=PRECISE)
    earlier = jnp.einsum('in,hpn->ihp', c_proj, carried, precision=PRECISE)
    outputs = within + jnp.exp(running)[:, :, None] * earlier
    to_end = jnp.exp(running[-1][None, :] - running) * dt_values
    fresh_state = jnp.einsum('jh,jhp,jn->hpn', to_end, inputs, b_proj, precision=PRECISE)
    carried = jnp.exp(running[-1])[:, None, None] * carried + fresh_state
    return (carried, outputs)

def run_blocks(inputs, b_proj, c_proj, dt_values, log_decay, initial, block_len):
    blocks = inputs.shape[0] // block_len

    def split_blocks(operand):
        return operand.reshape((blocks, block_len) + operand.shape[1:])
    final_state, outputs = lax.scan(block_step, initial, (split_blocks(inputs), split_blocks(b_proj), split_blocks(c_proj), split_blocks(dt_values), split_blocks(log_decay)))
    return (outputs.reshape(inputs.shape), final_state)

def direction(inputs, b_proj, c_proj, dt_values, log_decay, block_len):
    initial = jnp.zeros((HEADS, HEAD_DIM, STATE), jnp.float32)
    outputs, _ = run_blocks(inputs, b_proj, c_proj, dt_values, log_decay, initial, block_len)
    return outputs

def reference(tokens, norm_gain, in_weight, bc_weight, dt_weight, dt_bias, decay_rate, out_gain, out_weight):
    flat_tokens = tokens.reshape(-1, D).astype(jnp.float32)
    normed = stored(rms_scale(flat_tokens, norm_gain))
    projected = stored(jnp.dot(normed, in_weight, preferred_element_type=jnp.float32))
    bc_values = stored(jnp.dot(normed, bc_weight, preferred_element_type=jnp.float32)).astype(jnp.float32)
    dt_logits = stored(jnp.dot(normed, dt_weight, preferred_element_type=jnp.float32))
    dt_values = jax.nn.softplus(dt_logits.astype(jnp.float32) + dt_bias)
    log_decay = -dt_values * decay_rate.reshape(-1)
    grid = (FRAMES, ROWS, W)
    inputs = projected[:, :INNER].astype(jnp.float32).reshape(grid + (HEADS, HEAD_DIM))
    gate_values = projected[:, INNER:].astype(jnp.float32).reshape(grid + (INNER,))
    bc_values = bc_values.reshape(grid + (4 * STATE,))
    dt_values = dt_values.reshape(grid + (2 * HEADS,))
    log_decay = log_decay.reshape(grid + (2 * HEADS,))
    spatial_len = ROWS * W
    spatial_block = math.gcd(256, spatial_len)

    def spatial(pieces):
        inputs_f, bc_f, dt_f, decay_f = pieces
        outputs = direction(inputs_f.reshape(spatial_len, HEADS, HEAD_DIM), bc_f[..., :STATE].reshape(spatial_len, STATE), bc_f[..., STATE:2 * STATE].reshape(spatial_len, STATE), dt_f[..., :HEADS].reshape(spatial_len, HEADS), decay_f[..., :HEADS].reshape(spatial_len, HEADS), spatial_block)
        return outputs.reshape(ROWS, W, INNER)
    spatial_out = lax.map(spatial, (inputs, bc_values, dt_values, log_decay))
    temporal_len = W * FRAMES
    temporal_block = math.gcd(256, temporal_len)

    def temporal(pieces):
        inputs_r, bc_r, dt_r, decay_r = pieces
        outputs = direction(inputs_r.reshape(temporal_len, HEADS, HEAD_DIM), bc_r[..., 2 * STATE:3 * STATE].reshape(temporal_len, STATE), bc_r[..., 3 * STATE:].reshape(temporal_len, STATE), dt_r[..., HEADS:].reshape(temporal_len, HEADS), decay_r[..., HEADS:].reshape(temporal_len, HEADS), temporal_block)
        return outputs.reshape(W, FRAMES, INNER)

    def row_major(operand):
        return jnp.moveaxis(operand, 0, 2)
    temporal_out = lax.map(temporal, (row_major(inputs), row_major(bc_values), row_major(dt_values), row_major(log_decay)))
    temporal_out = stored(jnp.moveaxis(temporal_out, 2, 0))
    combined = spatial_out + temporal_out.astype(jnp.float32)
    gated = combined * jax.nn.silu(gate_values)
    normed_out = stored(rms_scale(gated, out_gain)).reshape(-1, INNER)
    mixed = jnp.dot(normed_out, out_weight, preferred_element_type=jnp.float32)
    return mixed.astype(jnp.bfloat16).reshape(FRAMES, ROWS, W, D)
```

```python
import functools
import math

import jax
import jax.numpy as jnp
from jax import lax
from jax.experimental import pallas as pl
from jax.experimental.pallas import tpu as pltpu
from jax.sharding import PartitionSpec as P

EPSILON = 1e-05
LANES = 128
TAIL = 16
F32 = jnp.float32
BF16 = jnp.bfloat16
EXACT = lax.Precision.HIGHEST
LARGE = 56 * 1024 * 1024
SMALL = 24 * 1024 * 1024

ANY = pl.BlockSpec(memory_space=pl.ANY)
HBM = pl.BlockSpec(memory_space=pltpu.HBM)
SCALAR = pl.BlockSpec(memory_space=pltpu.SMEM)
WHOLE = pl.BlockSpec(memory_space=pltpu.VMEM)


def call(kernel, name, out_shape, in_specs, limit=SMALL, outs=None, **options):
    return pl.pallas_call(
        kernel,
        out_shape=out_shape,
        in_specs=in_specs,
        out_specs=jax.tree.map(lambda _: WHOLE, out_shape) if outs is None else outs,
        compiler_params=pltpu.CompilerParams(vmem_limit_bytes=limit),
        cost_estimate=pl.CostEstimate(flops=1, bytes_accessed=1, transcendentals=0),
        name=name,
        **options,
    )


def shape_of(shape, dtype):
    return jax.ShapeDtypeStruct(shape, dtype)


def dot(left, right, **options):
    return jnp.dot(left, right, preferred_element_type=F32, **options)


def dot_tn(left, right):
    return lax.dot_general(left, right, (((0,), (0,)), ((), ())), preferred_element_type=F32)


def dot_nt(left, right):
    return lax.dot_general(left, right, (((1,), (1,)), ((), ())), preferred_element_type=F32)


def softplus(values):
    return jnp.maximum(values, 0.0) + jnp.log1p(jnp.exp(-jnp.abs(values)))


def iota(shape, dim):
    return lax.broadcasted_iota(jnp.int32, shape, dim)


def spread_matrix(first_head, width, head_dim):
    return (iota((LANES, width), 0) - first_head == iota((LANES, width), 1) // head_dim).astype(BF16)


def spread(values, matrix):
    high = values.astype(BF16)
    low = (values - high.astype(F32)).astype(BF16)
    return dot(high, matrix) + dot(low, matrix)


def head_mixes(scores, running, running_t, dt_t, x, first_head, heads, head_dim):
    length = scores.shape[0]
    outs = []

    def weights(head):
        spreads = running[:, head : head + 1] - running_t[head : head + 1, :]
        return (scores * jnp.exp(jnp.minimum(spreads, 0.0)) * dt_t[head : head + 1, :]).astype(BF16)

    head = 0
    while head < heads:
        here = first_head + head
        if head + 1 < heads and 2 * head_dim == LANES:
            both = x[:, head * head_dim : (head + 2) * head_dim]
            first = iota((length, LANES), 1) < head_dim
            zero = jnp.zeros_like(both)
            stacked = jnp.concatenate([jnp.where(first, both, zero), jnp.where(first, zero, both)], axis=0)
            pair = jnp.concatenate([weights(here), weights(here + 1)], axis=1)
            outs.append(dot(pair, stacked))
            head += 2
        else:
            outs.append(dot(weights(here), x[:, head * head_dim : (head + 1) * head_dim]))
            head += 1
    return outs[0] if len(outs) == 1 else jnp.concatenate(outs, axis=1)


def column_copies(weight, scratch, sems, first, offset, blocks):
    width = scratch.shape[1] // blocks
    return [
        pltpu.make_async_copy(
            weight.at[:, pl.ds(offset + index * width, width)],
            scratch.at[:, pl.ds(index * width, width)],
            sems.at[first + index],
        )
        for index in range(blocks)
    ]


def packing(length, group):
    columns = group // LANES
    rest = -(-(2 * length + TAIL) // columns)
    return length, -(-rest // TAIL) * TAIL


def pack_rest(ref, length, b_proj, c_proj, dt):
    columns, rest = ref.shape[1] // LANES, ref.shape[0] - length
    blank = jnp.zeros((columns * rest - 2 * length - TAIL, LANES), BF16)
    stacked = jnp.concatenate([b_proj, c_proj, dt, blank], axis=0)
    for column in range(columns):
        ref[length:, column * LANES : (column + 1) * LANES] = stacked[column * rest : (column + 1) * rest]


def unpacked_rest(ref, length):
    columns = ref.shape[1] // LANES
    stacked = jnp.concatenate(
        [ref[length:, column * LANES : (column + 1) * LANES] for column in range(columns)], axis=0
    )
    return stacked[:length], stacked[length : 2 * length], stacked[2 * length : 2 * length + TAIL]


def entry_kernel(shares, heads, state, blocks, *refs):
    here_ref, band, tokens, gain, bias, rates, dt_weight, bc_weight, weight = refs[:9]
    normed_out, payload_out, bc_own, logits, params, own_states, other_states = refs[9:16]
    held, dt_held, bc_held, held_weight, table, normed, payload, sems, out_sems = refs[16:]
    frames, rows, columns, width = tokens.shape
    length = frames * columns
    count = rows * length
    groups = shares // rows
    per_group = heads // groups
    group = held_weight.shape[1] // groups

    token_copies = [
        pltpu.make_async_copy(tokens.at[frame, row], held.at[row, frame], sems.at[row * frames + frame])
        for row in range(rows)
        for frame in range(frames)
    ]
    for copy in token_copies:
        copy.start()
    first = rows * frames
    dt_copy = pltpu.make_async_copy(dt_weight, dt_held, sems.at[first])
    dt_copy.start()
    bc_copy = pltpu.make_async_copy(bc_weight, bc_held, sems.at[first + 1])
    bc_copy.start()
    copies = column_copies(weight, held_weight, sems, first + 2, 0, blocks)
    for copy in copies:
        copy.start()

    table[...] = jnp.zeros_like(table)
    table[0:1, : 2 * heads] = bias[...].reshape(1, 2 * heads)
    table[1:2, :heads] = rates[0:1, :]
    table[1:2, heads : 2 * heads] = rates[1:2, :]
    first_head = heads + here_ref[0] // rows * per_group
    lane_in, lane_out = iota((LANES, LANES), 0), iota((LANES, LANES), 1)
    own = ((lane_in == lane_out + first_head) & (lane_out < per_group)).astype(F32)
    params[0:8, :] = table[...]
    params[8:16, :] = dot(table[...], own, precision=EXACT)
    logits[...] = jnp.zeros_like(logits)

    gains = gain[...].reshape(1, width)
    for index, copy in enumerate(token_copies):
        copy.wait()
        values = held[index // frames, index % frames].astype(F32)
        mean_square = jnp.mean(values * values, axis=-1, keepdims=True)
        normed[index * columns : (index + 1) * columns, :] = (
            values * lax.rsqrt(mean_square + EPSILON) * gains
        ).astype(BF16)
    outgoing = [pltpu.make_async_copy(normed, normed_out, out_sems.at[0])]
    outgoing[0].start()
    dt_copy.wait()
    logits[:, : 2 * heads] = dot_nt(normed[...], dt_held[...]).astype(BF16).astype(F32)
    dt_heads = dot_nt(dt_held[heads:, :], normed[...])
    dt_heads = jnp.concatenate([dt_heads, jnp.zeros((TAIL, count), F32)], axis=0).astype(BF16)
    bc_copy.wait()
    bc = dot(normed[...], bc_held[...]).astype(BF16)
    bc_own[...] = bc[:, : 2 * state]
    scan = [
        end_factors(frame_of(logits, frame, rows, frames, columns), params, rows * columns)
        for frame in range(frames)
    ]

    block = held_weight.shape[1] // blocks
    for index, copy in enumerate(copies):
        copy.wait()
        at = index * block
        values = dot(normed[...], held_weight[:, at : at + block]).astype(BF16)
        for inside in range(0, block, group):
            part = (at + inside) // group
            for row in range(rows):
                piece = part * rows + row
                here = slice(row * length, (row + 1) * length)
                payload[piece, :length, :] = values[here, inside : inside + group]
                pack_rest(
                    payload.at[piece],
                    length,
                    bc[here, 2 * state : 3 * state],
                    bc[here, 3 * state :],
                    dt_heads[part * per_group : part * per_group + TAIL, here],
                )
                outgoing.append(
                    pltpu.make_async_copy(
                        payload.at[piece], payload_out.at[piece], out_sems.at[1 + piece]
                    )
                )
                outgoing[-1].start()
    half = state // 2
    head_dim = groups * group // heads
    mine = band[0] % 2 == 0
    for frame in range(frames):
        b_proj = frame_of(bc_own, frame, rows, frames, columns)[:, :state]
        for part in range(groups):
            at = slice(part * group, (part + 1) * group)
            values = frame_x(payload, part, frame, rows, columns)
            matrix = spread_matrix(part * per_group, group, head_dim)
            scaled = (values.astype(F32) * dot(scan[frame][0], matrix)).astype(BF16)
            fresh = dot_tn(b_proj, scaled).astype(BF16)
            at_rows = slice(frame * half, (frame + 1) * half)
            own_states[at_rows, at] = jnp.where(mine, fresh[:half], fresh[half:])
            other_states[at_rows, at] = jnp.where(mine, fresh[half:], fresh[:half])
    whole = [decay for _, decay in scan] + [jnp.zeros((8 - frames, LANES), F32)]
    decays = spread(jnp.concatenate(whole, axis=0), spread_matrix(0, groups * group, head_dim))
    tail = tail_of(decays)
    own_states[frames * half :, :] = tail
    other_states[frames * half :, :] = tail
    for copy in outgoing:
        copy.wait()


def gate_kernel(blocks, after, normed, weight, out, held_weight, sems):
    inner = held_weight.shape[1]
    copies = column_copies(weight, held_weight, sems, 0, inner, blocks)
    for copy in copies:
        copy.start()
    block = inner // blocks
    for index, copy in enumerate(copies):
        copy.wait()
        at = slice(index * block, (index + 1) * block)
        out[:, at] = dot(normed[...], held_weight[:, at]).astype(BF16)


def frame_of(ref, frame, rows, frames, columns):
    return jnp.concatenate(
        [
            ref[(row * frames + frame) * columns : (row * frames + frame + 1) * columns, :]
            for row in range(rows)
        ],
        axis=0,
    )


def frame_x(payload, part, frame, rows, columns):
    return jnp.concatenate(
        [
            payload[part * rows + row, frame * columns : (frame + 1) * columns, :]
            for row in range(rows)
        ],
        axis=0,
    )


def scan_terms(logits, params, causal):
    dt = softplus(logits + params[0:1, :])
    running = dot(causal.astype(F32), -dt * params[1:2, :], precision=EXACT)
    return dt, running, jnp.min(running, axis=0, keepdims=True)


def end_factors(logits, params, length):
    causal = iota((length, length), 0) >= iota((length, length), 1)
    dt, running, last = scan_terms(logits, params, causal)
    return (jnp.exp(last - running) * dt).astype(BF16), jnp.exp(last)


def local_kernel(frames, rows, columns, head_dim, groups, *refs):
    after, bc, logits, params, x, out, reach = refs
    length = rows * columns
    group = x.shape[2]
    state = bc.shape[1] // 2
    per_group = group // head_dim
    causal = iota((length, length), 0) >= iota((length, length), 1)

    def stored(ref, values, frame, at):
        for row in range(rows):
            to = (row * frames + frame) * columns
            ref[to : to + columns, at] = values[row * columns : (row + 1) * columns]

    for frame in range(frames):
        dt, running, _ = scan_terms(frame_of(logits, frame, rows, frames, columns), params, causal)
        running_t, dt_t = jnp.transpose(running), jnp.transpose(dt)
        bc_rows = frame_of(bc, frame, rows, frames, columns)
        scores = jnp.where(causal, dot_nt(bc_rows[:, state:], bc_rows[:, :state]), 0.0)
        stored(reach, jnp.exp(running), frame, slice(None))
        for piece in range(groups):
            values = frame_x(x, piece, frame, rows, columns)
            mixed = head_mixes(
                scores, running, running_t, dt_t, values, piece * per_group, per_group, head_dim
            )
            stored(out, mixed, frame, slice(piece * group, (piece + 1) * group))


def tail_of(decays):
    high = decays.astype(BF16)
    return jnp.concatenate([high, (decays - high.astype(F32)).astype(BF16)], axis=0)


def pair_kernel(frames, band, own, far, total):
    rows = (own.shape[0] - TAIL) // frames
    own_decay = own[-TAIL:-8, :].astype(F32) + own[-8:, :].astype(F32)
    far_decay = far[-TAIL:-8, :].astype(F32) + far[-8:, :].astype(F32)
    lower = band[0] % 2 == 0
    through = jnp.where(lower, far_decay, own_decay)
    for frame in range(frames):
        at = slice(frame * rows, (frame + 1) * rows)
        first = jnp.where(lower, own[at, :], far[at, :]).astype(F32)
        second = jnp.where(lower, far[at, :], own[at, :]).astype(F32)
        total[at, :] = (through[frame : frame + 1, :] * first + second).astype(BF16)
    total[frames * rows :, :] = tail_of(own_decay * far_decay)


def merge_kernel(frames, distance, finish, *refs):
    _, band, own, far = refs[:4]
    start = distance == 2
    rest = list(refs[4:])
    before_in = None if start else rest.pop(0)
    band_own, band_far = (rest.pop(0), rest.pop(0)) if finish else (None, None)
    rows = (own.shape[0] - TAIL) // frames
    upper, lower_band = (band[0] // distance) % 2 == 1, band[0] % 2 == 0
    own_decay = own[-TAIL:-8, :].astype(F32) + own[-8:, :].astype(F32)
    far_decay = far[-TAIL:-8, :].astype(F32) + far[-8:, :].astype(F32)
    if start:
        before_decay = jnp.ones_like(own_decay)
    else:
        before_decay = before_in[-8:, :]
    if finish:
        first_decay = jnp.where(
            lower_band,
            band_own[-TAIL:-8, :].astype(F32) + band_own[-8:, :].astype(F32),
            band_far[-TAIL:-8, :].astype(F32) + band_far[-8:, :].astype(F32),
        )
    through = jnp.where(upper, own_decay, far_decay)
    for frame in range(frames):
        at = slice(frame * rows, (frame + 1) * rows)
        row = slice(frame, frame + 1)
        far_state = far[at, :].astype(F32)
        came = before_decay[row, :] * far_state
        if not start:
            came = came + before_in[at, :]
        before = jnp.where(upper, came, 0.0 if start else before_in[at, :])
        if finish:
            keep, give = rest
            first = jnp.where(lower_band, band_own[at, :], band_far[at, :]).astype(F32)
            after = first_decay[row, :] * before + first
            keep[at, :] = jnp.where(lower_band, before, after).astype(BF16)
            give[at, :] = jnp.where(lower_band, after, before).astype(BF16)
        else:
            total, before_out = rest
            own_state = own[at, :].astype(F32)
            early = jnp.where(upper, far_state, own_state)
            late = jnp.where(upper, own_state, far_state)
            total[at, :] = (through[row, :] * early + late).astype(BF16)
            before_out[at, :] = before
    if not finish:
        total[frames * rows :, :] = tail_of(own_decay * far_decay)
        before_out[frames * rows :, :] = jnp.where(upper, before_decay * far_decay, before_decay)


def incoming_kernel(frames, rows, columns, head_dim, band, out_local, bc, reach, own, other, out):
    state = bc.shape[1] // 2
    half = state // 2
    inner = out.shape[1]
    mine = band[0] % 2 == 0
    matrix = spread_matrix(0, inner, head_dim)
    for frame in range(frames):
        at = slice(frame * half, (frame + 1) * half)
        low = jnp.where(mine, own[at, :], other[at, :])
        high = jnp.where(mine, other[at, :], own[at, :])
        carried = jnp.concatenate([low, high], axis=0)
        for row in range(rows):
            to = (row * frames + frame) * columns
            here = slice(to, to + columns)
            factor = spread(reach[here, :], matrix)
            out[here, :] = out_local[here, :] + factor * dot(bc[here, state:], carried)


def temporal_kernel(
    part, parts, per_group, head_dim, rows, frames, columns, chunk_cols, shares, state, *refs
):
    here_ref, params, payload = refs[:3]
    rest = list(refs[3:])
    carried_in = rest.pop(0) if part > 0 else None
    outs, rest = rest[:shares], rest[shares:]
    carried_out = rest.pop(0) if part + 1 < parts else None
    b_all, c_all, dt_all, decay_all = rest
    here = here_ref[0]
    length = frames * columns
    part_cols = columns // parts
    group = outs[0].shape[1]
    eye = (iota((TAIL, LANES), 0) == iota((TAIL, LANES), 1)) & (iota((TAIL, LANES), 1) < per_group)
    eye = eye.astype(BF16)

    def came(distance):
        return payload.at[here ^ distance]

    for distance in range(shares):
        b_proj, c_proj, logits = unpacked_rest(came(distance), length)
        logits = dot_tn(logits, eye)
        for frame in range(frames):
            at = slice(frame * columns + part * part_cols, frame * columns + (part + 1) * part_cols)
            to = slice(frame * part_cols, (frame + 1) * part_cols)
            b_all[distance, to] = b_proj[at]
            c_all[distance, to] = c_proj[at]
            dt = softplus(logits[at] + params[8:9, :])
            dt_all[distance, to] = dt
            decay_all[distance, to] = -dt * params[9:10, :]

    all_frames = shares * frames
    size = all_frames * chunk_cols

    def order_key(dim):
        index = iota((size, size), dim)
        source = here ^ (index // (frames * chunk_cols))
        frame = source * frames + (index // chunk_cols) % frames
        return (index % chunk_cols) * all_frames + frame

    causal = order_key(0) >= order_key(1)
    order = causal.astype(F32)
    matrix = spread_matrix(0, group, head_dim)
    carried = jnp.zeros((state, group), F32) if part == 0 else carried_in[...]
    places = [(source, frame) for source in range(shares) for frame in range(frames)]
    for chunk in range(part_cols // chunk_cols):

        def gathered(ref_of, pitch=part_cols, offset=0):
            return jnp.concatenate(
                [
                    ref_of(source)[pl.ds(frame * pitch + offset + chunk * chunk_cols, chunk_cols), :]
                    for source, frame in places
                ],
                axis=0,
            )

        values = gathered(came, columns, part * part_cols)
        b_proj = gathered(lambda source: b_all.at[source])
        c_proj = gathered(lambda source: c_all.at[source])
        dt = gathered(lambda source: dt_all.at[source])
        running = dot(order, gathered(lambda source: decay_all.at[source]), precision=EXACT)
        running_t, dt_t = jnp.transpose(running), jnp.transpose(dt)
        scores = jnp.where(causal, dot_nt(c_proj, b_proj), 0.0)
        last = jnp.min(running, axis=0, keepdims=True)
        mixed = head_mixes(scores, running, running_t, dt_t, values, 0, per_group, head_dim)
        ends = jnp.concatenate([running, jnp.broadcast_to(last, (8, LANES))], axis=0)
        reach = spread(jnp.exp(ends), matrix)
        mixed = mixed + reach[:size] * dot(c_proj, carried.astype(BF16))
        to_end = (jnp.exp(last - running) * dt).astype(BF16)
        scaled = (values.astype(F32) * dot(to_end, matrix)).astype(BF16)
        carried = reach[size : size + 1, :] * carried + dot_tn(b_proj, scaled)
        mixed = mixed.astype(BF16)
        for index, (source, frame) in enumerate(places):
            to = frame * part_cols + chunk * chunk_cols
            outs[source][to : to + chunk_cols, :] = mixed[index * chunk_cols : (index + 1) * chunk_cols]
    if carried_out is not None:
        carried_out[...] = carried


def exit_kernel(part, parts, shares, *refs):
    here, spatial, gate, gain, weight = refs[:5]
    out, temporal, normed, mixed, sems = refs[-5:]
    frames, rows, columns, _ = out.shape
    part_cols = columns // parts
    _, part_len, group = temporal.shape
    groups = shares // rows
    inner = groups * group
    for distance in range(shares):
        temporal[here[0] ^ distance] = refs[5 + distance][...]

    def own(ref, row, at):
        return jnp.concatenate(
            [
                ref[pl.ds((row * frames + frame) * columns + part * part_cols, part_cols), at]
                for frame in range(frames)
            ],
            axis=0,
        )

    gains = gain[...].reshape(1, inner)
    for row in range(rows):
        total = jnp.zeros((part_len, 1), F32)
        kept = []
        for index in range(groups):
            at = slice(index * group, (index + 1) * group)
            gates = own(gate, row, at).astype(F32)
            gated = own(spatial, row, at) + temporal[index * rows + row].astype(F32)
            gated = gated * (gates / (1.0 + jnp.exp(-gates)))
            total = total + jnp.sum(gated * gated, axis=1, keepdims=True)
            kept.append(gated)
        scale = lax.rsqrt(total / inner + EPSILON)
        for index, gated in enumerate(kept):
            at = slice(index * group, (index + 1) * group)
            normed[row * part_len : (row + 1) * part_len, at] = (gated * scale * gains[:, at]).astype(BF16)
    mixed[...] = dot(normed[...], weight[...]).astype(BF16)
    copies = [
        pltpu.make_async_copy(
            mixed.at[pl.ds((row * frames + frame) * part_cols, part_cols), :],
            out.at[frame, row, pl.ds(part * part_cols, part_cols), :],
            sems.at[row * frames + frame],
        )
        for row in range(rows)
        for frame in range(frames)
    ]
    for copy in copies:
        copy.start()
    for copy in copies:
        copy.wait()


def swapped(value, axis, distance):
    count = lax.axis_size(axis)
    return lax.ppermute(value, axis, [(source, source ^ distance) for source in range(count)])


def per_device(
    tokens, norm_gain, in_weight, bc_weight, dt_weight, dt_bias, decay_rate, out_gain, out_weight
):
    frames, rows, columns, width = tokens.shape
    heads = decay_rate.shape[1]
    inner = out_weight.shape[0]
    head_dim = inner // heads
    state = bc_weight.shape[1] // 4
    shares = lax.axis_size("tm")
    bands = lax.axis_size("height")
    groups = shares // rows
    group = inner // groups
    per_group = heads // groups
    length = frames * columns
    count = rows * length
    half = state // 2
    chunk_cols = 16
    blocks = parts = 2
    part_len = length // parts
    here = lax.axis_index("tm").astype(jnp.int32).reshape(1)
    band = lax.axis_index("height").astype(jnp.int32).reshape(1)

    packed = (shares, sum(packing(length, group)), group)
    normed, payload, bc_own, logits, params, own, other = call(
        functools.partial(entry_kernel, shares, heads, state, blocks),
        "entry",
        [
            shape_of((count, width), BF16),
            shape_of(packed, BF16),
            shape_of((count, 2 * state), BF16),
            shape_of((count, LANES), F32),
            shape_of((16, LANES), F32),
        ]
        + [shape_of((frames * half + TAIL, inner), BF16)] * 2,
        [SCALAR, SCALAR, HBM, WHOLE, WHOLE, WHOLE, HBM, HBM, HBM],
        limit=LARGE,
        outs=[HBM, HBM] + [WHOLE] * 5,
        scratch_shapes=[
            pltpu.VMEM((rows, frames, columns, width), BF16),
            pltpu.VMEM((2 * heads, width), BF16),
            pltpu.VMEM((width, 4 * state), BF16),
            pltpu.VMEM((width, inner), BF16),
            pltpu.VMEM((8, LANES), F32),
            pltpu.VMEM((count, width), BF16),
            pltpu.VMEM(packed, BF16),
            pltpu.SemaphoreType.DMA((rows * frames + 2 + blocks,)),
            pltpu.SemaphoreType.DMA((1 + shares,)),
        ],
    )(here, band, tokens, norm_gain, dt_bias, decay_rate, dt_weight.T, bc_weight, in_weight)

    def sent(parts):
        return [parts[0]] + [swapped(parts[d], "tm", d) for d in range(1, shares)]

    received = lax.all_to_all(payload, "tm", split_axis=0, concat_axis=0, tiled=True)
    far = swapped(other, "height", 1)
    gate = call(
        functools.partial(gate_kernel, blocks),
        "gate",
        shape_of((count, inner), BF16),
        [ANY, WHOLE, HBM],
        scratch_shapes=[
            pltpu.VMEM((width, inner), BF16),
            pltpu.SemaphoreType.DMA((blocks,)),
        ],
    )(payload, normed, in_weight)

    out_local, reach = call(
        functools.partial(local_kernel, frames, rows, columns, head_dim, groups),
        "spatial_local",
        [shape_of((count, inner), F32), shape_of((count, LANES), F32)],
        [ANY] + [WHOLE] * 4,
    )(gate, bc_own, logits, params, payload)

    total = call(
        functools.partial(pair_kernel, frames),
        "pair_total",
        shape_of((frames * half + TAIL, inner), BF16),
        [SCALAR, WHOLE, WHOLE],
    )(band, own, far)
    returned, carried = [], []
    for part in range(parts):
        more = [shape_of((state, group), F32)] if part + 1 < parts else []
        results = call(
            functools.partial(
                temporal_kernel,
                part,
                parts,
                per_group,
                head_dim,
                rows,
                frames,
                columns,
                chunk_cols,
                shares,
                state,
            ),
            "temporal",
            [shape_of((part_len, group), BF16)] * shares + more,
            [SCALAR] + [WHOLE] * (2 + len(carried)),
            scratch_shapes=[
                pltpu.VMEM((shares, part_len, state), BF16),
                pltpu.VMEM((shares, part_len, state), BF16),
                pltpu.VMEM((shares, part_len, LANES), F32),
                pltpu.VMEM((shares, part_len, LANES), F32),
            ],
        )(here, params, received, *carried)
        returned.append(sent(results[:shares]))
        carried = results[shares:]

    before = []
    distance = 2
    while distance < bands:
        far_total = swapped(total, "height", distance)
        finish = distance * 2 >= bands
        operands = [reach, band, total, far_total] + before + ([own, far] if finish else [])
        outs = (
            [shape_of((frames * half, inner), BF16)] * 2
            if finish
            else [
                shape_of((frames * half + TAIL, inner), BF16),
                shape_of((frames * half + 8, inner), F32),
            ]
        )
        results = call(
            functools.partial(merge_kernel, frames, distance, finish),
            "merge",
            outs,
            [ANY, SCALAR] + [WHOLE] * (len(operands) - 2),
        )(*operands)
        if not finish:
            total, before = results[0], [results[1]]
        distance *= 2
    keep, give = results
    came = swapped(give, "height", 1)

    spatial_out = call(
        functools.partial(incoming_kernel, frames, rows, columns, head_dim),
        "spatial_incoming",
        shape_of((count, inner), F32),
        [SCALAR] + [WHOLE] * 5,
    )(band, out_local, bc_own, reach, keep, came)

    mixed = []
    for part in range(parts):
        mixed = [
            call(
                functools.partial(exit_kernel, part, parts, shares),
                "exit",
                shape_of(tokens.shape, BF16),
                [SCALAR] + [WHOLE] * (4 + shares) + [HBM] * len(mixed),
                outs=HBM,
                scratch_shapes=[
                    pltpu.VMEM((shares, part_len, group), BF16),
                    pltpu.VMEM((rows * part_len, inner), BF16),
                    pltpu.VMEM((rows * part_len, width), BF16),
                    pltpu.SemaphoreType.DMA((rows * frames,)),
                ],
                input_output_aliases={5 + shares: 0} if mixed else {},
            )(here, spatial_out, gate, out_gain, out_weight, *returned[part], *mixed)
        ]
    return mixed[0]


def solution(mesh):
    in_specs = (P("tm", "height", None, None), P(), P(), P(), P(), P(), P(), P(), P())
    out_specs = P("tm", "height", None, None)
    return jax.shard_map(
        per_device, mesh=mesh, in_specs=in_specs, out_specs=out_specs, check_vma=False
    )
```

```python
import functools
import math

import jax
import jax.numpy as jnp
from jax import lax
from jax.experimental import pallas as pl
from jax.experimental.pallas import tpu as pltpu
from jax.sharding import PartitionSpec as P

EPSILON = 1e-05
LANES = 128
TAIL = 16
F32 = jnp.float32
BF16 = jnp.bfloat16
EXACT = lax.Precision.HIGHEST
LARGE = 56 * 1024 * 1024
SMALL = 24 * 1024 * 1024

ANY = pl.BlockSpec(memory_space=pl.ANY)
HBM = pl.BlockSpec(memory_space=pltpu.HBM)
SCALAR = pl.BlockSpec(memory_space=pltpu.SMEM)
WHOLE = pl.BlockSpec(memory_space=pltpu.VMEM)


def call(kernel, name, out_shape, in_specs, limit=SMALL, outs=None, **options):
    return pl.pallas_call(
        kernel,
        out_shape=out_shape,
        in_specs=in_specs,
        out_specs=jax.tree.map(lambda _: WHOLE, out_shape) if outs is None else outs,
        compiler_params=pltpu.CompilerParams(vmem_limit_bytes=limit),
        cost_estimate=pl.CostEstimate(flops=1, bytes_accessed=1, transcendentals=0),
        name=name,
        **options,
    )


def shape_of(shape, dtype):
    return jax.ShapeDtypeStruct(shape, dtype)


def dot(left, right, **options):
    return jnp.dot(left, right, preferred_element_type=F32, **options)


def dot_tn(left, right):
    return lax.dot_general(left, right, (((0,), (0,)), ((), ())), preferred_element_type=F32)


def dot_nt(left, right):
    return lax.dot_general(left, right, (((1,), (1,)), ((), ())), preferred_element_type=F32)


def softplus(values):
    return jnp.maximum(values, 0.0) + jnp.log1p(jnp.exp(-jnp.abs(values)))


def iota(shape, dim):
    return lax.broadcasted_iota(jnp.int32, shape, dim)


def spread_matrix(first_head, width, head_dim):
    return (iota((LANES, width), 0) - first_head == iota((LANES, width), 1) // head_dim).astype(BF16)


def spread(values, matrix):
    high = values.astype(BF16)
    low = (values - high.astype(F32)).astype(BF16)
    return dot(high, matrix) + dot(low, matrix)


def head_mixes(scores, running, running_t, dt_t, x, first_head, heads, head_dim):
    length = scores.shape[0]
    outs = []

    def weights(head):
        spreads = running[:, head : head + 1] - running_t[head : head + 1, :]
        return (scores * jnp.exp(jnp.minimum(spreads, 0.0)) * dt_t[head : head + 1, :]).astype(BF16)

    head = 0
    while head < heads:
        here = first_head + head
        if head + 1 < heads and 2 * head_dim == LANES:
            both = x[:, head * head_dim : (head + 2) * head_dim]
            first = iota((length, LANES), 1) < head_dim
            zero = jnp.zeros_like(both)
            stacked = jnp.concatenate([jnp.where(first, both, zero), jnp.where(first, zero, both)], axis=0)
            pair = jnp.concatenate([weights(here), weights(here + 1)], axis=1)
            outs.append(dot(pair, stacked))
            head += 2
        else:
            outs.append(dot(weights(here), x[:, head * head_dim : (head + 1) * head_dim]))
            head += 1
    return outs[0] if len(outs) == 1 else jnp.concatenate(outs, axis=1)


def column_copies(weight, scratch, sems, first, offset, blocks):
    width = scratch.shape[1] // blocks
    return [
        pltpu.make_async_copy(
            weight.at[:, pl.ds(offset + index * width, width)],
            scratch.at[:, pl.ds(index * width, width)],
            sems.at[first + index],
        )
        for index in range(blocks)
    ]


def packing(length, group):
    columns = group // LANES
    rest = -(-(2 * length + TAIL) // columns)
    return length, -(-rest // TAIL) * TAIL


def pack_rest(ref, length, b_proj, c_proj, dt):
    columns, rest = ref.shape[1] // LANES, ref.shape[0] - length
    blank = jnp.zeros((columns * rest - 2 * length - TAIL, LANES), BF16)
    stacked = jnp.concatenate([b_proj, c_proj, dt, blank], axis=0)
    for column in range(columns):
        ref[length:, column * LANES : (column + 1) * LANES] = stacked[column * rest : (column + 1) * rest]


def unpacked_rest(ref, length):
    columns = ref.shape[1] // LANES
    stacked = jnp.concatenate(
        [ref[length:, column * LANES : (column + 1) * LANES] for column in range(columns)], axis=0
    )
    return stacked[:length], stacked[length : 2 * length], stacked[2 * length : 2 * length + TAIL]


def entry_kernel(shares, heads, state, blocks, *refs):
    here_ref, band, tokens, gain, bias, rates, dt_weight, bc_weight, weight = refs[:9]
    normed_out, x_out, bc_own, logits, params, own_states, other_states = refs[9:16]
    payloads = refs[16 : 16 + shares]
    held, dt_held, bc_held, held_weight, table, normed, payload, sems, out_sems = refs[-9:]
    frames, rows, columns, width = tokens.shape
    length = frames * columns
    count = rows * length
    groups = shares // rows
    per_group = heads // groups
    group = held_weight.shape[1] // groups

    token_copies = [
        pltpu.make_async_copy(tokens.at[frame, row], held.at[row, frame], sems.at[row * frames + frame])
        for row in range(rows)
        for frame in range(frames)
    ]
    for copy in token_copies:
        copy.start()
    first = rows * frames
    dt_copy = pltpu.make_async_copy(dt_weight, dt_held, sems.at[first])
    dt_copy.start()
    bc_copy = pltpu.make_async_copy(bc_weight, bc_held, sems.at[first + 1])
    bc_copy.start()
    copies = column_copies(weight, held_weight, sems, first + 2, 0, blocks)
    for copy in copies:
        copy.start()

    table[...] = jnp.zeros_like(table)
    table[0:1, : 2 * heads] = bias[...].reshape(1, 2 * heads)
    table[1:2, :heads] = rates[0:1, :]
    table[1:2, heads : 2 * heads] = rates[1:2, :]
    first_head = heads + here_ref[0] // rows * per_group
    lane_in, lane_out = iota((LANES, LANES), 0), iota((LANES, LANES), 1)
    own = ((lane_in == lane_out + first_head) & (lane_out < per_group)).astype(F32)
    params[0:8, :] = table[...]
    params[8:16, :] = dot(table[...], own, precision=EXACT)
    logits[...] = jnp.zeros_like(logits)

    gains = gain[...].reshape(1, width)
    for index, copy in enumerate(token_copies):
        copy.wait()
        values = held[index // frames, index % frames].astype(F32)
        mean_square = jnp.mean(values * values, axis=-1, keepdims=True)
        normed[index * columns : (index + 1) * columns, :] = (
            values * lax.rsqrt(mean_square + EPSILON) * gains
        ).astype(BF16)
    outgoing = [pltpu.make_async_copy(normed, normed_out, out_sems.at[0])]
    outgoing[0].start()
    dt_copy.wait()
    logits[:, : 2 * heads] = dot_nt(normed[...], dt_held[...]).astype(BF16).astype(F32)
    dt_heads = dot_nt(dt_held[heads:, :], normed[...])
    dt_heads = jnp.concatenate([dt_heads, jnp.zeros((TAIL, count), F32)], axis=0).astype(BF16)
    bc_copy.wait()
    bc = dot(normed[...], bc_held[...]).astype(BF16)
    bc_own[...] = bc[:, : 2 * state]
    scan = [
        end_factors(frame_of(logits, frame, rows, frames, columns), params, rows * columns)
        for frame in range(frames)
    ]

    block = held_weight.shape[1] // blocks
    for index, copy in enumerate(copies):
        copy.wait()
        at = index * block
        values = dot(normed[...], held_weight[:, at : at + block]).astype(BF16)
        for inside in range(0, block, group):
            part = (at + inside) // group
            for row in range(rows):
                piece = part * rows + row
                tokens_here = slice(row * length, (row + 1) * length)
                payload[piece, :length, :] = values[tokens_here, inside : inside + group]
                pack_rest(
                    payload.at[piece],
                    length,
                    bc[tokens_here, 2 * state : 3 * state],
                    bc[tokens_here, 3 * state :],
                    dt_heads[part * per_group : part * per_group + TAIL, tokens_here],
                )
    here = here_ref[0]
    for distance in range(shares):
        outgoing.append(
            pltpu.make_async_copy(payload.at[here ^ distance], payloads[distance], out_sems.at[1 + distance])
        )
        outgoing[-1].start()
    outgoing.append(pltpu.make_async_copy(payload, x_out, out_sems.at[1 + shares]))
    outgoing[-1].start()
    half = state // 2
    head_dim = groups * group // heads
    mine = band[0] % 2 == 0
    for frame in range(frames):
        b_proj = frame_of(bc_own, frame, rows, frames, columns)[:, :state]
        for part in range(groups):
            at = slice(part * group, (part + 1) * group)
            values = frame_x(payload, part, frame, rows, columns)
            matrix = spread_matrix(part * per_group, group, head_dim)
            scaled = (values.astype(F32) * dot(scan[frame][0], matrix)).astype(BF16)
            fresh = dot_tn(b_proj, scaled).astype(BF16)
            at_rows = slice(frame * half, (frame + 1) * half)
            own_states[at_rows, at] = jnp.where(mine, fresh[:half], fresh[half:])
            other_states[at_rows, at] = jnp.where(mine, fresh[half:], fresh[:half])
    whole = [decay for _, decay in scan] + [jnp.zeros((8 - frames, LANES), F32)]
    decays = spread(jnp.concatenate(whole, axis=0), spread_matrix(0, groups * group, head_dim))
    tail = tail_of(decays)
    own_states[frames * half :, :] = tail
    other_states[frames * half :, :] = tail
    for copy in outgoing:
        copy.wait()


def gate_kernel(blocks, after, normed, weight, out, held_weight, sems):
    inner = held_weight.shape[1]
    copies = column_copies(weight, held_weight, sems, 0, inner, blocks)
    for copy in copies:
        copy.start()
    block = inner // blocks
    for index, copy in enumerate(copies):
        copy.wait()
        at = slice(index * block, (index + 1) * block)
        out[:, at] = dot(normed[...], held_weight[:, at]).astype(BF16)


def frame_of(ref, frame, rows, frames, columns):
    return jnp.concatenate(
        [
            ref[(row * frames + frame) * columns : (row * frames + frame + 1) * columns, :]
            for row in range(rows)
        ],
        axis=0,
    )


def frame_x(payload, part, frame, rows, columns):
    return jnp.concatenate(
        [
            payload[part * rows + row, frame * columns : (frame + 1) * columns, :]
            for row in range(rows)
        ],
        axis=0,
    )


def scan_terms(logits, params, causal):
    dt = softplus(logits + params[0:1, :])
    running = dot(causal.astype(F32), -dt * params[1:2, :], precision=EXACT)
    return dt, running, jnp.min(running, axis=0, keepdims=True)


def end_factors(logits, params, length):
    causal = iota((length, length), 0) >= iota((length, length), 1)
    dt, running, last = scan_terms(logits, params, causal)
    return (jnp.exp(last - running) * dt).astype(BF16), jnp.exp(last)


def local_kernel(frames, rows, columns, head_dim, groups, *refs):
    after, bc, logits, params, x, out, reach = refs
    length = rows * columns
    group = x.shape[2]
    state = bc.shape[1] // 2
    per_group = group // head_dim
    causal = iota((length, length), 0) >= iota((length, length), 1)

    def stored(ref, values, frame, at):
        for row in range(rows):
            to = (row * frames + frame) * columns
            ref[to : to + columns, at] = values[row * columns : (row + 1) * columns]

    for frame in range(frames):
        dt, running, _ = scan_terms(frame_of(logits, frame, rows, frames, columns), params, causal)
        running_t, dt_t = jnp.transpose(running), jnp.transpose(dt)
        bc_rows = frame_of(bc, frame, rows, frames, columns)
        scores = jnp.where(causal, dot_nt(bc_rows[:, state:], bc_rows[:, :state]), 0.0)
        stored(reach, jnp.exp(running), frame, slice(None))
        for piece in range(groups):
            values = frame_x(x, piece, frame, rows, columns)
            mixed = head_mixes(
                scores, running, running_t, dt_t, values, piece * per_group, per_group, head_dim
            )
            stored(out, mixed, frame, slice(piece * group, (piece + 1) * group))


def tail_of(decays):
    high = decays.astype(BF16)
    return jnp.concatenate([high, (decays - high.astype(F32)).astype(BF16)], axis=0)


def pair_kernel(frames, band, own, far, total):
    rows = (own.shape[0] - TAIL) // frames
    own_decay = own[-TAIL:-8, :].astype(F32) + own[-8:, :].astype(F32)
    far_decay = far[-TAIL:-8, :].astype(F32) + far[-8:, :].astype(F32)
    lower = band[0] % 2 == 0
    through = jnp.where(lower, far_decay, own_decay)
    for frame in range(frames):
        at = slice(frame * rows, (frame + 1) * rows)
        first = jnp.where(lower, own[at, :], far[at, :]).astype(F32)
        second = jnp.where(lower, far[at, :], own[at, :]).astype(F32)
        total[at, :] = (through[frame : frame + 1, :] * first + second).astype(BF16)
    total[frames * rows :, :] = tail_of(own_decay * far_decay)


def merge_kernel(frames, distance, finish, *refs):
    _, band, own, far = refs[:4]
    start = distance == 2
    rest = list(refs[4:])
    before_in = None if start else rest.pop(0)
    band_own, band_far = (rest.pop(0), rest.pop(0)) if finish else (None, None)
    rows = (own.shape[0] - TAIL) // frames
    upper, lower_band = (band[0] // distance) % 2 == 1, band[0] % 2 == 0
    own_decay = own[-TAIL:-8, :].astype(F32) + own[-8:, :].astype(F32)
    far_decay = far[-TAIL:-8, :].astype(F32) + far[-8:, :].astype(F32)
    if start:
        before_decay = jnp.ones_like(own_decay)
    else:
        before_decay = before_in[-8:, :]
    if finish:
        first_decay = jnp.where(
            lower_band,
            band_own[-TAIL:-8, :].astype(F32) + band_own[-8:, :].astype(F32),
            band_far[-TAIL:-8, :].astype(F32) + band_far[-8:, :].astype(F32),
        )
    through = jnp.where(upper, own_decay, far_decay)
    for frame in range(frames):
        at = slice(frame * rows, (frame + 1) * rows)
        row = slice(frame, frame + 1)
        far_state = far[at, :].astype(F32)
        came = before_decay[row, :] * far_state
        if not start:
            came = came + before_in[at, :]
        before = jnp.where(upper, came, 0.0 if start else before_in[at, :])
        if finish:
            keep, give = rest
            first = jnp.where(lower_band, band_own[at, :], band_far[at, :]).astype(F32)
            after = first_decay[row, :] * before + first
            keep[at, :] = jnp.where(lower_band, before, after).astype(BF16)
            give[at, :] = jnp.where(lower_band, after, before).astype(BF16)
        else:
            total, before_out = rest
            own_state = own[at, :].astype(F32)
            early = jnp.where(upper, far_state, own_state)
            late = jnp.where(upper, own_state, far_state)
            total[at, :] = (through[row, :] * early + late).astype(BF16)
            before_out[at, :] = before
    if not finish:
        total[frames * rows :, :] = tail_of(own_decay * far_decay)
        before_out[frames * rows :, :] = jnp.where(upper, before_decay * far_decay, before_decay)


def incoming_kernel(frames, rows, columns, head_dim, band, out_local, bc, reach, own, other, out):
    state = bc.shape[1] // 2
    half = state // 2
    inner = out.shape[1]
    mine = band[0] % 2 == 0
    matrix = spread_matrix(0, inner, head_dim)
    for frame in range(frames):
        at = slice(frame * half, (frame + 1) * half)
        low = jnp.where(mine, own[at, :], other[at, :])
        high = jnp.where(mine, other[at, :], own[at, :])
        carried = jnp.concatenate([low, high], axis=0)
        for row in range(rows):
            to = (row * frames + frame) * columns
            here = slice(to, to + columns)
            factor = spread(reach[here, :], matrix)
            out[here, :] = out_local[here, :] + factor * dot(bc[here, state:], carried)


def temporal_kernel(
    part, parts, per_group, head_dim, rows, frames, columns, chunk_cols, shares, state, *refs
):
    here_ref, params = refs[:2]
    payloads, rest = refs[2 : 2 + shares], list(refs[2 + shares :])
    carried_in = rest.pop(0) if part > 0 else None
    rest.pop(0)
    outs, rest = rest[:shares], rest[shares:]
    carried_out = rest.pop(0) if part + 1 < parts else None
    b_all, c_all, dt_all, decay_all = rest
    here = here_ref[0]
    length = frames * columns
    part_cols = columns // parts
    group = outs[0].shape[1]
    eye = (iota((TAIL, LANES), 0) == iota((TAIL, LANES), 1)) & (iota((TAIL, LANES), 1) < per_group)
    eye = eye.astype(BF16)

    for distance in range(shares):
        b_proj, c_proj, logits = unpacked_rest(payloads[distance], length)
        logits = dot_tn(logits, eye)
        for frame in range(frames):
            at = slice(frame * columns + part * part_cols, frame * columns + (part + 1) * part_cols)
            to = slice(frame * part_cols, (frame + 1) * part_cols)
            b_all[distance, to] = b_proj[at]
            c_all[distance, to] = c_proj[at]
            dt = softplus(logits[at] + params[8:9, :])
            dt_all[distance, to] = dt
            decay_all[distance, to] = -dt * params[9:10, :]

    all_frames = shares * frames
    size = all_frames * chunk_cols

    def order_key(dim):
        index = iota((size, size), dim)
        source = here ^ (index // (frames * chunk_cols))
        frame = source * frames + (index // chunk_cols) % frames
        return (index % chunk_cols) * all_frames + frame

    causal = order_key(0) >= order_key(1)
    order = causal.astype(F32)
    matrix = spread_matrix(0, group, head_dim)
    carried = jnp.zeros((state, group), F32) if part == 0 else carried_in[...]
    places = [(source, frame) for source in range(shares) for frame in range(frames)]
    for chunk in range(part_cols // chunk_cols):

        def gathered(ref_of, pitch=part_cols, offset=0):
            return jnp.concatenate(
                [
                    ref_of(source)[pl.ds(frame * pitch + offset + chunk * chunk_cols, chunk_cols), :]
                    for source, frame in places
                ],
                axis=0,
            )

        values = gathered(lambda source: payloads[source], columns, part * part_cols)
        b_proj = gathered(lambda source: b_all.at[source])
        c_proj = gathered(lambda source: c_all.at[source])
        dt = gathered(lambda source: dt_all.at[source])
        running = dot(order, gathered(lambda source: decay_all.at[source]), precision=EXACT)
        running_t, dt_t = jnp.transpose(running), jnp.transpose(dt)
        scores = jnp.where(causal, dot_nt(c_proj, b_proj), 0.0)
        last = jnp.min(running, axis=0, keepdims=True)
        mixed = head_mixes(scores, running, running_t, dt_t, values, 0, per_group, head_dim)
        ends = jnp.concatenate([running, jnp.broadcast_to(last, (8, LANES))], axis=0)
        reach = spread(jnp.exp(ends), matrix)
        mixed = mixed + reach[:size] * dot(c_proj, carried.astype(BF16))
        to_end = (jnp.exp(last - running) * dt).astype(BF16)
        scaled = (values.astype(F32) * dot(to_end, matrix)).astype(BF16)
        carried = reach[size : size + 1, :] * carried + dot_tn(b_proj, scaled)
        mixed = mixed.astype(BF16)
        for index, (source, frame) in enumerate(places):
            to = frame * part_cols + chunk * chunk_cols
            outs[source][to : to + chunk_cols, :] = mixed[index * chunk_cols : (index + 1) * chunk_cols]
    if carried_out is not None:
        carried_out[...] = carried


def exit_kernel(part, parts, shares, *refs):
    here, spatial, gate, gain, weight = refs[:5]
    out, temporal, normed, mixed, sems = refs[-5:]
    frames, rows, columns, _ = out.shape
    part_cols = columns // parts
    _, part_len, group = temporal.shape
    groups = shares // rows
    inner = groups * group
    for distance in range(shares):
        temporal[here[0] ^ distance] = refs[5 + distance][...]

    def own(ref, row, at):
        return jnp.concatenate(
            [
                ref[pl.ds((row * frames + frame) * columns + part * part_cols, part_cols), at]
                for frame in range(frames)
            ],
            axis=0,
        )

    gains = gain[...].reshape(1, inner)
    for row in range(rows):
        total = jnp.zeros((part_len, 1), F32)
        kept = []
        for index in range(groups):
            at = slice(index * group, (index + 1) * group)
            gates = own(gate, row, at).astype(F32)
            gated = own(spatial, row, at) + temporal[index * rows + row].astype(F32)
            gated = gated * (gates / (1.0 + jnp.exp(-gates)))
            total = total + jnp.sum(gated * gated, axis=1, keepdims=True)
            kept.append(gated)
        scale = lax.rsqrt(total / inner + EPSILON)
        for index, gated in enumerate(kept):
            at = slice(index * group, (index + 1) * group)
            normed[row * part_len : (row + 1) * part_len, at] = (gated * scale * gains[:, at]).astype(BF16)
    mixed[...] = dot(normed[...], weight[...]).astype(BF16)
    copies = [
        pltpu.make_async_copy(
            mixed.at[pl.ds((row * frames + frame) * part_cols, part_cols), :],
            out.at[frame, row, pl.ds(part * part_cols, part_cols), :],
            sems.at[row * frames + frame],
        )
        for row in range(rows)
        for frame in range(frames)
    ]
    for copy in copies:
        copy.start()
    for copy in copies:
        copy.wait()


def swapped(value, axis, distance):
    count = lax.axis_size(axis)
    return lax.ppermute(value, axis, [(source, source ^ distance) for source in range(count)])


def per_device(
    tokens, norm_gain, in_weight, bc_weight, dt_weight, dt_bias, decay_rate, out_gain, out_weight
):
    frames, rows, columns, width = tokens.shape
    heads = decay_rate.shape[1]
    inner = out_weight.shape[0]
    head_dim = inner // heads
    state = bc_weight.shape[1] // 4
    shares = lax.axis_size("tm")
    bands = lax.axis_size("height")
    groups = shares // rows
    group = inner // groups
    per_group = heads // groups
    length = frames * columns
    count = rows * length
    half = state // 2
    chunk_cols = 16
    blocks = parts = 2
    part_len = length // parts
    here = lax.axis_index("tm").astype(jnp.int32).reshape(1)
    band = lax.axis_index("height").astype(jnp.int32).reshape(1)

    packed = (shares, sum(packing(length, group)), group)
    blanks = [
        shape_of((frames * half, inner), BF16),
        shape_of((frames * half, inner), BF16),
        shape_of((count, inner), BF16),
        shape_of((count, inner), F32),
        shape_of((count, LANES), F32),
    ]
    entry = call(
        functools.partial(entry_kernel, shares, heads, state, blocks),
        "entry",
        [
            shape_of((count, width), BF16),
            shape_of(packed, BF16),
            shape_of((count, 2 * state), BF16),
            shape_of((count, LANES), F32),
            shape_of((16, LANES), F32),
        ]
        + [shape_of((frames * half + TAIL, inner), BF16)] * 2
        + [shape_of(packed[1:], BF16)] * shares
        + blanks,
        [SCALAR, SCALAR, HBM, WHOLE, WHOLE, WHOLE, HBM, HBM, HBM],
        limit=LARGE,
        outs=[HBM, HBM] + [WHOLE] * 5 + [HBM] * (shares + len(blanks)),
        scratch_shapes=[
            pltpu.VMEM((rows, frames, columns, width), BF16),
            pltpu.VMEM((2 * heads, width), BF16),
            pltpu.VMEM((width, 4 * state), BF16),
            pltpu.VMEM((width, inner), BF16),
            pltpu.VMEM((8, LANES), F32),
            pltpu.VMEM((count, width), BF16),
            pltpu.VMEM(packed, BF16),
            pltpu.SemaphoreType.DMA((rows * frames + 2 + blocks,)),
            pltpu.SemaphoreType.DMA((2 + shares,)),
        ],
    )(here, band, tokens, norm_gain, dt_bias, decay_rate, dt_weight.T, bc_weight, in_weight)
    normed, x, bc_own, logits, params, own, other = entry[:7]
    payloads, blanks = entry[7 : 7 + shares], entry[7 + shares :]

    def sent(parts):
        return [parts[0]] + [swapped(parts[d], "tm", d) for d in range(1, shares)]

    received = sent(payloads)

    def exchange(_, carried):
        other = carried[-1]
        far = swapped(other, "height", 1)
        gate = call(
            functools.partial(gate_kernel, blocks),
            "gate",
            shape_of((count, inner), BF16),
            [ANY, WHOLE, HBM],
            scratch_shapes=[
                pltpu.VMEM((width, inner), BF16),
                pltpu.SemaphoreType.DMA((blocks,)),
            ],
        )(other, normed, in_weight)

        out_local, reach = call(
            functools.partial(local_kernel, frames, rows, columns, head_dim, groups),
            "spatial_local",
            [shape_of((count, inner), F32), shape_of((count, LANES), F32)],
            [ANY] + [WHOLE] * 4,
        )(gate, bc_own, logits, params, x)

        total = call(
            functools.partial(pair_kernel, frames),
            "pair_total",
            shape_of((frames * half + TAIL, inner), BF16),
            [SCALAR, WHOLE, WHOLE],
        )(band, own, far)
        before = []
        distance = 2
        while distance < bands:
            far_total = swapped(total, "height", distance)
            finish = distance * 2 >= bands
            if distance == 2:
                spent = total
            operands = [reach, band, total, far_total] + before + ([own, far] if finish else [])
            outs = (
                [shape_of((frames * half, inner), BF16)] * 2
                if finish
                else [
                    shape_of((frames * half + TAIL, inner), BF16),
                    shape_of((frames * half + 8, inner), F32),
                ]
            )
            results = call(
                functools.partial(merge_kernel, frames, distance, finish),
                "merge",
                outs,
                [ANY, SCALAR] + [WHOLE] * (len(operands) - 2),
            )(*operands)
            if not finish:
                total, before = results[0], [results[1]]
            distance *= 2
        keep, give = results
        return keep, give, gate, out_local, reach, spent

    turns = jnp.where(band[0] < bands, 1, 2)
    keep, give, gate, out_local, reach, _ = lax.fori_loop(0, turns, exchange, (*blanks, other))
    came = swapped(give, "height", 1)

    returned, carried = [], []
    for part in range(parts):
        more = [shape_of((state, group), F32)] if part + 1 < parts else []
        results = call(
            functools.partial(
                temporal_kernel,
                part,
                parts,
                per_group,
                head_dim,
                rows,
                frames,
                columns,
                chunk_cols,
                shares,
                state,
            ),
            "temporal",
            [shape_of((part_len, group), BF16)] * shares + more,
            [SCALAR] + [WHOLE] * (1 + shares + len(carried)) + [ANY],
            scratch_shapes=[
                pltpu.VMEM((shares, part_len, state), BF16),
                pltpu.VMEM((shares, part_len, state), BF16),
                pltpu.VMEM((shares, part_len, LANES), F32),
                pltpu.VMEM((shares, part_len, LANES), F32),
            ],
        )(here, params, *received, *carried, reach)
        returned.append(sent(results[:shares]))
        carried = results[shares:]

    spatial_out = call(
        functools.partial(incoming_kernel, frames, rows, columns, head_dim),
        "spatial_incoming",
        shape_of((count, inner), F32),
        [SCALAR] + [WHOLE] * 5,
    )(band, out_local, bc_own, reach, keep, came)

    mixed = []
    for part in range(parts):
        mixed = [
            call(
                functools.partial(exit_kernel, part, parts, shares),
                "exit",
                shape_of(tokens.shape, BF16),
                [SCALAR] + [WHOLE] * (4 + shares) + [HBM] * len(mixed),
                outs=HBM,
                scratch_shapes=[
                    pltpu.VMEM((shares, part_len, group), BF16),
                    pltpu.VMEM((rows * part_len, inner), BF16),
                    pltpu.VMEM((rows * part_len, width), BF16),
                    pltpu.SemaphoreType.DMA((rows * frames,)),
                ],
                input_output_aliases={5 + shares: 0} if mixed else {},
            )(here, spatial_out, gate, out_gain, out_weight, *returned[part], *mixed)
        ]
    return mixed[0]


def solution(mesh):
    in_specs = (P("tm", "height", None, None), P(), P(), P(), P(), P(), P(), P(), P())
    out_specs = P("tm", "height", None, None)
    return jax.shard_map(
        per_device, mesh=mesh, in_specs=in_specs, out_specs=out_specs, check_vma=False
    )
```

```python
import functools
import math

import jax
import jax.numpy as jnp
from jax import lax
from jax.experimental import pallas as pl
from jax.experimental.pallas import tpu as pltpu
from jax.sharding import PartitionSpec as P

EPSILON = 1e-05
LANES = 128
TAIL = 16
LOG2_E = 1.4426950408889634
F32 = jnp.float32
BF16 = jnp.bfloat16
EXACT = lax.Precision.HIGHEST
LARGE = 56 * 1024 * 1024
SMALL = 24 * 1024 * 1024

ANY = pl.BlockSpec(memory_space=pl.ANY)
HBM = pl.BlockSpec(memory_space=pltpu.HBM)
SCALAR = pl.BlockSpec(memory_space=pltpu.SMEM)
WHOLE = pl.BlockSpec(memory_space=pltpu.VMEM)


def call(kernel, name, out_shape, in_specs, limit=SMALL, outs=None, **options):
    return pl.pallas_call(
        kernel,
        out_shape=out_shape,
        in_specs=in_specs,
        out_specs=jax.tree.map(lambda _: WHOLE, out_shape) if outs is None else outs,
        compiler_params=pltpu.CompilerParams(vmem_limit_bytes=limit),
        cost_estimate=pl.CostEstimate(flops=1, bytes_accessed=1, transcendentals=0),
        name=name,
        **options,
    )


def shape_of(shape, dtype):
    return jax.ShapeDtypeStruct(shape, dtype)


def dot(left, right, **options):
    return jnp.dot(left, right, preferred_element_type=F32, **options)


def dot_tn(left, right):
    return lax.dot_general(left, right, (((0,), (0,)), ((), ())), preferred_element_type=F32)


def dot_nt(left, right):
    return lax.dot_general(left, right, (((1,), (1,)), ((), ())), preferred_element_type=F32)


def softplus(values):
    return jnp.maximum(values, 0.0) + jnp.log1p(jnp.exp(-jnp.abs(values)))


def iota(shape, dim):
    return lax.broadcasted_iota(jnp.int32, shape, dim)


def spread_matrix(first_head, width, head_dim):
    return (iota((LANES, width), 0) - first_head == iota((LANES, width), 1) // head_dim).astype(BF16)


def spread(values, matrix):
    high = values.astype(BF16)
    low = (values - high.astype(F32)).astype(BF16)
    return dot(high, matrix) + dot(low, matrix)


def head_mixes(scores, running, running_t, dt_t, x, first_head, heads, head_dim):
    length = scores.shape[0]
    running, running_t = running * LOG2_E, running_t * LOG2_E
    outs = []

    def weights(head):
        spreads = running[:, head : head + 1] - running_t[head : head + 1, :]
        return (scores * jnp.exp2(jnp.minimum(spreads, 0.0)) * dt_t[head : head + 1, :]).astype(BF16)

    head = 0
    while head < heads:
        here = first_head + head
        if head + 1 < heads and 2 * head_dim == LANES:
            both = x[:, head * head_dim : (head + 2) * head_dim]
            first = iota((length, LANES), 1) < head_dim
            zero = jnp.zeros_like(both)
            stacked = jnp.concatenate([jnp.where(first, both, zero), jnp.where(first, zero, both)], axis=0)
            pair = jnp.concatenate([weights(here), weights(here + 1)], axis=1)
            outs.append(dot(pair, stacked))
            head += 2
        else:
            outs.append(dot(weights(here), x[:, head * head_dim : (head + 1) * head_dim]))
            head += 1
    return outs[0] if len(outs) == 1 else jnp.concatenate(outs, axis=1)


def column_copies(weight, scratch, sems, first, offset, blocks):
    width = scratch.shape[1] // blocks
    return [
        pltpu.make_async_copy(
            weight.at[:, pl.ds(offset + index * width, width)],
            scratch.at[:, pl.ds(index * width, width)],
            sems.at[first + index],
        )
        for index in range(blocks)
    ]


def packing(length, group):
    columns = group // LANES
    rest = -(-(2 * length + TAIL) // columns)
    return length, -(-rest // TAIL) * TAIL


def pack_rest(ref, length, b_proj, c_proj, dt):
    columns, rest = ref.shape[1] // LANES, ref.shape[0] - length
    blank = jnp.zeros((columns * rest - 2 * length - TAIL, LANES), BF16)
    stacked = jnp.concatenate([b_proj, c_proj, dt, blank], axis=0)
    for column in range(columns):
        ref[length:, column * LANES : (column + 1) * LANES] = stacked[column * rest : (column + 1) * rest]


def unpacked_rest(ref, length):
    columns = ref.shape[1] // LANES
    stacked = jnp.concatenate(
        [ref[length:, column * LANES : (column + 1) * LANES] for column in range(columns)], axis=0
    )
    return stacked[:length], stacked[length : 2 * length], stacked[2 * length : 2 * length + TAIL]


def entry_kernel(shares, heads, state, blocks, *refs):
    here_ref, band, tokens, gain, bias, rates, dt_weight, bc_weight, weight = refs[:9]
    normed_out, payload_out, bc_own, logits, params, own_states, other_states = refs[9:16]
    held, dt_held, bc_held, held_weight, table, normed, payload, sems, out_sems = refs[16:]
    frames, rows, columns, width = tokens.shape
    length = frames * columns
    count = rows * length
    groups = shares // rows
    per_group = heads // groups
    group = held_weight.shape[1] // groups

    token_copies = [
        pltpu.make_async_copy(tokens.at[frame, row], held.at[row, frame], sems.at[row * frames + frame])
        for row in range(rows)
        for frame in range(frames)
    ]
    for copy in token_copies:
        copy.start()
    first = rows * frames
    dt_copy = pltpu.make_async_copy(dt_weight, dt_held, sems.at[first])
    dt_copy.start()
    bc_copy = pltpu.make_async_copy(bc_weight, bc_held, sems.at[first + 1])
    bc_copy.start()
    copies = column_copies(weight, held_weight, sems, first + 2, 0, blocks)
    for copy in copies:
        copy.start()

    table[...] = jnp.zeros_like(table)
    table[0:1, : 2 * heads] = bias[...].reshape(1, 2 * heads)
    table[1:2, :heads] = rates[0:1, :]
    table[1:2, heads : 2 * heads] = rates[1:2, :]
    first_head = heads + here_ref[0] // rows * per_group
    lane_in, lane_out = iota((LANES, LANES), 0), iota((LANES, LANES), 1)
    own = ((lane_in == lane_out + first_head) & (lane_out < per_group)).astype(F32)
    params[0:8, :] = table[...]
    params[8:16, :] = dot(table[...], own, precision=EXACT)
    logits[...] = jnp.zeros_like(logits)

    gains = gain[...].reshape(1, width)
    for index, copy in enumerate(token_copies):
        copy.wait()
        values = held[index // frames, index % frames].astype(F32)
        mean_square = jnp.mean(values * values, axis=-1, keepdims=True)
        normed[index * columns : (index + 1) * columns, :] = (
            values * lax.rsqrt(mean_square + EPSILON) * gains
        ).astype(BF16)
    outgoing = [pltpu.make_async_copy(normed, normed_out, out_sems.at[0])]
    outgoing[0].start()
    dt_copy.wait()
    bc_copy.wait()
    for copy in copies:
        copy.wait()
    logits[:, : 2 * heads] = dot_nt(normed[...], dt_held[...]).astype(BF16).astype(F32)
    dt_heads = dot_nt(dt_held[heads:, :], normed[...])
    dt_heads = jnp.concatenate([dt_heads, jnp.zeros((TAIL, count), F32)], axis=0).astype(BF16)
    bc = dot(normed[...], bc_held[...]).astype(BF16)
    bc_own[...] = bc[:, : 2 * state]
    scan = [
        end_factors(frame_of(logits, frame, rows, frames, columns), params, rows * columns)
        for frame in range(frames)
    ]

    block = 2 * LANES if group % (2 * LANES) == 0 else group
    for part in range(groups):
        for at in range(0, group, block):
            from_col = part * group + at
            values = dot(normed[...], held_weight[:, from_col : from_col + block]).astype(BF16)
            for row in range(rows):
                payload[part * rows + row, :length, at : at + block] = values[
                    row * length : (row + 1) * length
                ]
        for row in range(rows):
            piece = part * rows + row
            here = slice(row * length, (row + 1) * length)
            pack_rest(
                payload.at[piece],
                length,
                bc[here, 2 * state : 3 * state],
                bc[here, 3 * state :],
                dt_heads[part * per_group : part * per_group + TAIL, here],
            )
            outgoing.append(
                pltpu.make_async_copy(payload.at[piece], payload_out.at[piece], out_sems.at[1 + piece])
            )
            outgoing[-1].start()
    half = state // 2
    head_dim = groups * group // heads
    mine = band[0] % 2 == 0
    for frame in range(frames):
        b_proj = frame_of(bc_own, frame, rows, frames, columns)[:, :state]
        for part in range(groups):
            at = slice(part * group, (part + 1) * group)
            values = frame_x(payload, part, frame, rows, columns)
            matrix = spread_matrix(part * per_group, group, head_dim)
            scaled = (values.astype(F32) * dot(scan[frame][0], matrix)).astype(BF16)
            fresh = dot_tn(b_proj, scaled).astype(BF16)
            at_rows = slice(frame * half, (frame + 1) * half)
            own_states[at_rows, at] = jnp.where(mine, fresh[:half], fresh[half:])
            other_states[at_rows, at] = jnp.where(mine, fresh[half:], fresh[:half])
    whole = [decay for _, decay in scan] + [jnp.zeros((8 - frames, LANES), F32)]
    decays = spread(jnp.concatenate(whole, axis=0), spread_matrix(0, groups * group, head_dim))
    tail = tail_of(decays)
    own_states[frames * half :, :] = tail
    other_states[frames * half :, :] = tail
    for copy in outgoing:
        copy.wait()


def gate_kernel(blocks, after, normed, weight, out, held_weight, sems):
    inner = held_weight.shape[1]
    copies = column_copies(weight, held_weight, sems, 0, inner, blocks)
    for copy in copies:
        copy.start()
    block = inner // blocks
    for index, copy in enumerate(copies):
        copy.wait()
        at = slice(index * block, (index + 1) * block)
        out[:, at] = dot(normed[...], held_weight[:, at]).astype(BF16)


def frame_of(ref, frame, rows, frames, columns):
    return jnp.concatenate(
        [
            ref[(row * frames + frame) * columns : (row * frames + frame + 1) * columns, :]
            for row in range(rows)
        ],
        axis=0,
    )


def frame_x(payload, part, frame, rows, columns):
    return jnp.concatenate(
        [
            payload[part * rows + row, frame * columns : (frame + 1) * columns, :]
            for row in range(rows)
        ],
        axis=0,
    )


def scan_terms(logits, params, causal):
    dt = softplus(logits + params[0:1, :])
    running = dot(causal.astype(F32), -dt * params[1:2, :], precision=EXACT)
    return dt, running, jnp.min(running, axis=0, keepdims=True)


def end_factors(logits, params, length):
    causal = iota((length, length), 0) >= iota((length, length), 1)
    dt, running, last = scan_terms(logits, params, causal)
    return (jnp.exp(last - running) * dt).astype(BF16), jnp.exp(last)


def local_kernel(frames, rows, columns, head_dim, groups, *refs):
    after, bc, logits, params, x, out, reach = refs
    length = rows * columns
    group = x.shape[2]
    state = bc.shape[1] // 2
    per_group = group // head_dim
    causal = iota((length, length), 0) >= iota((length, length), 1)

    def stored(ref, values, frame, at):
        for row in range(rows):
            to = (row * frames + frame) * columns
            ref[to : to + columns, at] = values[row * columns : (row + 1) * columns]

    for frame in range(frames):
        dt, running, _ = scan_terms(frame_of(logits, frame, rows, frames, columns), params, causal)
        running_t, dt_t = jnp.transpose(running), jnp.transpose(dt)
        bc_rows = frame_of(bc, frame, rows, frames, columns)
        scores = jnp.where(causal, dot_nt(bc_rows[:, state:], bc_rows[:, :state]), 0.0)
        stored(reach, jnp.exp(running), frame, slice(None))
        for piece in range(groups):
            values = frame_x(x, piece, frame, rows, columns)
            mixed = head_mixes(
                scores, running, running_t, dt_t, values, piece * per_group, per_group, head_dim
            )
            stored(out, mixed, frame, slice(piece * group, (piece + 1) * group))


def tail_of(decays):
    high = decays.astype(BF16)
    return jnp.concatenate([high, (decays - high.astype(F32)).astype(BF16)], axis=0)


def pair_kernel(frames, band, own, far, total):
    rows = (own.shape[0] - TAIL) // frames
    own_decay = own[-TAIL:-8, :].astype(F32) + own[-8:, :].astype(F32)
    far_decay = far[-TAIL:-8, :].astype(F32) + far[-8:, :].astype(F32)
    lower = band[0] % 2 == 0
    through = jnp.where(lower, far_decay, own_decay)
    for frame in range(frames):
        at = slice(frame * rows, (frame + 1) * rows)
        first = jnp.where(lower, own[at, :], far[at, :]).astype(F32)
        second = jnp.where(lower, far[at, :], own[at, :]).astype(F32)
        total[at, :] = (through[frame : frame + 1, :] * first + second).astype(BF16)
    total[frames * rows :, :] = tail_of(own_decay * far_decay)


def merge_kernel(frames, distance, finish, *refs):
    _, band, own, far = refs[:4]
    start = distance == 2
    rest = list(refs[4:])
    before_in = None if start else rest.pop(0)
    band_own, band_far = (rest.pop(0), rest.pop(0)) if finish else (None, None)
    rows = (own.shape[0] - TAIL) // frames
    upper, lower_band = (band[0] // distance) % 2 == 1, band[0] % 2 == 0
    own_decay = own[-TAIL:-8, :].astype(F32) + own[-8:, :].astype(F32)
    far_decay = far[-TAIL:-8, :].astype(F32) + far[-8:, :].astype(F32)
    if start:
        before_decay = jnp.ones_like(own_decay)
    else:
        before_decay = before_in[-8:, :]
    if finish:
        first_decay = jnp.where(
            lower_band,
            band_own[-TAIL:-8, :].astype(F32) + band_own[-8:, :].astype(F32),
            band_far[-TAIL:-8, :].astype(F32) + band_far[-8:, :].astype(F32),
        )
    through = jnp.where(upper, own_decay, far_decay)
    for frame in range(frames):
        at = slice(frame * rows, (frame + 1) * rows)
        row = slice(frame, frame + 1)
        far_state = far[at, :].astype(F32)
        came = before_decay[row, :] * far_state
        if not start:
            came = came + before_in[at, :]
        before = jnp.where(upper, came, 0.0 if start else before_in[at, :])
        if finish:
            keep, give = rest
            first = jnp.where(lower_band, band_own[at, :], band_far[at, :]).astype(F32)
            after = first_decay[row, :] * before + first
            keep[at, :] = jnp.where(lower_band, before, after).astype(BF16)
            give[at, :] = jnp.where(lower_band, after, before).astype(BF16)
        else:
            total, before_out = rest
            own_state = own[at, :].astype(F32)
            early = jnp.where(upper, far_state, own_state)
            late = jnp.where(upper, own_state, far_state)
            total[at, :] = (through[row, :] * early + late).astype(BF16)
            before_out[at, :] = before
    if not finish:
        total[frames * rows :, :] = tail_of(own_decay * far_decay)
        before_out[frames * rows :, :] = jnp.where(upper, before_decay * far_decay, before_decay)


def incoming_kernel(
    frames, rows, columns, head_dim, band, out_local, bc, reach, own, other, weight, out, held, sem
):
    fetch = pltpu.make_async_copy(weight, held, sem)
    fetch.start()
    state = bc.shape[1] // 2
    half = state // 2
    inner = out.shape[1]
    mine = band[0] % 2 == 0
    matrix = spread_matrix(0, inner, head_dim)
    for frame in range(frames):
        at = slice(frame * half, (frame + 1) * half)
        low = jnp.where(mine, own[at, :], other[at, :])
        high = jnp.where(mine, other[at, :], own[at, :])
        carried = jnp.concatenate([low, high], axis=0)
        for row in range(rows):
            to = (row * frames + frame) * columns
            here = slice(to, to + columns)
            factor = spread(reach[here, :], matrix)
            out[here, :] = out_local[here, :] + factor * dot(bc[here, state:], carried)
    fetch.wait()


def temporal_kernel(
    part, parts, per_group, head_dim, rows, frames, columns, chunk_cols, shares, state, *refs
):
    here_ref, params, payload = refs[:3]
    rest = list(refs[3:])
    carried_in = rest.pop(0) if part > 0 else None
    outs, rest = rest[:shares], rest[shares:]
    carried_out = rest.pop(0) if part + 1 < parts else None
    b_all, c_all, dt_all, decay_all = rest
    here = here_ref[0]
    length = frames * columns
    part_cols = columns // parts
    group = outs[0].shape[1]
    eye = (iota((TAIL, LANES), 0) == iota((TAIL, LANES), 1)) & (iota((TAIL, LANES), 1) < per_group)
    eye = eye.astype(BF16)

    def came(distance):
        return payload.at[here ^ distance]

    for distance in range(shares):
        b_proj, c_proj, logits = unpacked_rest(came(distance), length)
        logits = dot_tn(logits, eye)
        for frame in range(frames):
            at = slice(frame * columns + part * part_cols, frame * columns + (part + 1) * part_cols)
            to = slice(frame * part_cols, (frame + 1) * part_cols)
            b_all[distance, to] = b_proj[at]
            c_all[distance, to] = c_proj[at]
            dt = softplus(logits[at] + params[8:9, :])
            dt_all[distance, to] = dt
            decay_all[distance, to] = -dt * params[9:10, :]

    all_frames = shares * frames
    size = all_frames * chunk_cols

    def order_key(dim):
        index = iota((size, size), dim)
        source = here ^ (index // (frames * chunk_cols))
        frame = source * frames + (index // chunk_cols) % frames
        return (index % chunk_cols) * all_frames + frame

    causal = order_key(0) >= order_key(1)
    order = causal.astype(F32)
    matrix = spread_matrix(0, group, head_dim)
    carried = jnp.zeros((state, group), F32) if part == 0 else carried_in[...]
    places = [(source, frame) for source in range(shares) for frame in range(frames)]
    for chunk in range(part_cols // chunk_cols):

        def gathered(ref_of, pitch=part_cols, offset=0):
            return jnp.concatenate(
                [
                    ref_of(source)[pl.ds(frame * pitch + offset + chunk * chunk_cols, chunk_cols), :]
                    for source, frame in places
                ],
                axis=0,
            )

        values = gathered(came, columns, part * part_cols)
        b_proj = gathered(lambda source: b_all.at[source])
        c_proj = gathered(lambda source: c_all.at[source])
        dt = gathered(lambda source: dt_all.at[source])
        running = dot(order, gathered(lambda source: decay_all.at[source]), precision=EXACT)
        running_t, dt_t = jnp.transpose(running), jnp.transpose(dt)
        scores = jnp.where(causal, dot_nt(c_proj, b_proj), 0.0)
        last = jnp.min(running, axis=0, keepdims=True)
        mixed = head_mixes(scores, running, running_t, dt_t, values, 0, per_group, head_dim)
        ends = jnp.concatenate([running, jnp.broadcast_to(last, (8, LANES))], axis=0)
        reach = dot(jnp.exp(ends).astype(BF16), matrix)
        mixed = mixed + reach[:size] * dot(c_proj, carried.astype(BF16))
        to_end = (jnp.exp(last - running) * dt).astype(BF16)
        scaled = (values.astype(F32) * dot(to_end, matrix)).astype(BF16)
        carried = reach[size : size + 1, :] * carried + dot_tn(b_proj, scaled)
        mixed = mixed.astype(BF16)
        for index, (source, frame) in enumerate(places):
            to = frame * part_cols + chunk * chunk_cols
            outs[source][to : to + chunk_cols, :] = mixed[index * chunk_cols : (index + 1) * chunk_cols]
    if carried_out is not None:
        carried_out[...] = carried


def exit_kernel(part, parts, shares, *refs):
    here, spatial, gate, gain, weight = refs[:5]
    out, temporal, normed, mixed, sems = refs[-5:]
    frames, rows, columns, _ = out.shape
    part_cols = columns // parts
    _, part_len, group = temporal.shape
    groups = shares // rows
    inner = groups * group
    for distance in range(shares):
        temporal[here[0] ^ distance] = refs[5 + distance][...]

    def own(ref, row, at):
        return jnp.concatenate(
            [
                ref[pl.ds((row * frames + frame) * columns + part * part_cols, part_cols), at]
                for frame in range(frames)
            ],
            axis=0,
        )

    gains = gain[...].reshape(1, inner)
    for row in range(rows):
        total = jnp.zeros((part_len, 1), F32)
        kept = []
        for index in range(groups):
            at = slice(index * group, (index + 1) * group)
            gates = own(gate, row, at).astype(F32)
            gated = own(spatial, row, at) + temporal[index * rows + row].astype(F32)
            gated = gated * (gates / (1.0 + jnp.exp(-gates)))
            total = total + jnp.sum(gated * gated, axis=1, keepdims=True)
            kept.append(gated)
        scale = lax.rsqrt(total / inner + EPSILON)
        for index, gated in enumerate(kept):
            at = slice(index * group, (index + 1) * group)
            normed[row * part_len : (row + 1) * part_len, at] = (gated * scale * gains[:, at]).astype(BF16)
    mixed[...] = dot(normed[...], weight[...]).astype(BF16)
    copies = [
        pltpu.make_async_copy(
            mixed.at[pl.ds((row * frames + frame) * part_cols, part_cols), :],
            out.at[frame, row, pl.ds(part * part_cols, part_cols), :],
            sems.at[row * frames + frame],
        )
        for row in range(rows)
        for frame in range(frames)
    ]
    for copy in copies:
        copy.start()
    for copy in copies:
        copy.wait()


def swapped(value, axis, distance):
    count = lax.axis_size(axis)
    return lax.ppermute(value, axis, [(source, source ^ distance) for source in range(count)])


def per_device(
    tokens, norm_gain, in_weight, bc_weight, dt_weight, dt_bias, decay_rate, out_gain, out_weight
):
    frames, rows, columns, width = tokens.shape
    heads = decay_rate.shape[1]
    inner = out_weight.shape[0]
    head_dim = inner // heads
    state = bc_weight.shape[1] // 4
    shares = lax.axis_size("tm")
    bands = lax.axis_size("height")
    groups = shares // rows
    group = inner // groups
    per_group = heads // groups
    length = frames * columns
    count = rows * length
    half = state // 2
    chunk_cols = 16
    blocks = parts = 2
    part_len = length // parts
    here = lax.axis_index("tm").astype(jnp.int32).reshape(1)
    band = lax.axis_index("height").astype(jnp.int32).reshape(1)

    packed = (shares, sum(packing(length, group)), group)
    normed, payload, bc_own, logits, params, own, other = call(
        functools.partial(entry_kernel, shares, heads, state, blocks),
        "entry",
        [
            shape_of((count, width), BF16),
            shape_of(packed, BF16),
            shape_of((count, 2 * state), BF16),
            shape_of((count, LANES), F32),
            shape_of((16, LANES), F32),
        ]
        + [shape_of((frames * half + TAIL, inner), BF16)] * 2,
        [SCALAR, SCALAR, HBM, WHOLE, WHOLE, WHOLE, HBM, HBM, HBM],
        limit=LARGE,
        outs=[HBM, HBM] + [WHOLE] * 5,
        scratch_shapes=[
            pltpu.VMEM((rows, frames, columns, width), BF16),
            pltpu.VMEM((2 * heads, width), BF16),
            pltpu.VMEM((width, 4 * state), BF16),
            pltpu.VMEM((width, inner), BF16),
            pltpu.VMEM((8, LANES), F32),
            pltpu.VMEM((count, width), BF16),
            pltpu.VMEM(packed, BF16),
            pltpu.SemaphoreType.DMA((rows * frames + 2 + blocks,)),
            pltpu.SemaphoreType.DMA((1 + shares,)),
        ],
    )(here, band, tokens, norm_gain, dt_bias, decay_rate, dt_weight.T, bc_weight, in_weight)

    def sent(parts):
        return [parts[0]] + [swapped(parts[d], "tm", d) for d in range(1, shares)]

    received = lax.all_to_all(payload, "tm", split_axis=0, concat_axis=0, tiled=True)
    far = swapped(other, "height", 1)
    gate = call(
        functools.partial(gate_kernel, blocks),
        "gate",
        shape_of((count, inner), BF16),
        [ANY, WHOLE, HBM],
        scratch_shapes=[
            pltpu.VMEM((width, inner), BF16),
            pltpu.SemaphoreType.DMA((blocks,)),
        ],
    )(payload, normed, in_weight)

    out_local, reach = call(
        functools.partial(local_kernel, frames, rows, columns, head_dim, groups),
        "spatial_local",
        [shape_of((count, inner), F32), shape_of((count, LANES), F32)],
        [ANY] + [WHOLE] * 4,
    )(gate, bc_own, logits, params, payload)

    total = call(
        functools.partial(pair_kernel, frames),
        "pair_total",
        shape_of((frames * half + TAIL, inner), BF16),
        [SCALAR, WHOLE, WHOLE],
    )(band, own, far)
    returned, carried = [], []
    for part in range(parts):
        more = [shape_of((state, group), F32)] if part + 1 < parts else []
        results = call(
            functools.partial(
                temporal_kernel,
                part,
                parts,
                per_group,
                head_dim,
                rows,
                frames,
                columns,
                chunk_cols,
                shares,
                state,
            ),
            "temporal",
            [shape_of((part_len, group), BF16)] * shares + more,
            [SCALAR] + [WHOLE] * (2 + len(carried)),
            scratch_shapes=[
                pltpu.VMEM((shares, part_len, state), BF16),
                pltpu.VMEM((shares, part_len, state), BF16),
                pltpu.VMEM((shares, part_len, LANES), F32),
                pltpu.VMEM((shares, part_len, LANES), F32),
            ],
        )(here, params, received, *carried)
        returned.append(sent(results[:shares]))
        carried = results[shares:]

    before = []
    distance = 2
    while distance < bands:
        far_total = swapped(total, "height", distance)
        finish = distance * 2 >= bands
        operands = [reach, band, total, far_total] + before + ([own, far] if finish else [])
        outs = (
            [shape_of((frames * half, inner), BF16)] * 2
            if finish
            else [
                shape_of((frames * half + TAIL, inner), BF16),
                shape_of((frames * half + 8, inner), F32),
            ]
        )
        results = call(
            functools.partial(merge_kernel, frames, distance, finish),
            "merge",
            outs,
            [ANY, SCALAR] + [WHOLE] * (len(operands) - 2),
        )(*operands)
        if not finish:
            total, before = results[0], [results[1]]
        distance *= 2
    keep, give = results
    came = swapped(give, "height", 1)

    spatial_out, held_weight = call(
        functools.partial(incoming_kernel, frames, rows, columns, head_dim),
        "spatial_incoming",
        [shape_of((count, inner), F32), shape_of((inner, width), BF16)],
        [SCALAR] + [WHOLE] * 5 + [HBM],
        scratch_shapes=[pltpu.SemaphoreType.DMA],
    )(band, out_local, bc_own, reach, keep, came, out_weight)

    mixed = []
    for part in range(parts):
        mixed = [
            call(
                functools.partial(exit_kernel, part, parts, shares),
                "exit",
                shape_of(tokens.shape, BF16),
                [SCALAR] + [WHOLE] * (4 + shares) + [HBM] * len(mixed),
                outs=HBM,
                scratch_shapes=[
                    pltpu.VMEM((shares, part_len, group), BF16),
                    pltpu.VMEM((rows * part_len, inner), BF16),
                    pltpu.VMEM((rows * part_len, width), BF16),
                    pltpu.SemaphoreType.DMA((rows * frames,)),
                ],
                input_output_aliases={5 + shares: 0} if mixed else {},
            )(here, spatial_out, gate, out_gain, held_weight, *returned[part], *mixed)
        ]
    return mixed[0]


def solution(mesh):
    in_specs = (P("tm", "height", None, None), P(), P(), P(), P(), P(), P(), P(), P())
    out_specs = P("tm", "height", None, None)
    return jax.shard_map(
        per_device, mesh=mesh, in_specs=in_specs, out_specs=out_specs, check_vma=False
    )
```

```python
import functools
import math

import jax
import jax.numpy as jnp
from jax import lax
from jax.experimental import pallas as pl
from jax.experimental.pallas import tpu as pltpu
from jax.sharding import PartitionSpec as P

EPSILON = 1e-05
LANES = 128
TAIL = 16
LOG2_E = 1.4426950408889634
F32 = jnp.float32
BF16 = jnp.bfloat16
EXACT = lax.Precision.HIGHEST
LARGE = 56 * 1024 * 1024
SMALL = 24 * 1024 * 1024

ANY = pl.BlockSpec(memory_space=pl.ANY)
HBM = pl.BlockSpec(memory_space=pltpu.HBM)
SCALAR = pl.BlockSpec(memory_space=pltpu.SMEM)
WHOLE = pl.BlockSpec(memory_space=pltpu.VMEM)


def call(kernel, name, out_shape, in_specs, limit=SMALL, outs=None, **options):
    return pl.pallas_call(
        kernel,
        out_shape=out_shape,
        in_specs=in_specs,
        out_specs=jax.tree.map(lambda _: WHOLE, out_shape) if outs is None else outs,
        compiler_params=pltpu.CompilerParams(vmem_limit_bytes=limit),
        cost_estimate=pl.CostEstimate(flops=1, bytes_accessed=1, transcendentals=0),
        name=name,
        **options,
    )


def shape_of(shape, dtype):
    return jax.ShapeDtypeStruct(shape, dtype)


def dot(left, right, **options):
    return jnp.dot(left, right, preferred_element_type=F32, **options)


def dot_tn(left, right):
    return lax.dot_general(left, right, (((0,), (0,)), ((), ())), preferred_element_type=F32)


def dot_nt(left, right):
    return lax.dot_general(left, right, (((1,), (1,)), ((), ())), preferred_element_type=F32)


def softplus(values):
    return jnp.maximum(values, 0.0) + jnp.log1p(jnp.exp(-jnp.abs(values)))


def iota(shape, dim):
    return lax.broadcasted_iota(jnp.int32, shape, dim)


def spread_matrix(first_head, width, head_dim):
    return (iota((LANES, width), 0) - first_head == iota((LANES, width), 1) // head_dim).astype(BF16)


def spread(values, matrix):
    high = values.astype(BF16)
    low = (values - high.astype(F32)).astype(BF16)
    return dot(high, matrix) + dot(low, matrix)


def head_mixes(scores, running, running_t, dt_t, x, first_head, heads, head_dim):
    length = scores.shape[0]
    running, running_t = running * LOG2_E, running_t * LOG2_E
    outs = []

    def weights(head):
        spreads = running[:, head : head + 1] - running_t[head : head + 1, :]
        return (scores * jnp.exp2(jnp.minimum(spreads, 0.0)) * dt_t[head : head + 1, :]).astype(BF16)

    head = 0
    while head < heads:
        here = first_head + head
        if head + 1 < heads and 2 * head_dim == LANES:
            both = x[:, head * head_dim : (head + 2) * head_dim]
            first = iota((length, LANES), 1) < head_dim
            zero = jnp.zeros_like(both)
            stacked = jnp.concatenate([jnp.where(first, both, zero), jnp.where(first, zero, both)], axis=0)
            pair = jnp.concatenate([weights(here), weights(here + 1)], axis=1)
            outs.append(dot(pair, stacked))
            head += 2
        else:
            outs.append(dot(weights(here), x[:, head * head_dim : (head + 1) * head_dim]))
            head += 1
    return outs[0] if len(outs) == 1 else jnp.concatenate(outs, axis=1)


def column_copies(weight, scratch, sems, first, offset, blocks):
    width = scratch.shape[1] // blocks
    return [
        pltpu.make_async_copy(
            weight.at[:, pl.ds(offset + index * width, width)],
            scratch.at[:, pl.ds(index * width, width)],
            sems.at[first + index],
        )
        for index in range(blocks)
    ]


def packing(length, group):
    columns = group // LANES
    rest = -(-(2 * length + TAIL) // columns)
    return length, -(-rest // TAIL) * TAIL


def pack_rest(ref, length, b_proj, c_proj, dt):
    columns, rest = ref.shape[1] // LANES, ref.shape[0] - length
    blank = jnp.zeros((columns * rest - 2 * length - TAIL, LANES), BF16)
    stacked = jnp.concatenate([b_proj, c_proj, dt, blank], axis=0)
    for column in range(columns):
        ref[length:, column * LANES : (column + 1) * LANES] = stacked[column * rest : (column + 1) * rest]


def unpacked_rest(ref, length):
    columns = ref.shape[1] // LANES
    stacked = jnp.concatenate(
        [ref[length:, column * LANES : (column + 1) * LANES] for column in range(columns)], axis=0
    )
    return stacked[:length], stacked[length : 2 * length], stacked[2 * length : 2 * length + TAIL]


def entry_kernel(shares, heads, state, blocks, *refs):
    here_ref, band, tokens, gain, bias, rates, dt_weight, bc_weight, weight = refs[:9]
    normed_out, payload_out, bc_own, logits, params, own_states, other_states, band_decays = refs[9:17]
    held, dt_held, bc_held, held_weight, table, normed, payload, sems, out_sems = refs[17:]
    frames, rows, columns, width = tokens.shape
    length = frames * columns
    count = rows * length
    groups = shares // rows
    per_group = heads // groups
    group = held_weight.shape[1] // groups

    token_copies = [
        pltpu.make_async_copy(tokens.at[frame, row], held.at[row, frame], sems.at[row * frames + frame])
        for row in range(rows)
        for frame in range(frames)
    ]
    for copy in token_copies:
        copy.start()
    first = rows * frames
    dt_copy = pltpu.make_async_copy(dt_weight, dt_held, sems.at[first])
    dt_copy.start()
    bc_copy = pltpu.make_async_copy(bc_weight, bc_held, sems.at[first + 1])
    bc_copy.start()
    copies = column_copies(weight, held_weight, sems, first + 2, 0, blocks)
    for copy in copies:
        copy.start()

    table[...] = jnp.zeros_like(table)
    table[0:1, : 2 * heads] = bias[...].reshape(1, 2 * heads)
    table[1:2, :heads] = rates[0:1, :]
    table[1:2, heads : 2 * heads] = rates[1:2, :]
    first_head = heads + here_ref[0] // rows * per_group
    lane_in, lane_out = iota((LANES, LANES), 0), iota((LANES, LANES), 1)
    own = ((lane_in == lane_out + first_head) & (lane_out < per_group)).astype(F32)
    params[0:8, :] = table[...]
    params[8:16, :] = dot(table[...], own, precision=EXACT)
    logits[...] = jnp.zeros_like(logits)

    gains = gain[...].reshape(1, width)
    for index, copy in enumerate(token_copies):
        copy.wait()
        values = held[index // frames, index % frames].astype(F32)
        mean_square = jnp.mean(values * values, axis=-1, keepdims=True)
        normed[index * columns : (index + 1) * columns, :] = (
            values * lax.rsqrt(mean_square + EPSILON) * gains
        ).astype(BF16)
    outgoing = [pltpu.make_async_copy(normed, normed_out, out_sems.at[0])]
    outgoing[0].start()
    dt_copy.wait()
    logits[:, : 2 * heads] = dot_nt(normed[...], dt_held[...]).astype(BF16).astype(F32)
    dt_heads = dot_nt(dt_held[heads:, :], normed[...])
    dt_heads = jnp.concatenate([dt_heads, jnp.zeros((TAIL, count), F32)], axis=0).astype(BF16)
    bc_copy.wait()
    bc = dot(normed[...], bc_held[...]).astype(BF16)
    bc_own[...] = bc[:, : 2 * state]
    scan = [
        end_factors(frame_of(logits, frame, rows, frames, columns), params, rows * columns)
        for frame in range(frames)
    ]

    block = held_weight.shape[1] // blocks
    for index, copy in enumerate(copies):
        copy.wait()
        at = index * block
        values = dot(normed[...], held_weight[:, at : at + block]).astype(BF16)
        for inside in range(0, block, group):
            part = (at + inside) // group
            for row in range(rows):
                piece = part * rows + row
                here = slice(row * length, (row + 1) * length)
                payload[piece, :length, :] = values[here, inside : inside + group]
                pack_rest(
                    payload.at[piece],
                    length,
                    bc[here, 2 * state : 3 * state],
                    bc[here, 3 * state :],
                    dt_heads[part * per_group : part * per_group + TAIL, here],
                )
                outgoing.append(
                    pltpu.make_async_copy(
                        payload.at[piece], payload_out.at[piece], out_sems.at[1 + piece]
                    )
                )
                outgoing[-1].start()
    half = state // 2
    head_dim = groups * group // heads
    mine = band[0] % 2 == 0
    for frame in range(frames):
        b_proj = frame_of(bc_own, frame, rows, frames, columns)[:, :state]
        for part in range(groups):
            at = slice(part * group, (part + 1) * group)
            values = frame_x(payload, part, frame, rows, columns)
            matrix = spread_matrix(part * per_group, group, head_dim)
            scaled = (values.astype(F32) * dot(scan[frame][0], matrix)).astype(BF16)
            fresh = dot_tn(b_proj, scaled).astype(BF16)
            at_rows = slice(frame * half, (frame + 1) * half)
            own_states[at_rows, at] = jnp.where(mine, fresh[:half], fresh[half:])
            other_states[at_rows, at] = jnp.where(mine, fresh[half:], fresh[:half])
    whole = [decay for _, decay in scan] + [jnp.zeros((8 - frames, LANES), F32)]
    decays = spread(jnp.concatenate(whole, axis=0), spread_matrix(0, groups * group, head_dim))
    tail = tail_of(decays)
    own_states[frames * half :, :] = tail
    other_states[frames * half :, :] = tail
    band_decays[...] = tail
    for copy in outgoing:
        copy.wait()


def gate_kernel(blocks, after, normed, weight, out, held_weight, sems):
    inner = held_weight.shape[1]
    copies = column_copies(weight, held_weight, sems, 0, inner, blocks)
    for copy in copies:
        copy.start()
    block = inner // blocks
    for index, copy in enumerate(copies):
        copy.wait()
        at = slice(index * block, (index + 1) * block)
        out[:, at] = dot(normed[...], held_weight[:, at]).astype(BF16)


def frame_of(ref, frame, rows, frames, columns):
    return jnp.concatenate(
        [
            ref[(row * frames + frame) * columns : (row * frames + frame + 1) * columns, :]
            for row in range(rows)
        ],
        axis=0,
    )


def frame_x(payload, part, frame, rows, columns):
    return jnp.concatenate(
        [
            payload[part * rows + row, frame * columns : (frame + 1) * columns, :]
            for row in range(rows)
        ],
        axis=0,
    )


def scan_terms(logits, params, causal):
    dt = softplus(logits + params[0:1, :])
    running = dot(causal.astype(F32), -dt * params[1:2, :], precision=EXACT)
    return dt, running, jnp.min(running, axis=0, keepdims=True)


def end_factors(logits, params, length):
    causal = iota((length, length), 0) >= iota((length, length), 1)
    dt, running, last = scan_terms(logits, params, causal)
    return (jnp.exp(last - running) * dt).astype(BF16), jnp.exp(last)


def local_kernel(frames, rows, columns, head_dim, groups, *refs):
    after, bc, logits, params, x, out, reach = refs
    length = rows * columns
    group = x.shape[2]
    state = bc.shape[1] // 2
    per_group = group // head_dim
    causal = iota((length, length), 0) >= iota((length, length), 1)

    def stored(ref, values, frame, at):
        for row in range(rows):
            to = (row * frames + frame) * columns
            ref[to : to + columns, at] = values[row * columns : (row + 1) * columns]

    for frame in range(frames):
        dt, running, _ = scan_terms(frame_of(logits, frame, rows, frames, columns), params, causal)
        running_t, dt_t = jnp.transpose(running), jnp.transpose(dt)
        bc_rows = frame_of(bc, frame, rows, frames, columns)
        scores = jnp.where(causal, dot_nt(bc_rows[:, state:], bc_rows[:, :state]), 0.0)
        stored(reach, jnp.exp(running), frame, slice(None))
        for piece in range(groups):
            values = frame_x(x, piece, frame, rows, columns)
            mixed = head_mixes(
                scores, running, running_t, dt_t, values, piece * per_group, per_group, head_dim
            )
            stored(out, mixed, frame, slice(piece * group, (piece + 1) * group))


def tail_of(decays):
    high = decays.astype(BF16)
    return jnp.concatenate([high, (decays - high.astype(F32)).astype(BF16)], axis=0)


def pair_kernel(frames, band, own, far, total):
    rows = (own.shape[0] - TAIL) // frames
    own_decay = own[-TAIL:-8, :].astype(F32) + own[-8:, :].astype(F32)
    far_decay = far[-TAIL:-8, :].astype(F32) + far[-8:, :].astype(F32)
    lower = band[0] % 2 == 0
    through = jnp.where(lower, far_decay, own_decay)
    for frame in range(frames):
        at = slice(frame * rows, (frame + 1) * rows)
        first = jnp.where(lower, own[at, :], far[at, :]).astype(F32)
        second = jnp.where(lower, far[at, :], own[at, :]).astype(F32)
        total[at, :] = (through[frame : frame + 1, :] * first + second).astype(BF16)
    total[frames * rows :, :] = tail_of(own_decay * far_decay)


def merge_kernel(frames, distance, finish, *refs):
    _, band, own, far = refs[:4]
    start = distance == 2
    rest = list(refs[4:])
    before_in = None if start else rest.pop(0)
    band_own, band_far = (rest.pop(0), rest.pop(0)) if finish else (None, None)
    rows = (own.shape[0] - TAIL) // frames
    upper, lower_band = (band[0] // distance) % 2 == 1, band[0] % 2 == 0
    own_decay = own[-TAIL:-8, :].astype(F32) + own[-8:, :].astype(F32)
    far_decay = far[-TAIL:-8, :].astype(F32) + far[-8:, :].astype(F32)
    if start:
        before_decay = jnp.ones_like(own_decay)
    else:
        before_decay = before_in[-8:, :]
    if finish:
        first_decay = jnp.where(
            lower_band,
            band_own[-TAIL:-8, :].astype(F32) + band_own[-8:, :].astype(F32),
            band_far[-TAIL:-8, :].astype(F32) + band_far[-8:, :].astype(F32),
        )
    through = jnp.where(upper, own_decay, far_decay)
    for frame in range(frames):
        at = slice(frame * rows, (frame + 1) * rows)
        row = slice(frame, frame + 1)
        far_state = far[at, :].astype(F32)
        came = before_decay[row, :] * far_state
        if not start:
            came = came + before_in[at, :]
        before = jnp.where(upper, came, 0.0 if start else before_in[at, :])
        if finish:
            keep, give = rest
            first = jnp.where(lower_band, band_own[at, :], band_far[at, :]).astype(F32)
            after = first_decay[row, :] * before + first
            keep[at, :] = jnp.where(lower_band, before, after).astype(BF16)
            give[at, :] = jnp.where(lower_band, after, before).astype(BF16)
        else:
            total, before_out = rest
            own_state = own[at, :].astype(F32)
            early = jnp.where(upper, far_state, own_state)
            late = jnp.where(upper, own_state, far_state)
            total[at, :] = (through[row, :] * early + late).astype(BF16)
            before_out[at, :] = before
    if not finish:
        total[frames * rows :, :] = tail_of(own_decay * far_decay)
        before_out[frames * rows :, :] = jnp.where(upper, before_decay * far_decay, before_decay)


def decays_of(ref):
    return ref[-TAIL:-8, :].astype(F32) + ref[-8:, :].astype(F32)


def places_of(band):
    return band % 2 == 0, (band // 2) % 2 == 1, band // 4 == 1


def cross_kernel(frames, _, band, total, first, near, far, message):
    even, x_high, y_high = places_of(band[0])
    own_decay, first_decay = decays_of(total), decays_of(first)
    diagonal = decays_of(near) * decays_of(far)
    one, zero = jnp.ones_like(own_decay), jnp.zeros_like(own_decay)
    odd_first = jnp.where(y_high, jnp.where(x_high, one, own_decay * diagonal), zero)
    odd_own = jnp.where(x_high & y_high, zero, one)
    of_first = jnp.where(even, jnp.where(x_high, own_decay, one), odd_first)
    of_own = jnp.where(even, jnp.where(x_high, one, first_decay), odd_own)
    rows = (total.shape[0] - TAIL) // frames
    for frame in range(frames):
        at, row = slice(frame * rows, (frame + 1) * rows), slice(frame, frame + 1)
        sent = of_first[row] * first[at, :].astype(F32) + of_own[row] * total[at, :].astype(F32)
        message[at, :] = sent.astype(BF16)
    message[frames * rows :, :] = tail_of(jnp.where(even, own_decay * first_decay, own_decay))


def settle_kernel(frames, _, band, first, second, near, far, band_own, band_far, keep, give):
    even, x_high, y_high = places_of(band[0])
    first_decay, second_decay = decays_of(first), decays_of(second)
    diagonal = decays_of(near) * decays_of(far)
    one, zero = jnp.ones_like(first_decay), jnp.zeros_like(first_decay)
    even_second = jnp.where(y_high, jnp.where(x_high, first_decay, one), zero)
    odd_second = jnp.where(x_high | y_high, one, zero)
    odd_first = jnp.where(y_high, jnp.where(x_high, second_decay, diagonal), zero)
    of_second = jnp.where(even, even_second, odd_second)
    of_first = jnp.where(even, jnp.where(x_high, one, zero), odd_first)
    band_decay = jnp.where(even, decays_of(band_own), decays_of(band_far))
    rows = keep.shape[0] // frames
    for frame in range(frames):
        at, row = slice(frame * rows, (frame + 1) * rows), slice(frame, frame + 1)
        before = of_second[row] * second[at, :].astype(F32) + of_first[row] * first[at, :].astype(F32)
        lower = jnp.where(even, band_own[at, :], band_far[at, :]).astype(F32)
        after = band_decay[row] * before + lower
        keep[at, :] = jnp.where(even, before, after).astype(BF16)
        give[at, :] = jnp.where(even, after, before).astype(BF16)


def incoming_kernel(
    frames, rows, columns, head_dim, band, out_local, bc, reach, own, other, weight, out, held, sem
):
    fetch = pltpu.make_async_copy(weight, held, sem)
    fetch.start()
    state = bc.shape[1] // 2
    half = state // 2
    inner = out.shape[1]
    mine = band[0] % 2 == 0
    matrix = spread_matrix(0, inner, head_dim)
    for frame in range(frames):
        at = slice(frame * half, (frame + 1) * half)
        low = jnp.where(mine, own[at, :], other[at, :])
        high = jnp.where(mine, other[at, :], own[at, :])
        carried = jnp.concatenate([low, high], axis=0)
        for row in range(rows):
            to = (row * frames + frame) * columns
            here = slice(to, to + columns)
            factor = spread(reach[here, :], matrix)
            out[here, :] = out_local[here, :] + factor * dot(bc[here, state:], carried)
    fetch.wait()


def temporal_kernel(
    part, parts, per_group, head_dim, rows, frames, columns, chunk_cols, shares, state, *refs
):
    here_ref, params, payload = refs[:3]
    rest = list(refs[3:])
    carried_in = rest.pop(0) if part > 0 else None
    outs, rest = rest[:shares], rest[shares:]
    carried_out = rest.pop(0) if part + 1 < parts else None
    b_all, c_all, dt_all, decay_all = rest
    here = here_ref[0]
    length = frames * columns
    part_cols = columns // parts
    group = outs[0].shape[1]
    eye = (iota((TAIL, LANES), 0) == iota((TAIL, LANES), 1)) & (iota((TAIL, LANES), 1) < per_group)
    eye = eye.astype(BF16)

    def came(distance):
        return payload.at[here ^ distance]

    for distance in range(shares):
        b_proj, c_proj, logits = unpacked_rest(came(distance), length)
        logits = dot_tn(logits, eye)
        for frame in range(frames):
            at = slice(frame * columns + part * part_cols, frame * columns + (part + 1) * part_cols)
            to = slice(frame * part_cols, (frame + 1) * part_cols)
            b_all[distance, to] = b_proj[at]
            c_all[distance, to] = c_proj[at]
            dt = softplus(logits[at] + params[8:9, :])
            dt_all[distance, to] = dt
            decay_all[distance, to] = -dt * params[9:10, :]

    all_frames = shares * frames
    size = all_frames * chunk_cols

    def order_key(dim):
        index = iota((size, size), dim)
        source = here ^ (index // (frames * chunk_cols))
        frame = source * frames + (index // chunk_cols) % frames
        return (index % chunk_cols) * all_frames + frame

    causal = order_key(0) >= order_key(1)
    order = causal.astype(F32)
    matrix = spread_matrix(0, group, head_dim)
    carried = jnp.zeros((state, group), F32) if part == 0 else carried_in[...]
    places = [(source, frame) for source in range(shares) for frame in range(frames)]
    for chunk in range(part_cols // chunk_cols):

        def gathered(ref_of, pitch=part_cols, offset=0):
            return jnp.concatenate(
                [
                    ref_of(source)[pl.ds(frame * pitch + offset + chunk * chunk_cols, chunk_cols), :]
                    for source, frame in places
                ],
                axis=0,
            )

        values = gathered(came, columns, part * part_cols)
        b_proj = gathered(lambda source: b_all.at[source])
        c_proj = gathered(lambda source: c_all.at[source])
        dt = gathered(lambda source: dt_all.at[source])
        running = dot(order, gathered(lambda source: decay_all.at[source]), precision=EXACT)
        running_t, dt_t = jnp.transpose(running), jnp.transpose(dt)
        scores = jnp.where(causal, dot_nt(c_proj, b_proj), 0.0)
        last = jnp.min(running, axis=0, keepdims=True)
        mixed = head_mixes(scores, running, running_t, dt_t, values, 0, per_group, head_dim)
        ends = jnp.concatenate([running, jnp.broadcast_to(last, (8, LANES))], axis=0)
        reach = dot(jnp.exp(ends).astype(BF16), matrix)
        mixed = mixed + reach[:size] * dot(c_proj, carried.astype(BF16))
        to_end = (jnp.exp(last - running) * dt).astype(BF16)
        scaled = (values.astype(F32) * dot(to_end, matrix)).astype(BF16)
        carried = reach[size : size + 1, :] * carried + dot_tn(b_proj, scaled)
        mixed = mixed.astype(BF16)
        for index, (source, frame) in enumerate(places):
            to = frame * part_cols + chunk * chunk_cols
            outs[source][to : to + chunk_cols, :] = mixed[index * chunk_cols : (index + 1) * chunk_cols]
    if carried_out is not None:
        carried_out[...] = carried


def exit_kernel(part, parts, shares, *refs):
    here, spatial, gate, gain, weight = refs[:5]
    out, temporal, normed, mixed, sems = refs[-5:]
    frames, rows, columns, _ = out.shape
    part_cols = columns // parts
    _, part_len, group = temporal.shape
    groups = shares // rows
    inner = groups * group
    for distance in range(shares):
        temporal[here[0] ^ distance] = refs[5 + distance][...]

    def own(ref, row, at):
        return jnp.concatenate(
            [
                ref[pl.ds((row * frames + frame) * columns + part * part_cols, part_cols), at]
                for frame in range(frames)
            ],
            axis=0,
        )

    gains = gain[...].reshape(1, inner)
    for row in range(rows):
        total = jnp.zeros((part_len, 1), F32)
        kept = []
        for index in range(groups):
            at = slice(index * group, (index + 1) * group)
            gates = own(gate, row, at).astype(F32)
            gated = own(spatial, row, at) + temporal[index * rows + row].astype(F32)
            gated = gated * (gates / (1.0 + jnp.exp(-gates)))
            total = total + jnp.sum(gated * gated, axis=1, keepdims=True)
            kept.append(gated)
        scale = lax.rsqrt(total / inner + EPSILON)
        for index, gated in enumerate(kept):
            at = slice(index * group, (index + 1) * group)
            normed[row * part_len : (row + 1) * part_len, at] = (gated * scale * gains[:, at]).astype(BF16)
    mixed[...] = dot(normed[...], weight[...]).astype(BF16)
    copies = [
        pltpu.make_async_copy(
            mixed.at[pl.ds((row * frames + frame) * part_cols, part_cols), :],
            out.at[frame, row, pl.ds(part * part_cols, part_cols), :],
            sems.at[row * frames + frame],
        )
        for row in range(rows)
        for frame in range(frames)
    ]
    for copy in copies:
        copy.start()
    for copy in copies:
        copy.wait()


def swapped(value, axis, distance):
    count = lax.axis_size(axis)
    return lax.ppermute(value, axis, [(source, source ^ distance) for source in range(count)])


def crossed(value, axis, even, odd):
    count = lax.axis_size(axis)
    pairs = [(source, source ^ (odd if source % 2 else even)) for source in range(count)]
    return lax.ppermute(value, axis, pairs)


def per_device(
    tokens, norm_gain, in_weight, bc_weight, dt_weight, dt_bias, decay_rate, out_gain, out_weight
):
    frames, rows, columns, width = tokens.shape
    heads = decay_rate.shape[1]
    inner = out_weight.shape[0]
    head_dim = inner // heads
    state = bc_weight.shape[1] // 4
    shares = lax.axis_size("tm")
    bands = lax.axis_size("height")
    groups = shares // rows
    group = inner // groups
    per_group = heads // groups
    length = frames * columns
    count = rows * length
    half = state // 2
    chunk_cols = 16
    blocks = parts = 2
    part_len = length // parts
    here = lax.axis_index("tm").astype(jnp.int32).reshape(1)
    band = lax.axis_index("height").astype(jnp.int32).reshape(1)

    packed = (shares, sum(packing(length, group)), group)
    normed, payload, bc_own, logits, params, own, other, band_decays = call(
        functools.partial(entry_kernel, shares, heads, state, blocks),
        "entry",
        [
            shape_of((count, width), BF16),
            shape_of(packed, BF16),
            shape_of((count, 2 * state), BF16),
            shape_of((count, LANES), F32),
            shape_of((16, LANES), F32),
        ]
        + [shape_of((frames * half + TAIL, inner), BF16)] * 2
        + [shape_of((TAIL, inner), BF16)],
        [SCALAR, SCALAR, HBM, WHOLE, WHOLE, WHOLE, HBM, HBM, HBM],
        limit=LARGE,
        outs=[HBM, HBM] + [WHOLE] * 6,
        scratch_shapes=[
            pltpu.VMEM((rows, frames, columns, width), BF16),
            pltpu.VMEM((2 * heads, width), BF16),
            pltpu.VMEM((width, 4 * state), BF16),
            pltpu.VMEM((width, inner), BF16),
            pltpu.VMEM((8, LANES), F32),
            pltpu.VMEM((count, width), BF16),
            pltpu.VMEM(packed, BF16),
            pltpu.SemaphoreType.DMA((rows * frames + 2 + blocks,)),
            pltpu.SemaphoreType.DMA((1 + shares,)),
        ],
    )(here, band, tokens, norm_gain, dt_bias, decay_rate, dt_weight.T, bc_weight, in_weight)

    def sent(parts):
        return [parts[0]] + [swapped(parts[d], "tm", d) for d in range(1, shares)]

    received = lax.all_to_all(payload, "tm", split_axis=0, concat_axis=0, tiled=True)
    far = swapped(other, "height", 1)
    gate = call(
        functools.partial(gate_kernel, blocks),
        "gate",
        shape_of((count, inner), BF16),
        [ANY, WHOLE, HBM],
        scratch_shapes=[
            pltpu.VMEM((width, inner), BF16),
            pltpu.SemaphoreType.DMA((blocks,)),
        ],
    )(payload, normed, in_weight)

    out_local, reach = call(
        functools.partial(local_kernel, frames, rows, columns, head_dim, groups),
        "spatial_local",
        [shape_of((count, inner), F32), shape_of((count, LANES), F32)],
        [ANY] + [WHOLE] * 4,
    )(gate, bc_own, logits, params, payload)

    total = call(
        functools.partial(pair_kernel, frames),
        "pair_total",
        shape_of((frames * half + TAIL, inner), BF16),
        [SCALAR, WHOLE, WHOLE],
    )(band, own, far)
    returned, carried = [], []
    for part in range(parts):
        more = [shape_of((state, group), F32)] if part + 1 < parts else []
        results = call(
            functools.partial(
                temporal_kernel,
                part,
                parts,
                per_group,
                head_dim,
                rows,
                frames,
                columns,
                chunk_cols,
                shares,
                state,
            ),
            "temporal",
            [shape_of((part_len, group), BF16)] * shares + more,
            [SCALAR] + [WHOLE] * (2 + len(carried)),
            scratch_shapes=[
                pltpu.VMEM((shares, part_len, state), BF16),
                pltpu.VMEM((shares, part_len, state), BF16),
                pltpu.VMEM((shares, part_len, LANES), F32),
                pltpu.VMEM((shares, part_len, LANES), F32),
            ],
        )(here, params, received, *carried)
        returned.append(sent(results[:shares]))
        carried = results[shares:]

    before = []
    distance = 2
    if bands == 8:
        near, far_decays = (swapped(band_decays, "height", distance) for distance in (6, 7))
        first = crossed(total, "height", 2, 4)
        message = call(
            functools.partial(cross_kernel, frames),
            "cross",
            shape_of((frames * half + TAIL, inner), BF16),
            [ANY, SCALAR] + [WHOLE] * 4,
        )(reach, band, total, first, near, far_decays)
        second = crossed(message, "height", 4, 2)
        results = call(
            functools.partial(settle_kernel, frames),
            "settle",
            [shape_of((frames * half, inner), BF16)] * 2,
            [ANY, SCALAR] + [WHOLE] * 6,
        )(reach, band, first, second, near, far_decays, own, far)
        distance = bands
    while distance < bands:
        far_total = swapped(total, "height", distance)
        finish = distance * 2 >= bands
        operands = [reach, band, total, far_total] + before + ([own, far] if finish else [])
        outs = (
            [shape_of((frames * half, inner), BF16)] * 2
            if finish
            else [
                shape_of((frames * half + TAIL, inner), BF16),
                shape_of((frames * half + 8, inner), F32),
            ]
        )
        results = call(
            functools.partial(merge_kernel, frames, distance, finish),
            "merge",
            outs,
            [ANY, SCALAR] + [WHOLE] * (len(operands) - 2),
        )(*operands)
        if not finish:
            total, before = results[0], [results[1]]
        distance *= 2
    keep, give = results
    came = swapped(give, "height", 1)

    spatial_out, held_weight = call(
        functools.partial(incoming_kernel, frames, rows, columns, head_dim),
        "spatial_incoming",
        [shape_of((count, inner), F32), shape_of((inner, width), BF16)],
        [SCALAR] + [WHOLE] * 5 + [HBM],
        scratch_shapes=[pltpu.SemaphoreType.DMA],
    )(band, out_local, bc_own, reach, keep, came, out_weight)

    mixed = []
    for part in range(parts):
        mixed = [
            call(
                functools.partial(exit_kernel, part, parts, shares),
                "exit",
                shape_of(tokens.shape, BF16),
                [SCALAR] + [WHOLE] * (4 + shares) + [HBM] * len(mixed),
                outs=HBM,
                scratch_shapes=[
                    pltpu.VMEM((shares, part_len, group), BF16),
                    pltpu.VMEM((rows * part_len, inner), BF16),
                    pltpu.VMEM((rows * part_len, width), BF16),
                    pltpu.SemaphoreType.DMA((rows * frames,)),
                ],
                input_output_aliases={5 + shares: 0} if mixed else {},
            )(here, spatial_out, gate, out_gain, held_weight, *returned[part], *mixed)
        ]
    return mixed[0]


def solution(mesh):
    in_specs = (P("tm", "height", None, None), P(), P(), P(), P(), P(), P(), P(), P())
    out_specs = P("tm", "height", None, None)
    return jax.shard_map(
        per_device, mesh=mesh, in_specs=in_specs, out_specs=out_specs, check_vma=False
    )
```

```python
import functools
import math

import jax
import jax.numpy as jnp
from jax import lax
from jax.experimental import pallas as pl
from jax.experimental.pallas import tpu as pltpu
from jax.sharding import PartitionSpec as P

EPSILON = 1e-05
LANES = 128
TAIL = 16
LOG2_E = 1.4426950408889634
F32 = jnp.float32
BF16 = jnp.bfloat16
EXACT = lax.Precision.HIGHEST
LARGE = 56 * 1024 * 1024
SMALL = 24 * 1024 * 1024

ANY = pl.BlockSpec(memory_space=pl.ANY)
HBM = pl.BlockSpec(memory_space=pltpu.HBM)
SCALAR = pl.BlockSpec(memory_space=pltpu.SMEM)
WHOLE = pl.BlockSpec(memory_space=pltpu.VMEM)


def call(kernel, name, out_shape, in_specs, limit=SMALL, outs=None, **options):
    return pl.pallas_call(
        kernel,
        out_shape=out_shape,
        in_specs=in_specs,
        out_specs=jax.tree.map(lambda _: WHOLE, out_shape) if outs is None else outs,
        compiler_params=pltpu.CompilerParams(vmem_limit_bytes=limit),
        cost_estimate=pl.CostEstimate(flops=1, bytes_accessed=1, transcendentals=0),
        name=name,
        **options,
    )


def shape_of(shape, dtype):
    return jax.ShapeDtypeStruct(shape, dtype)


def dot(left, right, **options):
    return jnp.dot(left, right, preferred_element_type=F32, **options)


def dot_tn(left, right):
    return lax.dot_general(left, right, (((0,), (0,)), ((), ())), preferred_element_type=F32)


def dot_nt(left, right):
    return lax.dot_general(left, right, (((1,), (1,)), ((), ())), preferred_element_type=F32)


def softplus(values):
    return jnp.maximum(values, 0.0) + jnp.log1p(jnp.exp(-jnp.abs(values)))


def iota(shape, dim):
    return lax.broadcasted_iota(jnp.int32, shape, dim)


def spread_matrix(first_head, width, head_dim):
    return (iota((LANES, width), 0) - first_head == iota((LANES, width), 1) // head_dim).astype(BF16)


def spread(values, matrix):
    high = values.astype(BF16)
    low = (values - high.astype(F32)).astype(BF16)
    return dot(high, matrix) + dot(low, matrix)


def head_mixes(scores, running, running_t, dt_t, x, first_head, heads, head_dim):
    length = scores.shape[0]
    running, running_t = running * LOG2_E, running_t * LOG2_E
    outs = []

    def weights(head):
        spreads = running[:, head : head + 1] - running_t[head : head + 1, :]
        return (scores * jnp.exp2(jnp.minimum(spreads, 0.0)) * dt_t[head : head + 1, :]).astype(BF16)

    head = 0
    while head < heads:
        here = first_head + head
        if head + 1 < heads and 2 * head_dim == LANES:
            both = x[:, head * head_dim : (head + 2) * head_dim]
            first = iota((length, LANES), 1) < head_dim
            zero = jnp.zeros_like(both)
            stacked = jnp.concatenate([jnp.where(first, both, zero), jnp.where(first, zero, both)], axis=0)
            pair = jnp.concatenate([weights(here), weights(here + 1)], axis=1)
            outs.append(dot(pair, stacked))
            head += 2
        else:
            outs.append(dot(weights(here), x[:, head * head_dim : (head + 1) * head_dim]))
            head += 1
    return outs[0] if len(outs) == 1 else jnp.concatenate(outs, axis=1)


def column_copies(weight, scratch, sems, first, offset, blocks):
    width = scratch.shape[1] // blocks
    return [
        pltpu.make_async_copy(
            weight.at[:, pl.ds(offset + index * width, width)],
            scratch.at[:, pl.ds(index * width, width)],
            sems.at[first + index],
        )
        for index in range(blocks)
    ]


def rank_of(device):
    return device ^ (device >> 1)


def packing(length, group):
    columns = group // LANES
    rest = -(-(2 * length + TAIL) // columns)
    return length, -(-rest // TAIL) * TAIL


def pack_rest(ref, length, b_proj, c_proj, dt):
    columns, rest = ref.shape[1] // LANES, ref.shape[0] - length
    blank = jnp.zeros((columns * rest - 2 * length - TAIL, LANES), BF16)
    stacked = jnp.concatenate([b_proj, c_proj, dt, blank], axis=0)
    for column in range(columns):
        ref[length:, column * LANES : (column + 1) * LANES] = stacked[column * rest : (column + 1) * rest]


def unpacked_rest(ref, length):
    columns = ref.shape[1] // LANES
    stacked = jnp.concatenate(
        [ref[length:, column * LANES : (column + 1) * LANES] for column in range(columns)], axis=0
    )
    return stacked[:length], stacked[length : 2 * length], stacked[2 * length : 2 * length + TAIL]


def entry_kernel(shares, heads, state, blocks, *refs):
    here_ref, band, tokens, gain, bias, rates, dt_weight, bc_weight, weight = refs[:9]
    normed_out, payload_out, bc_own, logits, params, own_states, other_states, band_decays = refs[9:17]
    held, dt_held, bc_held, held_weight, table, normed, payload, sems, out_sems = refs[17:]
    frames, rows, columns, width = tokens.shape
    length = frames * columns
    count = rows * length
    groups = shares // rows
    per_group = heads // groups
    group = held_weight.shape[1] // groups

    token_copies = [
        pltpu.make_async_copy(tokens.at[frame, row], held.at[row, frame], sems.at[row * frames + frame])
        for row in range(rows)
        for frame in range(frames)
    ]
    for copy in token_copies:
        copy.start()
    first = rows * frames
    dt_copy = pltpu.make_async_copy(dt_weight, dt_held, sems.at[first])
    dt_copy.start()
    bc_copy = pltpu.make_async_copy(bc_weight, bc_held, sems.at[first + 1])
    bc_copy.start()
    copies = column_copies(weight, held_weight, sems, first + 2, 0, blocks)
    for copy in copies:
        copy.start()

    table[...] = jnp.zeros_like(table)
    table[0:1, : 2 * heads] = bias[...].reshape(1, 2 * heads)
    table[1:2, :heads] = rates[0:1, :]
    table[1:2, heads : 2 * heads] = rates[1:2, :]
    first_head = heads + here_ref[0] // rows * per_group
    lane_in, lane_out = iota((LANES, LANES), 0), iota((LANES, LANES), 1)
    own = ((lane_in == lane_out + first_head) & (lane_out < per_group)).astype(F32)
    params[0:8, :] = table[...]
    params[8:16, :] = dot(table[...], own, precision=EXACT)
    logits[...] = jnp.zeros_like(logits)

    gains = gain[...].reshape(1, width)
    for index, copy in enumerate(token_copies):
        copy.wait()
        values = held[index // frames, index % frames].astype(F32)
        mean_square = jnp.mean(values * values, axis=-1, keepdims=True)
        normed[index * columns : (index + 1) * columns, :] = (
            values * lax.rsqrt(mean_square + EPSILON) * gains
        ).astype(BF16)
    outgoing = [pltpu.make_async_copy(normed, normed_out, out_sems.at[0])]
    outgoing[0].start()
    dt_copy.wait()
    logits[:, : 2 * heads] = dot_nt(normed[...], dt_held[...]).astype(BF16).astype(F32)
    dt_heads = dot_nt(dt_held[heads:, :], normed[...])
    dt_heads = jnp.concatenate([dt_heads, jnp.zeros((TAIL, count), F32)], axis=0).astype(BF16)
    bc_copy.wait()
    bc = dot(normed[...], bc_held[...]).astype(BF16)
    bc_own[...] = bc[:, : 2 * state]
    scan = [
        end_factors(frame_of(logits, frame, rows, frames, columns), params, rows * columns)
        for frame in range(frames)
    ]

    block = held_weight.shape[1] // blocks
    for index, copy in enumerate(copies):
        copy.wait()
        at = index * block
        values = dot(normed[...], held_weight[:, at : at + block]).astype(BF16)
        for inside in range(0, block, group):
            part = (at + inside) // group
            for row in range(rows):
                piece = rank_of(part * rows + row)
                here = slice(row * length, (row + 1) * length)
                payload[piece, :length, :] = values[here, inside : inside + group]
                pack_rest(
                    payload.at[piece],
                    length,
                    bc[here, 2 * state : 3 * state],
                    bc[here, 3 * state :],
                    dt_heads[part * per_group : part * per_group + TAIL, here],
                )
                outgoing.append(
                    pltpu.make_async_copy(
                        payload.at[piece], payload_out.at[piece], out_sems.at[1 + piece]
                    )
                )
                outgoing[-1].start()
    half = state // 2
    head_dim = groups * group // heads
    mine = band[0] % 2 == 0
    for frame in range(frames):
        b_proj = frame_of(bc_own, frame, rows, frames, columns)[:, :state]
        for part in range(groups):
            at = slice(part * group, (part + 1) * group)
            values = frame_x(payload, part, frame, rows, columns)
            matrix = spread_matrix(part * per_group, group, head_dim)
            scaled = (values.astype(F32) * dot(scan[frame][0], matrix)).astype(BF16)
            fresh = dot_tn(b_proj, scaled).astype(BF16)
            at_rows = slice(frame * half, (frame + 1) * half)
            own_states[at_rows, at] = jnp.where(mine, fresh[:half], fresh[half:])
            other_states[at_rows, at] = jnp.where(mine, fresh[half:], fresh[:half])
    whole = [decay for _, decay in scan] + [jnp.zeros((8 - frames, LANES), F32)]
    decays = spread(jnp.concatenate(whole, axis=0), spread_matrix(0, groups * group, head_dim))
    tail = tail_of(decays)
    own_states[frames * half :, :] = tail
    other_states[frames * half :, :] = tail
    band_decays[...] = tail
    for copy in outgoing:
        copy.wait()


def gate_kernel(blocks, after, normed, weight, out, held_weight, sems):
    inner = held_weight.shape[1]
    copies = column_copies(weight, held_weight, sems, 0, inner, blocks)
    for copy in copies:
        copy.start()
    block = inner // blocks
    for index, copy in enumerate(copies):
        copy.wait()
        at = slice(index * block, (index + 1) * block)
        out[:, at] = dot(normed[...], held_weight[:, at]).astype(BF16)


def frame_of(ref, frame, rows, frames, columns):
    return jnp.concatenate(
        [
            ref[(row * frames + frame) * columns : (row * frames + frame + 1) * columns, :]
            for row in range(rows)
        ],
        axis=0,
    )


def frame_x(payload, part, frame, rows, columns):
    return jnp.concatenate(
        [
            payload[rank_of(part * rows + row), frame * columns : (frame + 1) * columns, :]
            for row in range(rows)
        ],
        axis=0,
    )


def scan_terms(logits, params, causal):
    dt = softplus(logits + params[0:1, :])
    running = dot(causal.astype(F32), -dt * params[1:2, :], precision=EXACT)
    return dt, running, jnp.min(running, axis=0, keepdims=True)


def end_factors(logits, params, length):
    causal = iota((length, length), 0) >= iota((length, length), 1)
    dt, running, last = scan_terms(logits, params, causal)
    return (jnp.exp(last - running) * dt).astype(BF16), jnp.exp(last)


def local_kernel(frames, rows, columns, head_dim, groups, *refs):
    after, bc, logits, params, x, out, reach = refs
    length = rows * columns
    group = x.shape[2]
    state = bc.shape[1] // 2
    per_group = group // head_dim
    causal = iota((length, length), 0) >= iota((length, length), 1)

    def stored(ref, values, frame, at):
        for row in range(rows):
            to = (row * frames + frame) * columns
            ref[to : to + columns, at] = values[row * columns : (row + 1) * columns]

    for frame in range(frames):
        dt, running, _ = scan_terms(frame_of(logits, frame, rows, frames, columns), params, causal)
        running_t, dt_t = jnp.transpose(running), jnp.transpose(dt)
        bc_rows = frame_of(bc, frame, rows, frames, columns)
        scores = jnp.where(causal, dot_nt(bc_rows[:, state:], bc_rows[:, :state]), 0.0)
        stored(reach, jnp.exp(running), frame, slice(None))
        for piece in range(groups):
            values = frame_x(x, piece, frame, rows, columns)
            mixed = head_mixes(
                scores, running, running_t, dt_t, values, piece * per_group, per_group, head_dim
            )
            stored(out, mixed, frame, slice(piece * group, (piece + 1) * group))


def tail_of(decays):
    high = decays.astype(BF16)
    return jnp.concatenate([high, (decays - high.astype(F32)).astype(BF16)], axis=0)


def pair_kernel(frames, band, own, far, total):
    rows = (own.shape[0] - TAIL) // frames
    own_decay = own[-TAIL:-8, :].astype(F32) + own[-8:, :].astype(F32)
    far_decay = far[-TAIL:-8, :].astype(F32) + far[-8:, :].astype(F32)
    lower = band[0] % 2 == 0
    through = jnp.where(lower, far_decay, own_decay)
    for frame in range(frames):
        at = slice(frame * rows, (frame + 1) * rows)
        first = jnp.where(lower, own[at, :], far[at, :]).astype(F32)
        second = jnp.where(lower, far[at, :], own[at, :]).astype(F32)
        total[at, :] = (through[frame : frame + 1, :] * first + second).astype(BF16)
    total[frames * rows :, :] = tail_of(own_decay * far_decay)


def merge_kernel(frames, distance, finish, *refs):
    _, band, own, far = refs[:4]
    start = distance == 2
    rest = list(refs[4:])
    before_in = None if start else rest.pop(0)
    band_own, band_far = (rest.pop(0), rest.pop(0)) if finish else (None, None)
    rows = (own.shape[0] - TAIL) // frames
    upper, lower_band = (band[0] // distance) % 2 == 1, band[0] % 2 == 0
    own_decay = own[-TAIL:-8, :].astype(F32) + own[-8:, :].astype(F32)
    far_decay = far[-TAIL:-8, :].astype(F32) + far[-8:, :].astype(F32)
    if start:
        before_decay = jnp.ones_like(own_decay)
    else:
        before_decay = before_in[-8:, :]
    if finish:
        first_decay = jnp.where(
            lower_band,
            band_own[-TAIL:-8, :].astype(F32) + band_own[-8:, :].astype(F32),
            band_far[-TAIL:-8, :].astype(F32) + band_far[-8:, :].astype(F32),
        )
    through = jnp.where(upper, own_decay, far_decay)
    for frame in range(frames):
        at = slice(frame * rows, (frame + 1) * rows)
        row = slice(frame, frame + 1)
        far_state = far[at, :].astype(F32)
        came = before_decay[row, :] * far_state
        if not start:
            came = came + before_in[at, :]
        before = jnp.where(upper, came, 0.0 if start else before_in[at, :])
        if finish:
            keep, give = rest
            first = jnp.where(lower_band, band_own[at, :], band_far[at, :]).astype(F32)
            after = first_decay[row, :] * before + first
            keep[at, :] = jnp.where(lower_band, before, after).astype(BF16)
            give[at, :] = jnp.where(lower_band, after, before).astype(BF16)
        else:
            total, before_out = rest
            own_state = own[at, :].astype(F32)
            early = jnp.where(upper, far_state, own_state)
            late = jnp.where(upper, own_state, far_state)
            total[at, :] = (through[row, :] * early + late).astype(BF16)
            before_out[at, :] = before
    if not finish:
        total[frames * rows :, :] = tail_of(own_decay * far_decay)
        before_out[frames * rows :, :] = jnp.where(upper, before_decay * far_decay, before_decay)


def decays_of(ref):
    return ref[-TAIL:-8, :].astype(F32) + ref[-8:, :].astype(F32)


def places_of(band):
    return band % 2 == 0, (band // 2) % 2 == 1, band // 4 == 1


def cross_kernel(frames, _, band, total, first, near, far, message):
    even, x_high, y_high = places_of(band[0])
    own_decay, first_decay = decays_of(total), decays_of(first)
    diagonal = decays_of(near) * decays_of(far)
    one, zero = jnp.ones_like(own_decay), jnp.zeros_like(own_decay)
    odd_first = jnp.where(y_high, jnp.where(x_high, one, own_decay * diagonal), zero)
    odd_own = jnp.where(x_high & y_high, zero, one)
    of_first = jnp.where(even, jnp.where(x_high, own_decay, one), odd_first)
    of_own = jnp.where(even, jnp.where(x_high, one, first_decay), odd_own)
    rows = (total.shape[0] - TAIL) // frames
    for frame in range(frames):
        at, row = slice(frame * rows, (frame + 1) * rows), slice(frame, frame + 1)
        sent = of_first[row] * first[at, :].astype(F32) + of_own[row] * total[at, :].astype(F32)
        message[at, :] = sent.astype(BF16)
    message[frames * rows :, :] = tail_of(jnp.where(even, own_decay * first_decay, own_decay))


def settle_kernel(frames, _, band, first, second, near, far, band_own, band_far, keep, give):
    even, x_high, y_high = places_of(band[0])
    first_decay, second_decay = decays_of(first), decays_of(second)
    diagonal = decays_of(near) * decays_of(far)
    one, zero = jnp.ones_like(first_decay), jnp.zeros_like(first_decay)
    even_second = jnp.where(y_high, jnp.where(x_high, first_decay, one), zero)
    odd_second = jnp.where(x_high | y_high, one, zero)
    odd_first = jnp.where(y_high, jnp.where(x_high, second_decay, diagonal), zero)
    of_second = jnp.where(even, even_second, odd_second)
    of_first = jnp.where(even, jnp.where(x_high, one, zero), odd_first)
    band_decay = jnp.where(even, decays_of(band_own), decays_of(band_far))
    rows = keep.shape[0] // frames
    for frame in range(frames):
        at, row = slice(frame * rows, (frame + 1) * rows), slice(frame, frame + 1)
        before = of_second[row] * second[at, :].astype(F32) + of_first[row] * first[at, :].astype(F32)
        lower = jnp.where(even, band_own[at, :], band_far[at, :]).astype(F32)
        after = band_decay[row] * before + lower
        keep[at, :] = jnp.where(even, before, after).astype(BF16)
        give[at, :] = jnp.where(even, after, before).astype(BF16)


def incoming_kernel(
    frames, rows, columns, head_dim, band, out_local, bc, reach, own, other, weight, out, held, sem
):
    fetch = pltpu.make_async_copy(weight, held, sem)
    fetch.start()
    state = bc.shape[1] // 2
    half = state // 2
    inner = out.shape[1]
    mine = band[0] % 2 == 0
    matrix = spread_matrix(0, inner, head_dim)
    for frame in range(frames):
        at = slice(frame * half, (frame + 1) * half)
        low = jnp.where(mine, own[at, :], other[at, :])
        high = jnp.where(mine, other[at, :], own[at, :])
        carried = jnp.concatenate([low, high], axis=0)
        for row in range(rows):
            to = (row * frames + frame) * columns
            here = slice(to, to + columns)
            factor = spread(reach[here, :], matrix)
            out[here, :] = out_local[here, :] + factor * dot(bc[here, state:], carried)
    fetch.wait()


def temporal_kernel(
    part, parts, per_group, head_dim, rows, frames, columns, chunk_cols, shares, state, *refs
):
    here_ref, params, payload = refs[:3]
    rest = list(refs[3:])
    carried_in = rest.pop(0) if part > 0 else None
    outs, rest = rest[:shares], rest[shares:]
    carried_out = rest.pop(0) if part + 1 < parts else None
    b_all, c_all, dt_all, decay_all = rest
    here = here_ref[0]
    length = frames * columns
    part_cols = columns // parts
    group = outs[0].shape[1]
    eye = (iota((TAIL, LANES), 0) == iota((TAIL, LANES), 1)) & (iota((TAIL, LANES), 1) < per_group)
    eye = eye.astype(BF16)

    def came(distance):
        return payload.at[rank_of(here ^ distance)]

    for distance in range(shares):
        b_proj, c_proj, logits = unpacked_rest(came(distance), length)
        logits = dot_tn(logits, eye)
        for frame in range(frames):
            at = slice(frame * columns + part * part_cols, frame * columns + (part + 1) * part_cols)
            to = slice(frame * part_cols, (frame + 1) * part_cols)
            b_all[distance, to] = b_proj[at]
            c_all[distance, to] = c_proj[at]
            dt = softplus(logits[at] + params[8:9, :])
            dt_all[distance, to] = dt
            decay_all[distance, to] = -dt * params[9:10, :]

    all_frames = shares * frames
    size = all_frames * chunk_cols

    def order_key(dim):
        index = iota((size, size), dim)
        source = here ^ (index // (frames * chunk_cols))
        frame = source * frames + (index // chunk_cols) % frames
        return (index % chunk_cols) * all_frames + frame

    causal = order_key(0) >= order_key(1)
    order = causal.astype(F32)
    matrix = spread_matrix(0, group, head_dim)
    carried = jnp.zeros((state, group), F32) if part == 0 else carried_in[...]
    places = [(source, frame) for source in range(shares) for frame in range(frames)]
    for chunk in range(part_cols // chunk_cols):

        def gathered(ref_of, pitch=part_cols, offset=0):
            return jnp.concatenate(
                [
                    ref_of(source)[pl.ds(frame * pitch + offset + chunk * chunk_cols, chunk_cols), :]
                    for source, frame in places
                ],
                axis=0,
            )

        values = gathered(came, columns, part * part_cols)
        b_proj = gathered(lambda source: b_all.at[source])
        c_proj = gathered(lambda source: c_all.at[source])
        dt = gathered(lambda source: dt_all.at[source])
        running = dot(order, gathered(lambda source: decay_all.at[source]), precision=EXACT)
        running_t, dt_t = jnp.transpose(running), jnp.transpose(dt)
        scores = jnp.where(causal, dot_nt(c_proj, b_proj), 0.0)
        last = jnp.min(running, axis=0, keepdims=True)
        mixed = head_mixes(scores, running, running_t, dt_t, values, 0, per_group, head_dim)
        ends = jnp.concatenate([running, jnp.broadcast_to(last, (8, LANES))], axis=0)
        reach = dot(jnp.exp(ends).astype(BF16), matrix)
        mixed = mixed + reach[:size] * dot(c_proj, carried.astype(BF16))
        to_end = (jnp.exp(last - running) * dt).astype(BF16)
        scaled = (values.astype(F32) * dot(to_end, matrix)).astype(BF16)
        carried = reach[size : size + 1, :] * carried + dot_tn(b_proj, scaled)
        mixed = mixed.astype(BF16)
        for index, (source, frame) in enumerate(places):
            to = frame * part_cols + chunk * chunk_cols
            outs[source][to : to + chunk_cols, :] = mixed[index * chunk_cols : (index + 1) * chunk_cols]
    if carried_out is not None:
        carried_out[...] = carried


def exit_kernel(part, parts, shares, *refs):
    here, spatial, gate, gain, weight = refs[:5]
    out, temporal, normed, mixed, sems = refs[-5:]
    frames, rows, columns, _ = out.shape
    part_cols = columns // parts
    _, part_len, group = temporal.shape
    groups = shares // rows
    inner = groups * group
    for distance in range(shares):
        temporal[here[0] ^ distance] = refs[5 + distance][...]

    def own(ref, row, at):
        return jnp.concatenate(
            [
                ref[pl.ds((row * frames + frame) * columns + part * part_cols, part_cols), at]
                for frame in range(frames)
            ],
            axis=0,
        )

    gains = gain[...].reshape(1, inner)
    for row in range(rows):
        total = jnp.zeros((part_len, 1), F32)
        kept = []
        for index in range(groups):
            at = slice(index * group, (index + 1) * group)
            gates = own(gate, row, at).astype(F32)
            gated = own(spatial, row, at) + temporal[index * rows + row].astype(F32)
            gated = gated * (gates / (1.0 + jnp.exp(-gates)))
            total = total + jnp.sum(gated * gated, axis=1, keepdims=True)
            kept.append(gated)
        scale = lax.rsqrt(total / inner + EPSILON)
        for index, gated in enumerate(kept):
            at = slice(index * group, (index + 1) * group)
            normed[row * part_len : (row + 1) * part_len, at] = (gated * scale * gains[:, at]).astype(BF16)
    mixed[...] = dot(normed[...], weight[...]).astype(BF16)
    copies = [
        pltpu.make_async_copy(
            mixed.at[pl.ds((row * frames + frame) * part_cols, part_cols), :],
            out.at[frame, row, pl.ds(part * part_cols, part_cols), :],
            sems.at[row * frames + frame],
        )
        for row in range(rows)
        for frame in range(frames)
    ]
    for copy in copies:
        copy.start()
    for copy in copies:
        copy.wait()


def swapped(value, axis, distance):
    count = lax.axis_size(axis)
    return lax.ppermute(value, axis, [(source, source ^ distance) for source in range(count)])


def crossed(value, axis, even, odd):
    count = lax.axis_size(axis)
    pairs = [(source, source ^ (odd if source % 2 else even)) for source in range(count)]
    return lax.ppermute(value, axis, pairs)


def per_device(
    tokens, norm_gain, in_weight, bc_weight, dt_weight, dt_bias, decay_rate, out_gain, out_weight
):
    frames, rows, columns, width = tokens.shape
    heads = decay_rate.shape[1]
    inner = out_weight.shape[0]
    head_dim = inner // heads
    state = bc_weight.shape[1] // 4
    shares = lax.axis_size("tm")
    bands = lax.axis_size("height")
    groups = shares // rows
    group = inner // groups
    per_group = heads // groups
    length = frames * columns
    count = rows * length
    half = state // 2
    chunk_cols = 16
    blocks = parts = 2
    part_len = length // parts
    here = lax.axis_index("tm").astype(jnp.int32).reshape(1)
    band = lax.axis_index("height").astype(jnp.int32).reshape(1)

    packed = (shares, sum(packing(length, group)), group)
    normed, payload, bc_own, logits, params, own, other, band_decays = call(
        functools.partial(entry_kernel, shares, heads, state, blocks),
        "entry",
        [
            shape_of((count, width), BF16),
            shape_of(packed, BF16),
            shape_of((count, 2 * state), BF16),
            shape_of((count, LANES), F32),
            shape_of((16, LANES), F32),
        ]
        + [shape_of((frames * half + TAIL, inner), BF16)] * 2
        + [shape_of((TAIL, inner), BF16)],
        [SCALAR, SCALAR, HBM, WHOLE, WHOLE, WHOLE, HBM, HBM, HBM],
        limit=LARGE,
        outs=[HBM, HBM] + [WHOLE] * 6,
        scratch_shapes=[
            pltpu.VMEM((rows, frames, columns, width), BF16),
            pltpu.VMEM((2 * heads, width), BF16),
            pltpu.VMEM((width, 4 * state), BF16),
            pltpu.VMEM((width, inner), BF16),
            pltpu.VMEM((8, LANES), F32),
            pltpu.VMEM((count, width), BF16),
            pltpu.VMEM(packed, BF16),
            pltpu.SemaphoreType.DMA((rows * frames + 2 + blocks,)),
            pltpu.SemaphoreType.DMA((1 + shares,)),
        ],
    )(here, band, tokens, norm_gain, dt_bias, decay_rate, dt_weight.T, bc_weight, in_weight)

    def sent(parts):
        return [parts[0]] + [swapped(parts[d], "tm", d) for d in range(1, shares)]

    line = [rank_of(device) for device in range(shares)]
    received = lax.all_to_all(
        payload,
        "tm",
        split_axis=0,
        concat_axis=0,
        tiled=True,
        axis_index_groups=[[line.index(rank) for rank in range(shares)]],
    )
    far = swapped(other, "height", 1)
    gate = call(
        functools.partial(gate_kernel, blocks),
        "gate",
        shape_of((count, inner), BF16),
        [ANY, WHOLE, HBM],
        scratch_shapes=[
            pltpu.VMEM((width, inner), BF16),
            pltpu.SemaphoreType.DMA((blocks,)),
        ],
    )(payload, normed, in_weight)

    out_local, reach = call(
        functools.partial(local_kernel, frames, rows, columns, head_dim, groups),
        "spatial_local",
        [shape_of((count, inner), F32), shape_of((count, LANES), F32)],
        [ANY] + [WHOLE] * 4,
    )(gate, bc_own, logits, params, payload)

    total = call(
        functools.partial(pair_kernel, frames),
        "pair_total",
        shape_of((frames * half + TAIL, inner), BF16),
        [SCALAR, WHOLE, WHOLE],
    )(band, own, far)
    returned, carried = [], []
    for part in range(parts):
        more = [shape_of((state, group), F32)] if part + 1 < parts else []
        results = call(
            functools.partial(
                temporal_kernel,
                part,
                parts,
                per_group,
                head_dim,
                rows,
                frames,
                columns,
                chunk_cols,
                shares,
                state,
            ),
            "temporal",
            [shape_of((part_len, group), BF16)] * shares + more,
            [SCALAR] + [WHOLE] * (2 + len(carried)),
            scratch_shapes=[
                pltpu.VMEM((shares, part_len, state), BF16),
                pltpu.VMEM((shares, part_len, state), BF16),
                pltpu.VMEM((shares, part_len, LANES), F32),
                pltpu.VMEM((shares, part_len, LANES), F32),
            ],
        )(here, params, received, *carried)
        returned.append(sent(results[:shares]))
        carried = results[shares:]

    before = []
    distance = 2
    if bands == 8:
        near, far_decays = (swapped(band_decays, "height", distance) for distance in (6, 7))
        first = crossed(total, "height", 2, 4)
        message = call(
            functools.partial(cross_kernel, frames),
            "cross",
            shape_of((frames * half + TAIL, inner), BF16),
            [ANY, SCALAR] + [WHOLE] * 4,
        )(reach, band, total, first, near, far_decays)
        second = crossed(message, "height", 4, 2)
        results = call(
            functools.partial(settle_kernel, frames),
            "settle",
            [shape_of((frames * half, inner), BF16)] * 2,
            [ANY, SCALAR] + [WHOLE] * 6,
        )(reach, band, first, second, near, far_decays, own, far)
        distance = bands
    while distance < bands:
        far_total = swapped(total, "height", distance)
        finish = distance * 2 >= bands
        operands = [reach, band, total, far_total] + before + ([own, far] if finish else [])
        outs = (
            [shape_of((frames * half, inner), BF16)] * 2
            if finish
            else [
                shape_of((frames * half + TAIL, inner), BF16),
                shape_of((frames * half + 8, inner), F32),
            ]
        )
        results = call(
            functools.partial(merge_kernel, frames, distance, finish),
            "merge",
            outs,
            [ANY, SCALAR] + [WHOLE] * (len(operands) - 2),
        )(*operands)
        if not finish:
            total, before = results[0], [results[1]]
        distance *= 2
    keep, give = results
    came = swapped(give, "height", 1)

    spatial_out, held_weight = call(
        functools.partial(incoming_kernel, frames, rows, columns, head_dim),
        "spatial_incoming",
        [shape_of((count, inner), F32), shape_of((inner, width), BF16)],
        [SCALAR] + [WHOLE] * 5 + [HBM],
        scratch_shapes=[pltpu.SemaphoreType.DMA],
    )(band, out_local, bc_own, reach, keep, came, out_weight)

    mixed = []
    for part in range(parts):
        mixed = [
            call(
                functools.partial(exit_kernel, part, parts, shares),
                "exit",
                shape_of(tokens.shape, BF16),
                [SCALAR] + [WHOLE] * (4 + shares) + [HBM] * len(mixed),
                outs=HBM,
                scratch_shapes=[
                    pltpu.VMEM((shares, part_len, group), BF16),
                    pltpu.VMEM((rows * part_len, inner), BF16),
                    pltpu.VMEM((rows * part_len, width), BF16),
                    pltpu.SemaphoreType.DMA((rows * frames,)),
                ],
                input_output_aliases={5 + shares: 0} if mixed else {},
            )(here, spatial_out, gate, out_gain, held_weight, *returned[part], *mixed)
        ]
    return mixed[0]


def solution(mesh):
    in_specs = (P("tm", "height", None, None), P(), P(), P(), P(), P(), P(), P(), P())
    out_specs = P("tm", "height", None, None)
    return jax.shard_map(
        per_device, mesh=mesh, in_specs=in_specs, out_specs=out_specs, check_vma=False
    )
```

```python
import functools
import math

import jax
import jax.numpy as jnp
from jax import lax
from jax.experimental import pallas as pl
from jax.experimental.pallas import tpu as pltpu
from jax.sharding import PartitionSpec as P

EPSILON = 1e-05
LANES = 128
TAIL = 16
LOG2_E = 1.4426950408889634
F32 = jnp.float32
BF16 = jnp.bfloat16
EXACT = lax.Precision.HIGHEST
LARGE = 56 * 1024 * 1024
SMALL = 24 * 1024 * 1024

ANY = pl.BlockSpec(memory_space=pl.ANY)
HBM = pl.BlockSpec(memory_space=pltpu.HBM)
SCALAR = pl.BlockSpec(memory_space=pltpu.SMEM)
WHOLE = pl.BlockSpec(memory_space=pltpu.VMEM)


def call(kernel, name, out_shape, in_specs, limit=SMALL, outs=None, **options):
    return pl.pallas_call(
        kernel,
        out_shape=out_shape,
        in_specs=in_specs,
        out_specs=jax.tree.map(lambda _: WHOLE, out_shape) if outs is None else outs,
        compiler_params=pltpu.CompilerParams(vmem_limit_bytes=limit),
        cost_estimate=pl.CostEstimate(flops=1, bytes_accessed=1, transcendentals=0),
        name=name,
        **options,
    )


def shape_of(shape, dtype):
    return jax.ShapeDtypeStruct(shape, dtype)


def dot(left, right, **options):
    return jnp.dot(left, right, preferred_element_type=F32, **options)


def dot_tn(left, right):
    return lax.dot_general(left, right, (((0,), (0,)), ((), ())), preferred_element_type=F32)


def dot_nt(left, right):
    return lax.dot_general(left, right, (((1,), (1,)), ((), ())), preferred_element_type=F32)


def softplus(values):
    return jnp.maximum(values, 0.0) + jnp.log1p(jnp.exp(-jnp.abs(values)))


def iota(shape, dim):
    return lax.broadcasted_iota(jnp.int32, shape, dim)


def spread_matrix(first_head, width, head_dim):
    return (iota((LANES, width), 0) - first_head == iota((LANES, width), 1) // head_dim).astype(BF16)


def spread(values, matrix):
    high = values.astype(BF16)
    low = (values - high.astype(F32)).astype(BF16)
    return dot(high, matrix) + dot(low, matrix)


def head_mixes(scores, running, running_t, dt_t, x, first_head, heads, head_dim):
    length = scores.shape[0]
    running, running_t = running * LOG2_E, running_t * LOG2_E
    outs = []

    def weights(head):
        spreads = running[:, head : head + 1] - running_t[head : head + 1, :]
        return (scores * jnp.exp2(jnp.minimum(spreads, 0.0)) * dt_t[head : head + 1, :]).astype(BF16)

    head = 0
    while head < heads:
        here = first_head + head
        if head + 1 < heads and 2 * head_dim == LANES:
            both = x[:, head * head_dim : (head + 2) * head_dim]
            first = iota((length, LANES), 1) < head_dim
            zero = jnp.zeros_like(both)
            stacked = jnp.concatenate([jnp.where(first, both, zero), jnp.where(first, zero, both)], axis=0)
            pair = jnp.concatenate([weights(here), weights(here + 1)], axis=1)
            outs.append(dot(pair, stacked))
            head += 2
        else:
            outs.append(dot(weights(here), x[:, head * head_dim : (head + 1) * head_dim]))
            head += 1
    return outs[0] if len(outs) == 1 else jnp.concatenate(outs, axis=1)


def column_copies(weight, scratch, sems, first, offset, blocks):
    width = scratch.shape[1] // blocks
    return [
        pltpu.make_async_copy(
            weight.at[:, pl.ds(offset + index * width, width)],
            scratch.at[:, pl.ds(index * width, width)],
            sems.at[first + index],
        )
        for index in range(blocks)
    ]


def rank_of(device):
    return device ^ (device >> 1)


def packing(length, group):
    columns = group // LANES
    rest = -(-(2 * length + TAIL) // columns)
    return length, -(-rest // TAIL) * TAIL


def pack_rest(ref, length, b_proj, c_proj, dt):
    columns, rest = ref.shape[1] // LANES, ref.shape[0] - length
    blank = jnp.zeros((columns * rest - 2 * length - TAIL, LANES), BF16)
    stacked = jnp.concatenate([b_proj, c_proj, dt, blank], axis=0)
    for column in range(columns):
        ref[length:, column * LANES : (column + 1) * LANES] = stacked[column * rest : (column + 1) * rest]


def unpacked_rest(ref, length):
    columns = ref.shape[1] // LANES
    stacked = jnp.concatenate(
        [ref[length:, column * LANES : (column + 1) * LANES] for column in range(columns)], axis=0
    )
    return stacked[:length], stacked[length : 2 * length], stacked[2 * length : 2 * length + TAIL]


def entry_kernel(shares, heads, state, blocks, *refs):
    here_ref, band, tokens, gain, bias, rates, dt_weight, bc_weight, weight = refs[:9]
    normed_out, payload_out, bc_own, logits, params, own_states, other_states, band_decays = refs[9:17]
    held, dt_held, bc_held, held_weight, table, normed, payload, sems, out_sems = refs[17:]
    frames, rows, columns, width = tokens.shape
    length = frames * columns
    count = rows * length
    groups = shares // rows
    per_group = heads // groups
    group = held_weight.shape[1] // groups

    token_copies = [
        pltpu.make_async_copy(tokens.at[frame, row], held.at[row, frame], sems.at[row * frames + frame])
        for row in range(rows)
        for frame in range(frames)
    ]
    for copy in token_copies:
        copy.start()
    first = rows * frames
    dt_copy = pltpu.make_async_copy(dt_weight, dt_held, sems.at[first])
    dt_copy.start()
    bc_copy = pltpu.make_async_copy(bc_weight, bc_held, sems.at[first + 1])
    bc_copy.start()
    copies = column_copies(weight, held_weight, sems, first + 2, 0, blocks)
    for copy in copies:
        copy.start()

    table[...] = jnp.zeros_like(table)
    table[0:1, : 2 * heads] = bias[...].reshape(1, 2 * heads)
    table[1:2, :heads] = rates[0:1, :]
    table[1:2, heads : 2 * heads] = rates[1:2, :]
    first_head = heads + here_ref[0] // rows * per_group
    lane_in, lane_out = iota((LANES, LANES), 0), iota((LANES, LANES), 1)
    own = ((lane_in == lane_out + first_head) & (lane_out < per_group)).astype(F32)
    params[0:8, :] = table[...]
    params[8:16, :] = dot(table[...], own, precision=EXACT)
    logits[...] = jnp.zeros_like(logits)

    gains = gain[...].reshape(1, width)
    for index, copy in enumerate(token_copies):
        copy.wait()
        values = held[index // frames, index % frames].astype(F32)
        mean_square = jnp.mean(values * values, axis=-1, keepdims=True)
        normed[index * columns : (index + 1) * columns, :] = (
            values * lax.rsqrt(mean_square + EPSILON) * gains
        ).astype(BF16)
    outgoing = [pltpu.make_async_copy(normed, normed_out, out_sems.at[0])]
    outgoing[0].start()
    dt_copy.wait()
    logits[:, : 2 * heads] = dot_nt(normed[...], dt_held[...]).astype(BF16).astype(F32)
    dt_heads = dot_nt(dt_held[heads:, :], normed[...])
    dt_heads = jnp.concatenate([dt_heads, jnp.zeros((TAIL, count), F32)], axis=0).astype(BF16)
    bc_copy.wait()
    bc = dot(normed[...], bc_held[...]).astype(BF16)
    bc_own[...] = bc[:, : 2 * state]
    scan = [
        end_factors(frame_of(logits, frame, rows, frames, columns), params, rows * columns)
        for frame in range(frames)
    ]

    block = held_weight.shape[1] // blocks
    for index, copy in enumerate(copies):
        copy.wait()
        at = index * block
        values = dot(normed[...], held_weight[:, at : at + block]).astype(BF16)
        for inside in range(0, block, group):
            part = (at + inside) // group
            for row in range(rows):
                piece = rank_of(part * rows + row)
                here = slice(row * length, (row + 1) * length)
                payload[piece, :length, :] = values[here, inside : inside + group]
                pack_rest(
                    payload.at[piece],
                    length,
                    bc[here, 2 * state : 3 * state],
                    bc[here, 3 * state :],
                    dt_heads[part * per_group : part * per_group + TAIL, here],
                )
                outgoing.append(
                    pltpu.make_async_copy(
                        payload.at[piece], payload_out.at[piece], out_sems.at[1 + piece]
                    )
                )
                outgoing[-1].start()
    half = state // 2
    head_dim = groups * group // heads
    mine = band[0] % 2 == 0
    for frame in range(frames):
        b_proj = frame_of(bc_own, frame, rows, frames, columns)[:, :state]
        for part in range(groups):
            at = slice(part * group, (part + 1) * group)
            values = frame_x(payload, part, frame, rows, columns)
            matrix = spread_matrix(part * per_group, group, head_dim)
            scaled = (values.astype(F32) * dot(scan[frame][0], matrix)).astype(BF16)
            fresh = dot_tn(b_proj, scaled).astype(BF16)
            at_rows = slice(frame * half, (frame + 1) * half)
            own_states[at_rows, at] = jnp.where(mine, fresh[:half], fresh[half:])
            other_states[at_rows, at] = jnp.where(mine, fresh[half:], fresh[:half])
    whole = [decay for _, decay in scan] + [jnp.zeros((8 - frames, LANES), F32)]
    decays = spread(jnp.concatenate(whole, axis=0), spread_matrix(0, groups * group, head_dim))
    tail = tail_of(decays)
    own_states[frames * half :, :] = tail
    other_states[frames * half :, :] = tail
    band_decays[...] = tail
    for copy in outgoing:
        copy.wait()


def gate_kernel(blocks, after, normed, weight, out, held_weight, sems):
    inner = held_weight.shape[1]
    copies = column_copies(weight, held_weight, sems, 0, inner, blocks)
    for copy in copies:
        copy.start()
    block = inner // blocks
    for index, copy in enumerate(copies):
        copy.wait()
        at = slice(index * block, (index + 1) * block)
        out[:, at] = dot(normed[...], held_weight[:, at]).astype(BF16)


def frame_of(ref, frame, rows, frames, columns):
    return jnp.concatenate(
        [
            ref[(row * frames + frame) * columns : (row * frames + frame + 1) * columns, :]
            for row in range(rows)
        ],
        axis=0,
    )


def frame_x(payload, part, frame, rows, columns):
    return jnp.concatenate(
        [
            payload[rank_of(part * rows + row), frame * columns : (frame + 1) * columns, :]
            for row in range(rows)
        ],
        axis=0,
    )


def scan_terms(logits, params, causal):
    dt = softplus(logits + params[0:1, :])
    running = dot(causal.astype(F32), -dt * params[1:2, :], precision=EXACT)
    return dt, running, jnp.min(running, axis=0, keepdims=True)


def end_factors(logits, params, length):
    causal = iota((length, length), 0) >= iota((length, length), 1)
    dt, running, last = scan_terms(logits, params, causal)
    return (jnp.exp(last - running) * dt).astype(BF16), jnp.exp(last)


def local_kernel(frames, rows, columns, head_dim, groups, *refs):
    after, bc, logits, params, x, out, reach = refs
    length = rows * columns
    group = x.shape[2]
    state = bc.shape[1] // 2
    per_group = group // head_dim
    causal = iota((length, length), 0) >= iota((length, length), 1)

    def stored(ref, values, frame, at):
        for row in range(rows):
            to = (row * frames + frame) * columns
            ref[to : to + columns, at] = values[row * columns : (row + 1) * columns]

    for frame in range(frames):
        dt, running, _ = scan_terms(frame_of(logits, frame, rows, frames, columns), params, causal)
        running_t, dt_t = jnp.transpose(running), jnp.transpose(dt)
        bc_rows = frame_of(bc, frame, rows, frames, columns)
        scores = jnp.where(causal, dot_nt(bc_rows[:, state:], bc_rows[:, :state]), 0.0)
        stored(reach, jnp.exp(running), frame, slice(None))
        for piece in range(groups):
            values = frame_x(x, piece, frame, rows, columns)
            mixed = head_mixes(
                scores, running, running_t, dt_t, values, piece * per_group, per_group, head_dim
            )
            stored(out, mixed.astype(BF16), frame, slice(piece * group, (piece + 1) * group))


def tail_of(decays):
    high = decays.astype(BF16)
    return jnp.concatenate([high, (decays - high.astype(F32)).astype(BF16)], axis=0)


def pair_kernel(frames, band, own, far, total):
    rows = (own.shape[0] - TAIL) // frames
    own_decay = own[-TAIL:-8, :].astype(F32) + own[-8:, :].astype(F32)
    far_decay = far[-TAIL:-8, :].astype(F32) + far[-8:, :].astype(F32)
    lower = band[0] % 2 == 0
    through = jnp.where(lower, far_decay, own_decay)
    for frame in range(frames):
        at = slice(frame * rows, (frame + 1) * rows)
        first = jnp.where(lower, own[at, :], far[at, :]).astype(F32)
        second = jnp.where(lower, far[at, :], own[at, :]).astype(F32)
        total[at, :] = (through[frame : frame + 1, :] * first + second).astype(BF16)
    total[frames * rows :, :] = tail_of(own_decay * far_decay)


def merge_kernel(frames, distance, finish, *refs):
    _, band, own, far = refs[:4]
    start = distance == 2
    rest = list(refs[4:])
    before_in = None if start else rest.pop(0)
    band_own, band_far = (rest.pop(0), rest.pop(0)) if finish else (None, None)
    rows = (own.shape[0] - TAIL) // frames
    upper, lower_band = (band[0] // distance) % 2 == 1, band[0] % 2 == 0
    own_decay = own[-TAIL:-8, :].astype(F32) + own[-8:, :].astype(F32)
    far_decay = far[-TAIL:-8, :].astype(F32) + far[-8:, :].astype(F32)
    if start:
        before_decay = jnp.ones_like(own_decay)
    else:
        before_decay = before_in[-8:, :]
    if finish:
        first_decay = jnp.where(
            lower_band,
            band_own[-TAIL:-8, :].astype(F32) + band_own[-8:, :].astype(F32),
            band_far[-TAIL:-8, :].astype(F32) + band_far[-8:, :].astype(F32),
        )
    through = jnp.where(upper, own_decay, far_decay)
    for frame in range(frames):
        at = slice(frame * rows, (frame + 1) * rows)
        row = slice(frame, frame + 1)
        far_state = far[at, :].astype(F32)
        came = before_decay[row, :] * far_state
        if not start:
            came = came + before_in[at, :]
        before = jnp.where(upper, came, 0.0 if start else before_in[at, :])
        if finish:
            keep, give = rest
            first = jnp.where(lower_band, band_own[at, :], band_far[at, :]).astype(F32)
            after = first_decay[row, :] * before + first
            keep[at, :] = jnp.where(lower_band, before, after).astype(BF16)
            give[at, :] = jnp.where(lower_band, after, before).astype(BF16)
        else:
            total, before_out = rest
            own_state = own[at, :].astype(F32)
            early = jnp.where(upper, far_state, own_state)
            late = jnp.where(upper, own_state, far_state)
            total[at, :] = (through[row, :] * early + late).astype(BF16)
            before_out[at, :] = before
    if not finish:
        total[frames * rows :, :] = tail_of(own_decay * far_decay)
        before_out[frames * rows :, :] = jnp.where(upper, before_decay * far_decay, before_decay)


def decays_of(ref):
    return ref[-TAIL:-8, :].astype(F32) + ref[-8:, :].astype(F32)


def places_of(band):
    return band % 2 == 0, (band // 2) % 2 == 1, band // 4 == 1


def cross_kernel(frames, _, band, total, first, near, far, message):
    even, x_high, y_high = places_of(band[0])
    own_decay, first_decay = decays_of(total), decays_of(first)
    diagonal = decays_of(near) * decays_of(far)
    one, zero = jnp.ones_like(own_decay), jnp.zeros_like(own_decay)
    odd_first = jnp.where(y_high, jnp.where(x_high, one, own_decay * diagonal), zero)
    odd_own = jnp.where(x_high & y_high, zero, one)
    of_first = jnp.where(even, jnp.where(x_high, own_decay, one), odd_first)
    of_own = jnp.where(even, jnp.where(x_high, one, first_decay), odd_own)
    rows = (total.shape[0] - TAIL) // frames
    for frame in range(frames):
        at, row = slice(frame * rows, (frame + 1) * rows), slice(frame, frame + 1)
        sent = of_first[row] * first[at, :].astype(F32) + of_own[row] * total[at, :].astype(F32)
        message[at, :] = sent.astype(BF16)
    message[frames * rows :, :] = tail_of(jnp.where(even, own_decay * first_decay, own_decay))


def settle_kernel(frames, _, band, first, second, near, far, band_own, band_far, keep, give):
    even, x_high, y_high = places_of(band[0])
    first_decay, second_decay = decays_of(first), decays_of(second)
    diagonal = decays_of(near) * decays_of(far)
    one, zero = jnp.ones_like(first_decay), jnp.zeros_like(first_decay)
    even_second = jnp.where(y_high, jnp.where(x_high, first_decay, one), zero)
    odd_second = jnp.where(x_high | y_high, one, zero)
    odd_first = jnp.where(y_high, jnp.where(x_high, second_decay, diagonal), zero)
    of_second = jnp.where(even, even_second, odd_second)
    of_first = jnp.where(even, jnp.where(x_high, one, zero), odd_first)
    band_decay = jnp.where(even, decays_of(band_own), decays_of(band_far))
    rows = keep.shape[0] // frames
    for frame in range(frames):
        at, row = slice(frame * rows, (frame + 1) * rows), slice(frame, frame + 1)
        before = of_second[row] * second[at, :].astype(F32) + of_first[row] * first[at, :].astype(F32)
        lower = jnp.where(even, band_own[at, :], band_far[at, :]).astype(F32)
        after = band_decay[row] * before + lower
        keep[at, :] = jnp.where(even, before, after).astype(BF16)
        give[at, :] = jnp.where(even, after, before).astype(BF16)


def incoming_kernel(frames, rows, columns, head_dim, band, out_local, bc, reach, own, other, out):
    state = bc.shape[1] // 2
    half = state // 2
    inner = out.shape[1]
    mine = band[0] % 2 == 0
    matrix = spread_matrix(0, inner, head_dim)
    for frame in range(frames):
        at = slice(frame * half, (frame + 1) * half)
        low = jnp.where(mine, own[at, :], other[at, :])
        high = jnp.where(mine, other[at, :], own[at, :])
        carried = jnp.concatenate([low, high], axis=0)
        for row in range(rows):
            to = (row * frames + frame) * columns
            here = slice(to, to + columns)
            factor = spread(reach[here, :], matrix)
            out[here, :] = out_local[here, :].astype(F32) + factor * dot(bc[here, state:], carried)


def temporal_kernel(
    part, parts, per_group, head_dim, rows, frames, columns, chunk_cols, shares, state, *refs
):
    here_ref, params, payload = refs[:3]
    rest = list(refs[3:])
    carried_in = rest.pop(0) if part > 0 else None
    del rest[:part]
    outs, rest = rest[:shares], rest[shares:]
    carried_out = rest.pop(0) if part + 1 < parts else None
    b_all, c_all, dt_all, decay_all = rest
    here = here_ref[0]
    length = frames * columns
    part_cols = columns // parts
    group = outs[0].shape[1]
    eye = (iota((TAIL, LANES), 0) == iota((TAIL, LANES), 1)) & (iota((TAIL, LANES), 1) < per_group)
    eye = eye.astype(BF16)

    def came(distance):
        return payload.at[rank_of(here ^ distance)]

    for distance in range(shares):
        b_proj, c_proj, logits = unpacked_rest(came(distance), length)
        logits = dot_tn(logits, eye)
        for frame in range(frames):
            at = slice(frame * columns + part * part_cols, frame * columns + (part + 1) * part_cols)
            to = slice(frame * part_cols, (frame + 1) * part_cols)
            b_all[distance, to] = b_proj[at]
            c_all[distance, to] = c_proj[at]
            dt = softplus(logits[at] + params[8:9, :])
            dt_all[distance, to] = dt
            decay_all[distance, to] = -dt * params[9:10, :]

    all_frames = shares * frames
    size = all_frames * chunk_cols

    def order_key(dim):
        index = iota((size, size), dim)
        source = here ^ (index // (frames * chunk_cols))
        frame = source * frames + (index // chunk_cols) % frames
        return (index % chunk_cols) * all_frames + frame

    causal = order_key(0) >= order_key(1)
    order = causal.astype(F32)
    matrix = spread_matrix(0, group, head_dim)
    carried = jnp.zeros((state, group), F32) if part == 0 else carried_in[...]
    places = [(source, frame) for source in range(shares) for frame in range(frames)]
    for chunk in range(part_cols // chunk_cols):

        def gathered(ref_of, pitch=part_cols, offset=0):
            return jnp.concatenate(
                [
                    ref_of(source)[pl.ds(frame * pitch + offset + chunk * chunk_cols, chunk_cols), :]
                    for source, frame in places
                ],
                axis=0,
            )

        values = gathered(came, columns, part * part_cols)
        b_proj = gathered(lambda source: b_all.at[source])
        c_proj = gathered(lambda source: c_all.at[source])
        dt = gathered(lambda source: dt_all.at[source])
        running = dot(order, gathered(lambda source: decay_all.at[source]), precision=EXACT)
        running_t, dt_t = jnp.transpose(running), jnp.transpose(dt)
        scores = jnp.where(causal, dot_nt(c_proj, b_proj), 0.0)
        last = jnp.min(running, axis=0, keepdims=True)
        mixed = head_mixes(scores, running, running_t, dt_t, values, 0, per_group, head_dim)
        ends = jnp.concatenate([running, jnp.broadcast_to(last, (8, LANES))], axis=0)
        reach = dot(jnp.exp(ends).astype(BF16), matrix)
        mixed = mixed + reach[:size] * dot(c_proj, carried.astype(BF16))
        to_end = (jnp.exp(last - running) * dt).astype(BF16)
        scaled = (values.astype(F32) * dot(to_end, matrix)).astype(BF16)
        carried = reach[size : size + 1, :] * carried + dot_tn(b_proj, scaled)
        mixed = mixed.astype(BF16)
        for index, (source, frame) in enumerate(places):
            to = frame * part_cols + chunk * chunk_cols
            outs[source][to : to + chunk_cols, :] = mixed[index * chunk_cols : (index + 1) * chunk_cols]
    if carried_out is not None:
        carried_out[...] = carried


def exit_kernel(part, parts, shares, *refs):
    here, spatial, gate, gain, weight = refs[:5]
    out, temporal, normed, mixed, sems = refs[-5:]
    frames, rows, columns, _ = out.shape
    part_cols = columns // parts
    _, part_len, group = temporal.shape
    groups = shares // rows
    inner = groups * group
    for index in range(shares):
        distance = (shares - index) % shares
        temporal[here[0] ^ distance] = refs[5 + index][...]

    def own(ref, row, at):
        return jnp.concatenate(
            [
                ref[pl.ds((row * frames + frame) * columns + part * part_cols, part_cols), at]
                for frame in range(frames)
            ],
            axis=0,
        )

    gains = gain[...].reshape(1, inner)
    for row in range(rows):
        total = jnp.zeros((part_len, 1), F32)
        kept = []
        for index in range(groups):
            at = slice(index * group, (index + 1) * group)
            gates = own(gate, row, at).astype(F32)
            gated = own(spatial, row, at) + temporal[index * rows + row].astype(F32)
            gated = gated * (gates / (1.0 + jnp.exp(-gates)))
            total = total + jnp.sum(gated * gated, axis=1, keepdims=True)
            kept.append(gated)
        scale = lax.rsqrt(total / inner + EPSILON)
        for index, gated in enumerate(kept):
            at = slice(index * group, (index + 1) * group)
            normed[row * part_len : (row + 1) * part_len, at] = (gated * scale * gains[:, at]).astype(BF16)
    mixed[...] = dot(normed[...], weight[...]).astype(BF16)
    copies = [
        pltpu.make_async_copy(
            mixed.at[pl.ds((row * frames + frame) * part_cols, part_cols), :],
            out.at[frame, row, pl.ds(part * part_cols, part_cols), :],
            sems.at[row * frames + frame],
        )
        for row in range(rows)
        for frame in range(frames)
    ]
    for copy in copies:
        copy.start()
    for copy in copies:
        copy.wait()


def swapped(value, axis, distance):
    count = lax.axis_size(axis)
    return lax.ppermute(value, axis, [(source, source ^ distance) for source in range(count)])


def crossed(value, axis, even, odd):
    count = lax.axis_size(axis)
    pairs = [(source, source ^ (odd if source % 2 else even)) for source in range(count)]
    return lax.ppermute(value, axis, pairs)


def per_device(
    tokens, norm_gain, in_weight, bc_weight, dt_weight, dt_bias, decay_rate, out_gain, out_weight
):
    frames, rows, columns, width = tokens.shape
    heads = decay_rate.shape[1]
    inner = out_weight.shape[0]
    head_dim = inner // heads
    state = bc_weight.shape[1] // 4
    shares = lax.axis_size("tm")
    bands = lax.axis_size("height")
    groups = shares // rows
    group = inner // groups
    per_group = heads // groups
    length = frames * columns
    count = rows * length
    half = state // 2
    chunk_cols = 16
    blocks = parts = 2
    part_len = length // parts
    here = lax.axis_index("tm").astype(jnp.int32).reshape(1)
    band = lax.axis_index("height").astype(jnp.int32).reshape(1)

    packed = (shares, sum(packing(length, group)), group)
    normed, payload, bc_own, logits, params, own, other, band_decays = call(
        functools.partial(entry_kernel, shares, heads, state, blocks),
        "entry",
        [
            shape_of((count, width), BF16),
            shape_of(packed, BF16),
            shape_of((count, 2 * state), BF16),
            shape_of((count, LANES), F32),
            shape_of((16, LANES), F32),
        ]
        + [shape_of((frames * half + TAIL, inner), BF16)] * 2
        + [shape_of((TAIL, inner), BF16)],
        [SCALAR, SCALAR, HBM, WHOLE, WHOLE, WHOLE, HBM, HBM, HBM],
        limit=LARGE,
        outs=[HBM, HBM] + [WHOLE] * 6,
        scratch_shapes=[
            pltpu.VMEM((rows, frames, columns, width), BF16),
            pltpu.VMEM((2 * heads, width), BF16),
            pltpu.VMEM((width, 4 * state), BF16),
            pltpu.VMEM((width, inner), BF16),
            pltpu.VMEM((8, LANES), F32),
            pltpu.VMEM((count, width), BF16),
            pltpu.VMEM(packed, BF16),
            pltpu.SemaphoreType.DMA((rows * frames + 2 + blocks,)),
            pltpu.SemaphoreType.DMA((1 + shares,)),
        ],
    )(here, band, tokens, norm_gain, dt_bias, decay_rate, dt_weight.T, bc_weight, in_weight)

    def sent(parts):
        moved = {d: swapped(parts[d], "tm", d) for d in range(shares - 1, 0, -1)}
        return [parts[0]] + list(moved.values())

    line = [rank_of(device) for device in range(shares)]
    received = lax.all_to_all(
        payload,
        "tm",
        split_axis=0,
        concat_axis=0,
        tiled=True,
        axis_index_groups=[[line.index(rank) for rank in range(shares)]],
    )
    far = swapped(other, "height", 1)
    gate = call(
        functools.partial(gate_kernel, blocks),
        "gate",
        shape_of((count, inner), BF16),
        [ANY, WHOLE, HBM],
        scratch_shapes=[
            pltpu.VMEM((width, inner), BF16),
            pltpu.SemaphoreType.DMA((blocks,)),
        ],
    )(payload, normed, in_weight)

    out_local, reach = call(
        functools.partial(local_kernel, frames, rows, columns, head_dim, groups),
        "spatial_local",
        [shape_of((count, inner), BF16), shape_of((count, LANES), F32)],
        [ANY] + [WHOLE] * 4,
    )(gate, bc_own, logits, params, payload)

    total = call(
        functools.partial(pair_kernel, frames),
        "pair_total",
        shape_of((frames * half + TAIL, inner), BF16),
        [SCALAR, WHOLE, WHOLE],
    )(band, own, far)
    before = []
    distance = 2
    if bands == 8:
        near, far_decays = (swapped(band_decays, "height", distance) for distance in (6, 7))
        first = crossed(total, "height", 2, 4)
        message = call(
            functools.partial(cross_kernel, frames),
            "cross",
            shape_of((frames * half + TAIL, inner), BF16),
            [ANY, SCALAR] + [WHOLE] * 4,
        )(reach, band, total, first, near, far_decays)
        second = crossed(message, "height", 4, 2)
        results = call(
            functools.partial(settle_kernel, frames),
            "settle",
            [shape_of((frames * half, inner), BF16)] * 2,
            [ANY, SCALAR] + [WHOLE] * 6,
        )(reach, band, first, second, near, far_decays, own, far)
        distance = bands
    while distance < bands:
        far_total = swapped(total, "height", distance)
        finish = distance * 2 >= bands
        operands = [reach, band, total, far_total] + before + ([own, far] if finish else [])
        outs = (
            [shape_of((frames * half, inner), BF16)] * 2
            if finish
            else [
                shape_of((frames * half + TAIL, inner), BF16),
                shape_of((frames * half + 8, inner), F32),
            ]
        )
        results = call(
            functools.partial(merge_kernel, frames, distance, finish),
            "merge",
            outs,
            [ANY, SCALAR] + [WHOLE] * (len(operands) - 2),
        )(*operands)
        if not finish:
            total, before = results[0], [results[1]]
        distance *= 2
    keep, give = results
    came = swapped(give, "height", 1)

    spatial_out = call(
        functools.partial(incoming_kernel, frames, rows, columns, head_dim),
        "spatial_incoming",
        shape_of((count, inner), F32),
        [SCALAR] + [WHOLE] * 5,
    )(band, out_local, bc_own, reach, keep, came)

    returned, carried = [], []
    for part in range(parts):
        more = [shape_of((state, group), F32)] if part + 1 < parts else []
        results = call(
            functools.partial(
                temporal_kernel,
                part,
                parts,
                per_group,
                head_dim,
                rows,
                frames,
                columns,
                chunk_cols,
                shares,
                state,
            ),
            "temporal",
            [shape_of((part_len, group), BF16)] * shares + more,
            [SCALAR] + [WHOLE] * (2 + len(carried)) + [ANY] * part,
            scratch_shapes=[
                pltpu.VMEM((shares, part_len, state), BF16),
                pltpu.VMEM((shares, part_len, state), BF16),
                pltpu.VMEM((shares, part_len, LANES), F32),
                pltpu.VMEM((shares, part_len, LANES), F32),
            ],
        )(here, params, received, *carried, *([spatial_out] * part))
        returned.append(sent(results[:shares]))
        carried = results[shares:]

    mixed = []
    for part in range(parts):
        mixed = [
            call(
                functools.partial(exit_kernel, part, parts, shares),
                "exit",
                shape_of(tokens.shape, BF16),
                [SCALAR] + [WHOLE] * (4 + shares) + [HBM] * len(mixed),
                outs=HBM,
                scratch_shapes=[
                    pltpu.VMEM((shares, part_len, group), BF16),
                    pltpu.VMEM((rows * part_len, inner), BF16),
                    pltpu.VMEM((rows * part_len, width), BF16),
                    pltpu.SemaphoreType.DMA((rows * frames,)),
                ],
                input_output_aliases={5 + shares: 0} if mixed else {},
            )(here, spatial_out, gate, out_gain, out_weight, *returned[part], *mixed)
        ]
    return mixed[0]


def solution(mesh):
    in_specs = (P("tm", "height", None, None), P(), P(), P(), P(), P(), P(), P(), P())
    out_specs = P("tm", "height", None, None)
    return jax.shard_map(
        per_device, mesh=mesh, in_specs=in_specs, out_specs=out_specs, check_vma=False
    )
```

```python
import functools
import math

import jax
import jax.numpy as jnp
from jax import lax
from jax.experimental import pallas as pl
from jax.experimental.pallas import tpu as pltpu
from jax.sharding import PartitionSpec as P

EPSILON = 1e-05
LANES = 128
TAIL = 16
LOG2_E = 1.4426950408889634
F32 = jnp.float32
BF16 = jnp.bfloat16
EXACT = lax.Precision.HIGHEST
LARGE = 56 * 1024 * 1024
SMALL = 24 * 1024 * 1024

ANY = pl.BlockSpec(memory_space=pl.ANY)
HBM = pl.BlockSpec(memory_space=pltpu.HBM)
SCALAR = pl.BlockSpec(memory_space=pltpu.SMEM)
WHOLE = pl.BlockSpec(memory_space=pltpu.VMEM)


def call(kernel, name, out_shape, in_specs, limit=SMALL, outs=None, **options):
    return pl.pallas_call(
        kernel,
        out_shape=out_shape,
        in_specs=in_specs,
        out_specs=jax.tree.map(lambda _: WHOLE, out_shape) if outs is None else outs,
        compiler_params=pltpu.CompilerParams(vmem_limit_bytes=limit),
        cost_estimate=pl.CostEstimate(flops=1, bytes_accessed=1, transcendentals=0),
        name=name,
        **options,
    )


def shape_of(shape, dtype):
    return jax.ShapeDtypeStruct(shape, dtype)


def dot(left, right, **options):
    return jnp.dot(left, right, preferred_element_type=F32, **options)


def dot_tn(left, right):
    return lax.dot_general(left, right, (((0,), (0,)), ((), ())), preferred_element_type=F32)


def dot_nt(left, right):
    return lax.dot_general(left, right, (((1,), (1,)), ((), ())), preferred_element_type=F32)


def softplus(values):
    return jnp.maximum(values, 0.0) + jnp.log1p(jnp.exp(-jnp.abs(values)))


def iota(shape, dim):
    return lax.broadcasted_iota(jnp.int32, shape, dim)


def spread_matrix(first_head, width, head_dim):
    return (iota((LANES, width), 0) - first_head == iota((LANES, width), 1) // head_dim).astype(BF16)


def spread(values, matrix):
    high = values.astype(BF16)
    low = (values - high.astype(F32)).astype(BF16)
    return dot(high, matrix) + dot(low, matrix)


def head_mixes(scores, running, running_t, dt_t, x, first_head, heads, head_dim):
    length = scores.shape[0]
    running, running_t = running * LOG2_E, running_t * LOG2_E
    outs = []

    def weights(head):
        spreads = running[:, head : head + 1] - running_t[head : head + 1, :]
        return (scores * jnp.exp2(jnp.minimum(spreads, 0.0)) * dt_t[head : head + 1, :]).astype(BF16)

    head = 0
    while head < heads:
        here = first_head + head
        if head + 1 < heads and 2 * head_dim == LANES:
            both = x[:, head * head_dim : (head + 2) * head_dim]
            first = iota((length, LANES), 1) < head_dim
            zero = jnp.zeros_like(both)
            stacked = jnp.concatenate([jnp.where(first, both, zero), jnp.where(first, zero, both)], axis=0)
            pair = jnp.concatenate([weights(here), weights(here + 1)], axis=1)
            outs.append(dot(pair, stacked))
            head += 2
        else:
            outs.append(dot(weights(here), x[:, head * head_dim : (head + 1) * head_dim]))
            head += 1
    return outs[0] if len(outs) == 1 else jnp.concatenate(outs, axis=1)


def column_copies(weight, scratch, sems, first, offset, blocks):
    width = scratch.shape[1] // blocks
    return [
        pltpu.make_async_copy(
            weight.at[:, pl.ds(offset + index * width, width)],
            scratch.at[:, pl.ds(index * width, width)],
            sems.at[first + index],
        )
        for index in range(blocks)
    ]


def rank_of(device):
    return device ^ (device >> 1)


def packing(length, group):
    columns = group // LANES
    rest = -(-(2 * length + TAIL) // columns)
    return length, -(-rest // TAIL) * TAIL


def pack_rest(ref, length, b_proj, c_proj, dt):
    columns, rest = ref.shape[1] // LANES, ref.shape[0] - length
    blank = jnp.zeros((columns * rest - 2 * length - TAIL, LANES), BF16)
    stacked = jnp.concatenate([b_proj, c_proj, dt, blank], axis=0)
    for column in range(columns):
        ref[length:, column * LANES : (column + 1) * LANES] = stacked[column * rest : (column + 1) * rest]


def unpacked_rest(ref, length):
    columns = ref.shape[1] // LANES
    stacked = jnp.concatenate(
        [ref[length:, column * LANES : (column + 1) * LANES] for column in range(columns)], axis=0
    )
    return stacked[:length], stacked[length : 2 * length], stacked[2 * length : 2 * length + TAIL]


def entry_kernel(shares, heads, state, blocks, *refs):
    here_ref, band, tokens, gain, bias, rates, dt_weight, bc_weight, weight = refs[:9]
    normed_out, payload_out, bc_own, logits, params, own_states, other_states, band_decays = refs[9:17]
    held, dt_held, bc_held, held_weight, table, normed, payload, sems, out_sems = refs[17:]
    frames, rows, columns, width = tokens.shape
    length = frames * columns
    count = rows * length
    groups = shares // rows
    per_group = heads // groups
    group = held_weight.shape[1] // groups

    token_copies = [
        pltpu.make_async_copy(tokens.at[frame, row], held.at[row, frame], sems.at[row * frames + frame])
        for row in range(rows)
        for frame in range(frames)
    ]
    for copy in token_copies:
        copy.start()
    first = rows * frames
    dt_copy = pltpu.make_async_copy(dt_weight, dt_held, sems.at[first])
    dt_copy.start()
    bc_copy = pltpu.make_async_copy(bc_weight, bc_held, sems.at[first + 1])
    bc_copy.start()
    copies = column_copies(weight, held_weight, sems, first + 2, 0, blocks)
    for copy in copies:
        copy.start()

    table[...] = jnp.zeros_like(table)
    table[0:1, : 2 * heads] = bias[...].reshape(1, 2 * heads)
    table[1:2, :heads] = rates[0:1, :]
    table[1:2, heads : 2 * heads] = rates[1:2, :]
    first_head = heads + here_ref[0] // rows * per_group
    lane_in, lane_out = iota((LANES, LANES), 0), iota((LANES, LANES), 1)
    own = ((lane_in == lane_out + first_head) & (lane_out < per_group)).astype(F32)
    params[0:8, :] = table[...]
    params[8:16, :] = dot(table[...], own, precision=EXACT)
    logits[...] = jnp.zeros_like(logits)

    gains = gain[...].reshape(1, width)
    for index, copy in enumerate(token_copies):
        copy.wait()
        values = held[index // frames, index % frames].astype(F32)
        mean_square = jnp.mean(values * values, axis=-1, keepdims=True)
        normed[index * columns : (index + 1) * columns, :] = (
            values * lax.rsqrt(mean_square + EPSILON) * gains
        ).astype(BF16)
    outgoing = [pltpu.make_async_copy(normed, normed_out, out_sems.at[0])]
    outgoing[0].start()
    dt_copy.wait()
    logits[:, : 2 * heads] = dot_nt(normed[...], dt_held[...]).astype(BF16).astype(F32)
    dt_heads = jnp.transpose(logits[...]).astype(BF16)[heads : 2 * heads + TAIL]
    bc_copy.wait()
    bc = dot(normed[...], bc_held[...]).astype(BF16)
    bc_own[...] = bc[:, : 2 * state]
    scan = [
        end_factors(frame_of(logits, frame, rows, frames, columns), params, rows * columns)
        for frame in range(frames)
    ]

    half = state // 2
    head_dim = groups * group // heads
    mine = band[0] % 2 == 0
    b_frames = [frame_of(bc_own, frame, rows, frames, columns)[:, :state] for frame in range(frames)]
    block = held_weight.shape[1] // blocks
    waits = list(copies)
    for part in range(groups):
        for at in range(0, group, block):
            waits.pop(0).wait()
            from_col = part * group + at
            values = dot(normed[...], held_weight[:, from_col : from_col + block]).astype(BF16)
            for row in range(rows):
                payload[rank_of(part * rows + row), :length, at : at + block] = values[
                    row * length : (row + 1) * length
                ]
        for row in range(rows):
            piece = rank_of(part * rows + row)
            here = slice(row * length, (row + 1) * length)
            pack_rest(
                payload.at[piece],
                length,
                bc[here, 2 * state : 3 * state],
                bc[here, 3 * state :],
                dt_heads[part * per_group : part * per_group + TAIL, here],
            )
            outgoing.append(
                pltpu.make_async_copy(payload.at[piece], payload_out.at[piece], out_sems.at[1 + piece])
            )
            outgoing[-1].start()
        cols = slice(part * group, (part + 1) * group)
        matrix = spread_matrix(part * per_group, group, head_dim)
        for frame in range(frames):
            values = frame_x(payload, part, frame, rows, columns)
            scaled = (values.astype(F32) * dot(scan[frame][0], matrix)).astype(BF16)
            fresh = dot_tn(b_frames[frame], scaled).astype(BF16)
            at_rows = slice(frame * half, (frame + 1) * half)
            own_states[at_rows, cols] = jnp.where(mine, fresh[:half], fresh[half:])
            other_states[at_rows, cols] = jnp.where(mine, fresh[half:], fresh[:half])
    whole = [decay for _, decay in scan] + [jnp.zeros((8 - frames, LANES), F32)]
    decays = spread(jnp.concatenate(whole, axis=0), spread_matrix(0, groups * group, head_dim))
    tail = tail_of(decays)
    own_states[frames * half :, :] = tail
    other_states[frames * half :, :] = tail
    band_decays[...] = tail
    for copy in outgoing:
        copy.wait()


def gate_kernel(blocks, after, normed, weight, out, held_weight, sems):
    inner = held_weight.shape[1]
    copies = column_copies(weight, held_weight, sems, 0, inner, blocks)
    for copy in copies:
        copy.start()
    block = inner // blocks
    for index, copy in enumerate(copies):
        copy.wait()
        at = slice(index * block, (index + 1) * block)
        out[:, at] = dot(normed[...], held_weight[:, at]).astype(BF16)


def frame_of(ref, frame, rows, frames, columns):
    return jnp.concatenate(
        [
            ref[(row * frames + frame) * columns : (row * frames + frame + 1) * columns, :]
            for row in range(rows)
        ],
        axis=0,
    )


def frame_x(payload, part, frame, rows, columns):
    return jnp.concatenate(
        [
            payload[rank_of(part * rows + row), frame * columns : (frame + 1) * columns, :]
            for row in range(rows)
        ],
        axis=0,
    )


def scan_terms(logits, params, causal):
    dt = softplus(logits + params[0:1, :])
    running = dot(causal.astype(F32), -dt * params[1:2, :], precision=EXACT)
    return dt, running, jnp.min(running, axis=0, keepdims=True)


def end_factors(logits, params, length):
    causal = iota((length, length), 0) >= iota((length, length), 1)
    dt, running, last = scan_terms(logits, params, causal)
    return (jnp.exp(last - running) * dt).astype(BF16), jnp.exp(last)


def local_kernel(frames, rows, columns, head_dim, groups, *refs):
    after, bc, logits, params, x, out, reach = refs
    length = rows * columns
    group = x.shape[2]
    state = bc.shape[1] // 2
    per_group = group // head_dim
    causal = iota((length, length), 0) >= iota((length, length), 1)

    def stored(ref, values, frame, at):
        for row in range(rows):
            to = (row * frames + frame) * columns
            ref[to : to + columns, at] = values[row * columns : (row + 1) * columns]

    for frame in range(frames):
        dt, running, _ = scan_terms(frame_of(logits, frame, rows, frames, columns), params, causal)
        running_t, dt_t = jnp.transpose(running), jnp.transpose(dt)
        bc_rows = frame_of(bc, frame, rows, frames, columns)
        scores = jnp.where(causal, dot_nt(bc_rows[:, state:], bc_rows[:, :state]), 0.0)
        stored(reach, jnp.exp(running), frame, slice(None))
        for piece in range(groups):
            values = frame_x(x, piece, frame, rows, columns)
            mixed = head_mixes(
                scores, running, running_t, dt_t, values, piece * per_group, per_group, head_dim
            )
            stored(out, mixed.astype(BF16), frame, slice(piece * group, (piece + 1) * group))


def tail_of(decays):
    high = decays.astype(BF16)
    return jnp.concatenate([high, (decays - high.astype(F32)).astype(BF16)], axis=0)


def pair_kernel(frames, band, own, far, total):
    rows = (own.shape[0] - TAIL) // frames
    own_decay = own[-TAIL:-8, :].astype(F32) + own[-8:, :].astype(F32)
    far_decay = far[-TAIL:-8, :].astype(F32) + far[-8:, :].astype(F32)
    lower = band[0] % 2 == 0
    through = jnp.where(lower, far_decay, own_decay)
    for frame in range(frames):
        at = slice(frame * rows, (frame + 1) * rows)
        first = jnp.where(lower, own[at, :], far[at, :]).astype(F32)
        second = jnp.where(lower, far[at, :], own[at, :]).astype(F32)
        total[at, :] = (through[frame : frame + 1, :] * first + second).astype(BF16)
    total[frames * rows :, :] = tail_of(own_decay * far_decay)


def merge_kernel(frames, distance, finish, *refs):
    _, band, own, far = refs[:4]
    start = distance == 2
    rest = list(refs[4:])
    before_in = None if start else rest.pop(0)
    band_own, band_far = (rest.pop(0), rest.pop(0)) if finish else (None, None)
    rows = (own.shape[0] - TAIL) // frames
    upper, lower_band = (band[0] // distance) % 2 == 1, band[0] % 2 == 0
    own_decay = own[-TAIL:-8, :].astype(F32) + own[-8:, :].astype(F32)
    far_decay = far[-TAIL:-8, :].astype(F32) + far[-8:, :].astype(F32)
    if start:
        before_decay = jnp.ones_like(own_decay)
    else:
        before_decay = before_in[-8:, :]
    if finish:
        first_decay = jnp.where(
            lower_band,
            band_own[-TAIL:-8, :].astype(F32) + band_own[-8:, :].astype(F32),
            band_far[-TAIL:-8, :].astype(F32) + band_far[-8:, :].astype(F32),
        )
    through = jnp.where(upper, own_decay, far_decay)
    for frame in range(frames):
        at = slice(frame * rows, (frame + 1) * rows)
        row = slice(frame, frame + 1)
        far_state = far[at, :].astype(F32)
        came = before_decay[row, :] * far_state
        if not start:
            came = came + before_in[at, :]
        before = jnp.where(upper, came, 0.0 if start else before_in[at, :])
        if finish:
            keep, give = rest
            first = jnp.where(lower_band, band_own[at, :], band_far[at, :]).astype(F32)
            after = first_decay[row, :] * before + first
            keep[at, :] = jnp.where(lower_band, before, after).astype(BF16)
            give[at, :] = jnp.where(lower_band, after, before).astype(BF16)
        else:
            total, before_out = rest
            own_state = own[at, :].astype(F32)
            early = jnp.where(upper, far_state, own_state)
            late = jnp.where(upper, own_state, far_state)
            total[at, :] = (through[row, :] * early + late).astype(BF16)
            before_out[at, :] = before
    if not finish:
        total[frames * rows :, :] = tail_of(own_decay * far_decay)
        before_out[frames * rows :, :] = jnp.where(upper, before_decay * far_decay, before_decay)


def decays_of(ref):
    return ref[-TAIL:-8, :].astype(F32) + ref[-8:, :].astype(F32)


def places_of(band):
    return band % 2 == 0, (band // 2) % 2 == 1, band // 4 == 1


def cross_kernel(frames, _, band, total, first, near, far, message):
    even, x_high, y_high = places_of(band[0])
    own_decay, first_decay = decays_of(total), decays_of(first)
    diagonal = decays_of(near) * decays_of(far)
    one, zero = jnp.ones_like(own_decay), jnp.zeros_like(own_decay)
    odd_first = jnp.where(y_high, jnp.where(x_high, one, own_decay * diagonal), zero)
    odd_own = jnp.where(x_high & y_high, zero, one)
    of_first = jnp.where(even, jnp.where(x_high, own_decay, one), odd_first)
    of_own = jnp.where(even, jnp.where(x_high, one, first_decay), odd_own)
    rows = (total.shape[0] - TAIL) // frames
    for frame in range(frames):
        at, row = slice(frame * rows, (frame + 1) * rows), slice(frame, frame + 1)
        sent = of_first[row] * first[at, :].astype(F32) + of_own[row] * total[at, :].astype(F32)
        message[at, :] = sent.astype(BF16)
    message[frames * rows :, :] = tail_of(jnp.where(even, own_decay * first_decay, own_decay))


def settle_kernel(frames, _, band, first, second, near, far, band_own, band_far, keep, give):
    even, x_high, y_high = places_of(band[0])
    first_decay, second_decay = decays_of(first), decays_of(second)
    diagonal = decays_of(near) * decays_of(far)
    one, zero = jnp.ones_like(first_decay), jnp.zeros_like(first_decay)
    even_second = jnp.where(y_high, jnp.where(x_high, first_decay, one), zero)
    odd_second = jnp.where(x_high | y_high, one, zero)
    odd_first = jnp.where(y_high, jnp.where(x_high, second_decay, diagonal), zero)
    of_second = jnp.where(even, even_second, odd_second)
    of_first = jnp.where(even, jnp.where(x_high, one, zero), odd_first)
    band_decay = jnp.where(even, decays_of(band_own), decays_of(band_far))
    rows = keep.shape[0] // frames
    for frame in range(frames):
        at, row = slice(frame * rows, (frame + 1) * rows), slice(frame, frame + 1)
        before = of_second[row] * second[at, :].astype(F32) + of_first[row] * first[at, :].astype(F32)
        lower = jnp.where(even, band_own[at, :], band_far[at, :]).astype(F32)
        after = band_decay[row] * before + lower
        keep[at, :] = jnp.where(even, before, after).astype(BF16)
        give[at, :] = jnp.where(even, after, before).astype(BF16)


def incoming_kernel(frames, rows, columns, head_dim, band, out_local, bc, reach, own, other, out):
    state = bc.shape[1] // 2
    half = state // 2
    inner = out.shape[1]
    mine = band[0] % 2 == 0
    matrix = spread_matrix(0, inner, head_dim)
    for frame in range(frames):
        at = slice(frame * half, (frame + 1) * half)
        low = jnp.where(mine, own[at, :], other[at, :])
        high = jnp.where(mine, other[at, :], own[at, :])
        carried = jnp.concatenate([low, high], axis=0)
        for row in range(rows):
            to = (row * frames + frame) * columns
            here = slice(to, to + columns)
            factor = spread(reach[here, :], matrix)
            out[here, :] = out_local[here, :].astype(F32) + factor * dot(bc[here, state:], carried)


def temporal_kernel(
    part, parts, per_group, head_dim, rows, frames, columns, chunk_cols, shares, state, *refs
):
    here_ref, params, payload = refs[:3]
    rest = list(refs[3:])
    carried_in = rest.pop(0) if part > 0 else None
    del rest[:part]
    outs, rest = rest[:shares], rest[shares:]
    carried_out = rest.pop(0) if part + 1 < parts else None
    b_all, c_all, dt_all, decay_all = rest
    here = here_ref[0]
    length = frames * columns
    part_cols = columns // parts
    group = outs[0].shape[1]
    eye = (iota((TAIL, LANES), 0) == iota((TAIL, LANES), 1)) & (iota((TAIL, LANES), 1) < per_group)
    eye = eye.astype(BF16)

    def came(distance):
        return payload.at[rank_of(here ^ distance)]

    for distance in range(shares):
        b_proj, c_proj, logits = unpacked_rest(came(distance), length)
        logits = dot_tn(logits, eye)
        for frame in range(frames):
            at = slice(frame * columns + part * part_cols, frame * columns + (part + 1) * part_cols)
            to = slice(frame * part_cols, (frame + 1) * part_cols)
            b_all[distance, to] = b_proj[at]
            c_all[distance, to] = c_proj[at]
            dt = softplus(logits[at] + params[8:9, :])
            dt_all[distance, to] = dt
            decay_all[distance, to] = -dt * params[9:10, :]

    all_frames = shares * frames
    size = all_frames * chunk_cols

    def order_key(dim):
        index = iota((size, size), dim)
        source = here ^ (index // (frames * chunk_cols))
        frame = source * frames + (index // chunk_cols) % frames
        return (index % chunk_cols) * all_frames + frame

    causal = order_key(0) >= order_key(1)
    order = causal.astype(F32)
    matrix = spread_matrix(0, group, head_dim)
    carried = jnp.zeros((state, group), F32) if part == 0 else carried_in[...]
    places = [(source, frame) for source in range(shares) for frame in range(frames)]
    for chunk in range(part_cols // chunk_cols):

        def gathered(ref_of, pitch=part_cols, offset=0):
            return jnp.concatenate(
                [
                    ref_of(source)[pl.ds(frame * pitch + offset + chunk * chunk_cols, chunk_cols), :]
                    for source, frame in places
                ],
                axis=0,
            )

        values = gathered(came, columns, part * part_cols)
        b_proj = gathered(lambda source: b_all.at[source])
        c_proj = gathered(lambda source: c_all.at[source])
        dt = gathered(lambda source: dt_all.at[source])
        running = dot(order, gathered(lambda source: decay_all.at[source]), precision=EXACT)
        running_t, dt_t = jnp.transpose(running), jnp.transpose(dt)
        scores = jnp.where(causal, dot_nt(c_proj, b_proj), 0.0)
        last = jnp.min(running, axis=0, keepdims=True)
        mixed = head_mixes(scores, running, running_t, dt_t, values, 0, per_group, head_dim)
        ends = jnp.concatenate([running, jnp.broadcast_to(last, (8, LANES))], axis=0)
        reach = dot(jnp.exp(ends).astype(BF16), matrix)
        mixed = mixed + reach[:size] * dot(c_proj, carried.astype(BF16))
        to_end = (jnp.exp(last - running) * dt).astype(BF16)
        scaled = (values.astype(F32) * dot(to_end, matrix)).astype(BF16)
        carried = reach[size : size + 1, :] * carried + dot_tn(b_proj, scaled)
        mixed = mixed.astype(BF16)
        for index, (source, frame) in enumerate(places):
            to = frame * part_cols + chunk * chunk_cols
            outs[source][to : to + chunk_cols, :] = mixed[index * chunk_cols : (index + 1) * chunk_cols]
    if carried_out is not None:
        carried_out[...] = carried


def exit_kernel(part, parts, shares, *refs):
    here, spatial, gate, gain, weight = refs[:5]
    out, temporal, normed, mixed, sems = refs[-5:]
    frames, rows, columns, _ = out.shape
    part_cols = columns // parts
    _, part_len, group = temporal.shape
    groups = shares // rows
    inner = groups * group
    for index in range(shares):
        distance = (shares - index) % shares
        temporal[here[0] ^ distance] = refs[5 + index][...]

    def own(ref, row, at):
        return jnp.concatenate(
            [
                ref[pl.ds((row * frames + frame) * columns + part * part_cols, part_cols), at]
                for frame in range(frames)
            ],
            axis=0,
        )

    gains = gain[...].reshape(1, inner)
    for row in range(rows):
        total = jnp.zeros((part_len, 1), F32)
        kept = []
        for index in range(groups):
            at = slice(index * group, (index + 1) * group)
            gates = own(gate, row, at).astype(F32)
            gated = own(spatial, row, at) + temporal[index * rows + row].astype(F32)
            gated = gated * (gates / (1.0 + jnp.exp(-gates)))
            total = total + jnp.sum(gated * gated, axis=1, keepdims=True)
            kept.append(gated)
        scale = lax.rsqrt(total / inner + EPSILON)
        for index, gated in enumerate(kept):
            at = slice(index * group, (index + 1) * group)
            normed[row * part_len : (row + 1) * part_len, at] = (gated * scale * gains[:, at]).astype(BF16)
    mixed[...] = dot(normed[...], weight[...]).astype(BF16)
    copies = [
        pltpu.make_async_copy(
            mixed.at[pl.ds((row * frames + frame) * part_cols, part_cols), :],
            out.at[frame, row, pl.ds(part * part_cols, part_cols), :],
            sems.at[row * frames + frame],
        )
        for row in range(rows)
        for frame in range(frames)
    ]
    for copy in copies:
        copy.start()
    for copy in copies:
        copy.wait()


def swapped(value, axis, distance):
    count = lax.axis_size(axis)
    return lax.ppermute(value, axis, [(source, source ^ distance) for source in range(count)])


def crossed(value, axis, even, odd):
    count = lax.axis_size(axis)
    pairs = [(source, source ^ (odd if source % 2 else even)) for source in range(count)]
    return lax.ppermute(value, axis, pairs)


def per_device(
    tokens, norm_gain, in_weight, bc_weight, dt_weight, dt_bias, decay_rate, out_gain, out_weight
):
    frames, rows, columns, width = tokens.shape
    heads = decay_rate.shape[1]
    inner = out_weight.shape[0]
    head_dim = inner // heads
    state = bc_weight.shape[1] // 4
    shares = lax.axis_size("tm")
    bands = lax.axis_size("height")
    groups = shares // rows
    group = inner // groups
    per_group = heads // groups
    length = frames * columns
    count = rows * length
    half = state // 2
    chunk_cols = 16
    parts = 2
    blocks = inner // (2 * LANES) if group % (2 * LANES) == 0 else groups
    part_len = length // parts
    here = lax.axis_index("tm").astype(jnp.int32).reshape(1)
    band = lax.axis_index("height").astype(jnp.int32).reshape(1)

    packed = (shares, sum(packing(length, group)), group)
    normed, payload, bc_own, logits, params, own, other, band_decays = call(
        functools.partial(entry_kernel, shares, heads, state, blocks),
        "entry",
        [
            shape_of((count, width), BF16),
            shape_of(packed, BF16),
            shape_of((count, 2 * state), BF16),
            shape_of((count, LANES), F32),
            shape_of((16, LANES), F32),
        ]
        + [shape_of((frames * half + TAIL, inner), BF16)] * 2
        + [shape_of((TAIL, inner), BF16)],
        [SCALAR, SCALAR, HBM, WHOLE, WHOLE, WHOLE, HBM, HBM, HBM],
        limit=LARGE,
        outs=[HBM, HBM] + [WHOLE] * 6,
        scratch_shapes=[
            pltpu.VMEM((rows, frames, columns, width), BF16),
            pltpu.VMEM((2 * heads, width), BF16),
            pltpu.VMEM((width, 4 * state), BF16),
            pltpu.VMEM((width, inner), BF16),
            pltpu.VMEM((8, LANES), F32),
            pltpu.VMEM((count, width), BF16),
            pltpu.VMEM(packed, BF16),
            pltpu.SemaphoreType.DMA((rows * frames + 2 + blocks,)),
            pltpu.SemaphoreType.DMA((1 + shares,)),
        ],
    )(here, band, tokens, norm_gain, dt_bias, decay_rate, dt_weight.T, bc_weight, in_weight)

    def sent(parts):
        moved = {d: swapped(parts[d], "tm", d) for d in range(shares - 1, 0, -1)}
        return [parts[0]] + list(moved.values())

    line = [rank_of(device) for device in range(shares)]
    received = lax.all_to_all(
        payload,
        "tm",
        split_axis=0,
        concat_axis=0,
        tiled=True,
        axis_index_groups=[[line.index(rank) for rank in range(shares)]],
    )
    far = swapped(other, "height", 1)
    gate = call(
        functools.partial(gate_kernel, 2),
        "gate",
        shape_of((count, inner), BF16),
        [ANY, WHOLE, HBM],
        scratch_shapes=[
            pltpu.VMEM((width, inner), BF16),
            pltpu.SemaphoreType.DMA((2,)),
        ],
    )(payload, normed, in_weight)

    out_local, reach = call(
        functools.partial(local_kernel, frames, rows, columns, head_dim, groups),
        "spatial_local",
        [shape_of((count, inner), BF16), shape_of((count, LANES), F32)],
        [ANY] + [WHOLE] * 4,
    )(gate, bc_own, logits, params, payload)

    total = call(
        functools.partial(pair_kernel, frames),
        "pair_total",
        shape_of((frames * half + TAIL, inner), BF16),
        [SCALAR, WHOLE, WHOLE],
    )(band, own, far)
    before = []
    distance = 2
    if bands == 8:
        near, far_decays = (swapped(band_decays, "height", distance) for distance in (6, 7))
        first = crossed(total, "height", 2, 4)
        message = call(
            functools.partial(cross_kernel, frames),
            "cross",
            shape_of((frames * half + TAIL, inner), BF16),
            [ANY, SCALAR] + [WHOLE] * 4,
        )(reach, band, total, first, near, far_decays)
        second = crossed(message, "height", 4, 2)
        results = call(
            functools.partial(settle_kernel, frames),
            "settle",
            [shape_of((frames * half, inner), BF16)] * 2,
            [ANY, SCALAR] + [WHOLE] * 6,
        )(reach, band, first, second, near, far_decays, own, far)
        distance = bands
    while distance < bands:
        far_total = swapped(total, "height", distance)
        finish = distance * 2 >= bands
        operands = [reach, band, total, far_total] + before + ([own, far] if finish else [])
        outs = (
            [shape_of((frames * half, inner), BF16)] * 2
            if finish
            else [
                shape_of((frames * half + TAIL, inner), BF16),
                shape_of((frames * half + 8, inner), F32),
            ]
        )
        results = call(
            functools.partial(merge_kernel, frames, distance, finish),
            "merge",
            outs,
            [ANY, SCALAR] + [WHOLE] * (len(operands) - 2),
        )(*operands)
        if not finish:
            total, before = results[0], [results[1]]
        distance *= 2
    keep, give = results
    came = swapped(give, "height", 1)

    spatial_out = call(
        functools.partial(incoming_kernel, frames, rows, columns, head_dim),
        "spatial_incoming",
        shape_of((count, inner), F32),
        [SCALAR] + [WHOLE] * 5,
    )(band, out_local, bc_own, reach, keep, came)

    returned, carried = [], []
    for part in range(parts):
        more = [shape_of((state, group), F32)] if part + 1 < parts else []
        results = call(
            functools.partial(
                temporal_kernel,
                part,
                parts,
                per_group,
                head_dim,
                rows,
                frames,
                columns,
                chunk_cols,
                shares,
                state,
            ),
            "temporal",
            [shape_of((part_len, group), BF16)] * shares + more,
            [SCALAR] + [WHOLE] * (2 + len(carried)) + [ANY] * part,
            scratch_shapes=[
                pltpu.VMEM((shares, part_len, state), BF16),
                pltpu.VMEM((shares, part_len, state), BF16),
                pltpu.VMEM((shares, part_len, LANES), F32),
                pltpu.VMEM((shares, part_len, LANES), F32),
            ],
        )(here, params, received, *carried, *([spatial_out] * part))
        returned.append(sent(results[:shares]))
        carried = results[shares:]

    mixed = []
    for part in range(parts):
        mixed = [
            call(
                functools.partial(exit_kernel, part, parts, shares),
                "exit",
                shape_of(tokens.shape, BF16),
                [SCALAR] + [WHOLE] * (4 + shares) + [HBM] * len(mixed),
                outs=HBM,
                scratch_shapes=[
                    pltpu.VMEM((shares, part_len, group), BF16),
                    pltpu.VMEM((rows * part_len, inner), BF16),
                    pltpu.VMEM((rows * part_len, width), BF16),
                    pltpu.SemaphoreType.DMA((rows * frames,)),
                ],
                input_output_aliases={5 + shares: 0} if mixed else {},
            )(here, spatial_out, gate, out_gain, out_weight, *returned[part], *mixed)
        ]
    return mixed[0]


def solution(mesh):
    in_specs = (P("tm", "height", None, None), P(), P(), P(), P(), P(), P(), P(), P())
    out_specs = P("tm", "height", None, None)
    return jax.shard_map(
        per_device, mesh=mesh, in_specs=in_specs, out_specs=out_specs, check_vma=False
    )
```

```python
import functools
import math

import jax
import jax.numpy as jnp
from jax import lax
from jax.experimental import pallas as pl
from jax.experimental.pallas import tpu as pltpu
from jax.sharding import PartitionSpec as P

EPSILON = 1e-05
LANES = 128
TAIL = 16
LOG2_E = 1.4426950408889634
F32 = jnp.float32
BF16 = jnp.bfloat16
EXACT = lax.Precision.HIGHEST
LARGE = 56 * 1024 * 1024
SMALL = 24 * 1024 * 1024

ANY = pl.BlockSpec(memory_space=pl.ANY)
HBM = pl.BlockSpec(memory_space=pltpu.HBM)
SCALAR = pl.BlockSpec(memory_space=pltpu.SMEM)
WHOLE = pl.BlockSpec(memory_space=pltpu.VMEM)


def call(kernel, name, out_shape, in_specs, limit=SMALL, outs=None, **options):
    return pl.pallas_call(
        kernel,
        out_shape=out_shape,
        in_specs=in_specs,
        out_specs=jax.tree.map(lambda _: WHOLE, out_shape) if outs is None else outs,
        compiler_params=pltpu.CompilerParams(vmem_limit_bytes=limit),
        cost_estimate=pl.CostEstimate(flops=1, bytes_accessed=1, transcendentals=0),
        name=name,
        **options,
    )


def shape_of(shape, dtype):
    return jax.ShapeDtypeStruct(shape, dtype)


def dot(left, right, **options):
    return jnp.dot(left, right, preferred_element_type=F32, **options)


def dot_tn(left, right):
    return lax.dot_general(left, right, (((0,), (0,)), ((), ())), preferred_element_type=F32)


def dot_nt(left, right):
    return lax.dot_general(left, right, (((1,), (1,)), ((), ())), preferred_element_type=F32)


def softplus(values):
    return jnp.maximum(values, 0.0) + jnp.log1p(jnp.exp(-jnp.abs(values)))


def iota(shape, dim):
    return lax.broadcasted_iota(jnp.int32, shape, dim)


def spread_matrix(first_head, width, head_dim):
    return (iota((LANES, width), 0) - first_head == iota((LANES, width), 1) // head_dim).astype(BF16)


def spread(values, matrix):
    high = values.astype(BF16)
    low = (values - high.astype(F32)).astype(BF16)
    return dot(high, matrix) + dot(low, matrix)


def head_mixes(scores, running, running_t, dt_t, x, first_head, heads, head_dim):
    length = scores.shape[0]
    running, running_t = running * LOG2_E, running_t * LOG2_E
    outs = []

    def weights(head):
        spreads = running[:, head : head + 1] - running_t[head : head + 1, :]
        return (scores * jnp.exp2(jnp.minimum(spreads, 0.0)) * dt_t[head : head + 1, :]).astype(BF16)

    head = 0
    while head < heads:
        here = first_head + head
        if head + 1 < heads and 2 * head_dim == LANES:
            both = x[:, head * head_dim : (head + 2) * head_dim]
            first = iota((length, LANES), 1) < head_dim
            zero = jnp.zeros_like(both)
            stacked = jnp.concatenate([jnp.where(first, both, zero), jnp.where(first, zero, both)], axis=0)
            pair = jnp.concatenate([weights(here), weights(here + 1)], axis=1)
            outs.append(dot(pair, stacked))
            head += 2
        else:
            outs.append(dot(weights(here), x[:, head * head_dim : (head + 1) * head_dim]))
            head += 1
    return outs[0] if len(outs) == 1 else jnp.concatenate(outs, axis=1)


def column_copies(weight, scratch, sems, first, offset, blocks):
    width = scratch.shape[1] // blocks
    return [
        pltpu.make_async_copy(
            weight.at[:, pl.ds(offset + index * width, width)],
            scratch.at[:, pl.ds(index * width, width)],
            sems.at[first + index],
        )
        for index in range(blocks)
    ]


def rank_of(device):
    return device ^ (device >> 1)


def packing(length, group):
    columns = group // LANES
    rest = -(-(2 * length + TAIL) // columns)
    return length, -(-rest // TAIL) * TAIL


def pack_rest(ref, length, b_proj, c_proj, dt):
    columns, rest = ref.shape[1] // LANES, ref.shape[0] - length
    blank = jnp.zeros((columns * rest - 2 * length - TAIL, LANES), BF16)
    stacked = jnp.concatenate([b_proj, c_proj, dt, blank], axis=0)
    for column in range(columns):
        ref[length:, column * LANES : (column + 1) * LANES] = stacked[column * rest : (column + 1) * rest]


def unpacked_rest(ref, length):
    columns = ref.shape[1] // LANES
    stacked = jnp.concatenate(
        [ref[length:, column * LANES : (column + 1) * LANES] for column in range(columns)], axis=0
    )
    return stacked[:length], stacked[length : 2 * length], stacked[2 * length : 2 * length + TAIL]


def entry_kernel(shares, heads, state, blocks, *refs):
    here_ref, band, tokens, gain, bias, rates, dt_weight, bc_weight, weight = refs[:9]
    normed_out, payload_out, bc_own, logits, params, own_states, other_states, band_decays = refs[9:17]
    held, dt_held, bc_held, held_weight, table, normed, payload, sems, out_sems = refs[17:]
    frames, rows, columns, width = tokens.shape
    length = frames * columns
    count = rows * length
    groups = shares // rows
    per_group = heads // groups
    group = held_weight.shape[1] // groups

    token_copies = [
        pltpu.make_async_copy(tokens.at[frame, row], held.at[row, frame], sems.at[row * frames + frame])
        for row in range(rows)
        for frame in range(frames)
    ]
    for copy in token_copies:
        copy.start()
    first = rows * frames
    dt_copy = pltpu.make_async_copy(dt_weight, dt_held, sems.at[first])
    dt_copy.start()
    bc_copy = pltpu.make_async_copy(bc_weight, bc_held, sems.at[first + 1])
    bc_copy.start()
    copies = column_copies(weight, held_weight, sems, first + 2, 0, blocks)
    for copy in copies:
        copy.start()

    table[...] = jnp.zeros_like(table)
    table[0:1, : 2 * heads] = bias[...].reshape(1, 2 * heads)
    table[1:2, :heads] = rates[0:1, :]
    table[1:2, heads : 2 * heads] = rates[1:2, :]
    first_head = heads + here_ref[0] // rows * per_group
    lane_in, lane_out = iota((LANES, LANES), 0), iota((LANES, LANES), 1)
    own = ((lane_in == lane_out + first_head) & (lane_out < per_group)).astype(F32)
    params[0:8, :] = table[...]
    params[8:16, :] = dot(table[...], own, precision=EXACT)
    logits[...] = jnp.zeros_like(logits)

    gains = gain[...].reshape(1, width)
    for index, copy in enumerate(token_copies):
        copy.wait()
        values = held[index // frames, index % frames].astype(F32)
        mean_square = jnp.mean(values * values, axis=-1, keepdims=True)
        normed[index * columns : (index + 1) * columns, :] = (
            values * lax.rsqrt(mean_square + EPSILON) * gains
        ).astype(BF16)
    outgoing = [pltpu.make_async_copy(normed, normed_out, out_sems.at[0])]
    outgoing[0].start()
    dt_copy.wait()
    logits[:, : 2 * heads] = dot_nt(normed[...], dt_held[...]).astype(BF16).astype(F32)
    dt_heads = jnp.transpose(logits[...]).astype(BF16)[heads : 2 * heads + TAIL]
    bc_copy.wait()
    bc = dot(normed[...], bc_held[...]).astype(BF16)
    bc_own[...] = bc[:, : 2 * state]
    scan = [
        end_factors(frame_of(logits, frame, rows, frames, columns), params, rows * columns)
        for frame in range(frames)
    ]

    block = held_weight.shape[1] // blocks
    for index, copy in enumerate(copies):
        copy.wait()
        at = index * block
        values = dot(normed[...], held_weight[:, at : at + block]).astype(BF16)
        for inside in range(0, block, group):
            part = (at + inside) // group
            for row in range(rows):
                piece = rank_of(part * rows + row)
                here = slice(row * length, (row + 1) * length)
                payload[piece, :length, :] = values[here, inside : inside + group]
                pack_rest(
                    payload.at[piece],
                    length,
                    bc[here, 2 * state : 3 * state],
                    bc[here, 3 * state :],
                    dt_heads[part * per_group : part * per_group + TAIL, here],
                )
                outgoing.append(
                    pltpu.make_async_copy(
                        payload.at[piece], payload_out.at[piece], out_sems.at[1 + piece]
                    )
                )
                outgoing[-1].start()
    half = state // 2
    head_dim = groups * group // heads
    mine = band[0] % 2 == 0
    matrix = spread_matrix(0, groups * group, head_dim)
    factors = dot(jnp.concatenate([factor for factor, _ in scan], axis=0), matrix)
    span = rows * columns
    for frame in range(frames):
        b_proj = frame_of(bc_own, frame, rows, frames, columns)[:, :state]
        values = jnp.concatenate(
            [frame_x(payload, part, frame, rows, columns) for part in range(groups)], axis=1
        )
        scaled = (values.astype(F32) * factors[frame * span : (frame + 1) * span]).astype(BF16)
        fresh = dot_tn(b_proj, scaled).astype(BF16)
        at_rows = slice(frame * half, (frame + 1) * half)
        own_states[at_rows, :] = jnp.where(mine, fresh[:half], fresh[half:])
        other_states[at_rows, :] = jnp.where(mine, fresh[half:], fresh[:half])
    whole = [decay for _, decay in scan] + [jnp.zeros((8 - frames, LANES), F32)]
    decays = spread(jnp.concatenate(whole, axis=0), matrix)
    tail = tail_of(decays)
    own_states[frames * half :, :] = tail
    other_states[frames * half :, :] = tail
    band_decays[...] = tail
    for copy in outgoing:
        copy.wait()


def gate_kernel(blocks, after, normed, weight, out, held_weight, sems):
    inner = held_weight.shape[1]
    copies = column_copies(weight, held_weight, sems, 0, inner, blocks)
    for copy in copies:
        copy.start()
    block = inner // blocks
    for index, copy in enumerate(copies):
        copy.wait()
        at = slice(index * block, (index + 1) * block)
        out[:, at] = dot(normed[...], held_weight[:, at]).astype(BF16)


def frame_of(ref, frame, rows, frames, columns):
    return jnp.concatenate(
        [
            ref[(row * frames + frame) * columns : (row * frames + frame + 1) * columns, :]
            for row in range(rows)
        ],
        axis=0,
    )


def frame_x(payload, part, frame, rows, columns):
    return jnp.concatenate(
        [
            payload[rank_of(part * rows + row), frame * columns : (frame + 1) * columns, :]
            for row in range(rows)
        ],
        axis=0,
    )


def scan_terms(logits, params, causal):
    dt = softplus(logits + params[0:1, :])
    running = dot(causal.astype(F32), -dt * params[1:2, :], precision=EXACT)
    return dt, running, jnp.min(running, axis=0, keepdims=True)


def end_factors(logits, params, length):
    causal = iota((length, length), 0) >= iota((length, length), 1)
    dt, running, last = scan_terms(logits, params, causal)
    return (jnp.exp(last - running) * dt).astype(BF16), jnp.exp(last)


def local_kernel(frames, rows, columns, head_dim, groups, *refs):
    after, bc, logits, params, x, out, reach = refs
    length = rows * columns
    group = x.shape[2]
    state = bc.shape[1] // 2
    per_group = group // head_dim
    causal = iota((length, length), 0) >= iota((length, length), 1)

    def stored(ref, values, frame, at):
        for row in range(rows):
            to = (row * frames + frame) * columns
            ref[to : to + columns, at] = values[row * columns : (row + 1) * columns]

    for frame in range(frames):
        dt, running, _ = scan_terms(frame_of(logits, frame, rows, frames, columns), params, causal)
        running_t, dt_t = jnp.transpose(running), jnp.transpose(dt)
        bc_rows = frame_of(bc, frame, rows, frames, columns)
        scores = jnp.where(causal, dot_nt(bc_rows[:, state:], bc_rows[:, :state]), 0.0)
        stored(reach, jnp.exp(running), frame, slice(None))
        for piece in range(groups):
            values = frame_x(x, piece, frame, rows, columns)
            mixed = head_mixes(
                scores, running, running_t, dt_t, values, piece * per_group, per_group, head_dim
            )
            stored(out, mixed.astype(BF16), frame, slice(piece * group, (piece + 1) * group))


def tail_of(decays):
    high = decays.astype(BF16)
    return jnp.concatenate([high, (decays - high.astype(F32)).astype(BF16)], axis=0)


def pair_kernel(frames, band, own, far, total):
    rows = (own.shape[0] - TAIL) // frames
    own_decay = own[-TAIL:-8, :].astype(F32) + own[-8:, :].astype(F32)
    far_decay = far[-TAIL:-8, :].astype(F32) + far[-8:, :].astype(F32)
    lower = band[0] % 2 == 0
    through = jnp.where(lower, far_decay, own_decay)
    for frame in range(frames):
        at = slice(frame * rows, (frame + 1) * rows)
        first = jnp.where(lower, own[at, :], far[at, :]).astype(F32)
        second = jnp.where(lower, far[at, :], own[at, :]).astype(F32)
        total[at, :] = (through[frame : frame + 1, :] * first + second).astype(BF16)
    total[frames * rows :, :] = tail_of(own_decay * far_decay)


def merge_kernel(frames, distance, finish, *refs):
    _, band, own, far = refs[:4]
    start = distance == 2
    rest = list(refs[4:])
    before_in = None if start else rest.pop(0)
    band_own, band_far = (rest.pop(0), rest.pop(0)) if finish else (None, None)
    rows = (own.shape[0] - TAIL) // frames
    upper, lower_band = (band[0] // distance) % 2 == 1, band[0] % 2 == 0
    own_decay = own[-TAIL:-8, :].astype(F32) + own[-8:, :].astype(F32)
    far_decay = far[-TAIL:-8, :].astype(F32) + far[-8:, :].astype(F32)
    if start:
        before_decay = jnp.ones_like(own_decay)
    else:
        before_decay = before_in[-8:, :]
    if finish:
        first_decay = jnp.where(
            lower_band,
            band_own[-TAIL:-8, :].astype(F32) + band_own[-8:, :].astype(F32),
            band_far[-TAIL:-8, :].astype(F32) + band_far[-8:, :].astype(F32),
        )
    through = jnp.where(upper, own_decay, far_decay)
    for frame in range(frames):
        at = slice(frame * rows, (frame + 1) * rows)
        row = slice(frame, frame + 1)
        far_state = far[at, :].astype(F32)
        came = before_decay[row, :] * far_state
        if not start:
            came = came + before_in[at, :]
        before = jnp.where(upper, came, 0.0 if start else before_in[at, :])
        if finish:
            keep, give = rest
            first = jnp.where(lower_band, band_own[at, :], band_far[at, :]).astype(F32)
            after = first_decay[row, :] * before + first
            keep[at, :] = jnp.where(lower_band, before, after).astype(BF16)
            give[at, :] = jnp.where(lower_band, after, before).astype(BF16)
        else:
            total, before_out = rest
            own_state = own[at, :].astype(F32)
            early = jnp.where(upper, far_state, own_state)
            late = jnp.where(upper, own_state, far_state)
            total[at, :] = (through[row, :] * early + late).astype(BF16)
            before_out[at, :] = before
    if not finish:
        total[frames * rows :, :] = tail_of(own_decay * far_decay)
        before_out[frames * rows :, :] = jnp.where(upper, before_decay * far_decay, before_decay)


def decays_of(ref):
    return ref[-TAIL:-8, :].astype(F32) + ref[-8:, :].astype(F32)


def places_of(band):
    return band % 2 == 0, (band // 2) % 2 == 1, band // 4 == 1


def cross_kernel(frames, _, band, total, first, near, far, message):
    even, x_high, y_high = places_of(band[0])
    own_decay, first_decay = decays_of(total), decays_of(first)
    diagonal = decays_of(near) * decays_of(far)
    one, zero = jnp.ones_like(own_decay), jnp.zeros_like(own_decay)
    odd_first = jnp.where(y_high, jnp.where(x_high, one, own_decay * diagonal), zero)
    odd_own = jnp.where(x_high & y_high, zero, one)
    of_first = jnp.where(even, jnp.where(x_high, own_decay, one), odd_first)
    of_own = jnp.where(even, jnp.where(x_high, one, first_decay), odd_own)
    rows = (total.shape[0] - TAIL) // frames
    for frame in range(frames):
        at, row = slice(frame * rows, (frame + 1) * rows), slice(frame, frame + 1)
        sent = of_first[row] * first[at, :].astype(F32) + of_own[row] * total[at, :].astype(F32)
        message[at, :] = sent.astype(BF16)
    message[frames * rows :, :] = tail_of(jnp.where(even, own_decay * first_decay, own_decay))


def settle_kernel(frames, _, band, first, second, near, far, band_own, band_far, keep, give):
    even, x_high, y_high = places_of(band[0])
    first_decay, second_decay = decays_of(first), decays_of(second)
    diagonal = decays_of(near) * decays_of(far)
    one, zero = jnp.ones_like(first_decay), jnp.zeros_like(first_decay)
    even_second = jnp.where(y_high, jnp.where(x_high, first_decay, one), zero)
    odd_second = jnp.where(x_high | y_high, one, zero)
    odd_first = jnp.where(y_high, jnp.where(x_high, second_decay, diagonal), zero)
    of_second = jnp.where(even, even_second, odd_second)
    of_first = jnp.where(even, jnp.where(x_high, one, zero), odd_first)
    band_decay = jnp.where(even, decays_of(band_own), decays_of(band_far))
    rows = keep.shape[0] // frames
    for frame in range(frames):
        at, row = slice(frame * rows, (frame + 1) * rows), slice(frame, frame + 1)
        before = of_second[row] * second[at, :].astype(F32) + of_first[row] * first[at, :].astype(F32)
        lower = jnp.where(even, band_own[at, :], band_far[at, :]).astype(F32)
        after = band_decay[row] * before + lower
        keep[at, :] = jnp.where(even, before, after).astype(BF16)
        give[at, :] = jnp.where(even, after, before).astype(BF16)


def incoming_kernel(frames, rows, columns, head_dim, band, out_local, bc, reach, own, other, out):
    state = bc.shape[1] // 2
    half = state // 2
    inner = out.shape[1]
    mine = band[0] % 2 == 0
    matrix = spread_matrix(0, inner, head_dim)
    for frame in range(frames):
        at = slice(frame * half, (frame + 1) * half)
        low = jnp.where(mine, own[at, :], other[at, :])
        high = jnp.where(mine, other[at, :], own[at, :])
        carried = jnp.concatenate([low, high], axis=0)
        for row in range(rows):
            to = (row * frames + frame) * columns
            here = slice(to, to + columns)
            factor = spread(reach[here, :], matrix)
            out[here, :] = out_local[here, :].astype(F32) + factor * dot(bc[here, state:], carried)


def temporal_kernel(
    part, parts, per_group, head_dim, rows, frames, columns, chunk_cols, shares, state, *refs
):
    here_ref, params, payload = refs[:3]
    rest = list(refs[3:])
    carried_in = rest.pop(0) if part > 0 else None
    del rest[:part]
    outs, rest = rest[:shares], rest[shares:]
    carried_out = rest.pop(0) if part + 1 < parts else None
    b_all, c_all, dt_all, decay_all = rest
    here = here_ref[0]
    length = frames * columns
    part_cols = columns // parts
    group = outs[0].shape[1]
    eye = (iota((TAIL, LANES), 0) == iota((TAIL, LANES), 1)) & (iota((TAIL, LANES), 1) < per_group)
    eye = eye.astype(BF16)

    def came(distance):
        return payload.at[rank_of(here ^ distance)]

    for distance in range(shares):
        b_proj, c_proj, logits = unpacked_rest(came(distance), length)
        logits = dot_tn(logits, eye)
        for frame in range(frames):
            at = slice(frame * columns + part * part_cols, frame * columns + (part + 1) * part_cols)
            to = slice(frame * part_cols, (frame + 1) * part_cols)
            b_all[distance, to] = b_proj[at]
            c_all[distance, to] = c_proj[at]
            dt = softplus(logits[at] + params[8:9, :])
            dt_all[distance, to] = dt
            decay_all[distance, to] = -dt * params[9:10, :]

    all_frames = shares * frames
    size = all_frames * chunk_cols

    def order_key(dim):
        index = iota((size, size), dim)
        source = here ^ (index // (frames * chunk_cols))
        frame = source * frames + (index // chunk_cols) % frames
        return (index % chunk_cols) * all_frames + frame

    causal = order_key(0) >= order_key(1)
    order = causal.astype(F32)
    matrix = spread_matrix(0, group, head_dim)
    carried = jnp.zeros((state, group), F32) if part == 0 else carried_in[...]
    places = [(source, frame) for source in range(shares) for frame in range(frames)]
    for chunk in range(part_cols // chunk_cols):

        def gathered(ref_of, pitch=part_cols, offset=0):
            return jnp.concatenate(
                [
                    ref_of(source)[pl.ds(frame * pitch + offset + chunk * chunk_cols, chunk_cols), :]
                    for source, frame in places
                ],
                axis=0,
            )

        values = gathered(came, columns, part * part_cols)
        b_proj = gathered(lambda source: b_all.at[source])
        c_proj = gathered(lambda source: c_all.at[source])
        dt = gathered(lambda source: dt_all.at[source])
        running = dot(order, gathered(lambda source: decay_all.at[source]), precision=EXACT)
        running_t, dt_t = jnp.transpose(running), jnp.transpose(dt)
        scores = jnp.where(causal, dot_nt(c_proj, b_proj), 0.0)
        last = jnp.min(running, axis=0, keepdims=True)
        mixed = head_mixes(scores, running, running_t, dt_t, values, 0, per_group, head_dim)
        ends = jnp.concatenate([running, jnp.broadcast_to(last, (8, LANES))], axis=0)
        to_end = jnp.exp(last - running) * dt
        factors = dot(jnp.concatenate([jnp.exp(ends), to_end], axis=0).astype(BF16), matrix)
        mixed = mixed + factors[:size] * dot(c_proj, carried.astype(BF16))
        scaled = (values.astype(F32) * factors[size + 8 :]).astype(BF16)
        carried = factors[size : size + 1, :] * carried + dot_tn(b_proj, scaled)
        mixed = mixed.astype(BF16)
        for index, (source, frame) in enumerate(places):
            to = frame * part_cols + chunk * chunk_cols
            outs[source][to : to + chunk_cols, :] = mixed[index * chunk_cols : (index + 1) * chunk_cols]
    if carried_out is not None:
        carried_out[...] = carried


def exit_kernel(part, parts, shares, *refs):
    here, spatial, gate, gain, weight = refs[:5]
    out, temporal, normed, mixed, sems = refs[-5:]
    frames, rows, columns, _ = out.shape
    part_cols = columns // parts
    _, part_len, group = temporal.shape
    groups = shares // rows
    inner = groups * group
    for index in range(shares):
        distance = (shares - index) % shares
        temporal[here[0] ^ distance] = refs[5 + index][...]

    def own(ref, row, at):
        return jnp.concatenate(
            [
                ref[pl.ds((row * frames + frame) * columns + part * part_cols, part_cols), at]
                for frame in range(frames)
            ],
            axis=0,
        )

    gains = gain[...].reshape(1, inner)
    for row in range(rows):
        total = jnp.zeros((part_len, 1), F32)
        kept = []
        for index in range(groups):
            at = slice(index * group, (index + 1) * group)
            gates = own(gate, row, at).astype(F32)
            gated = own(spatial, row, at) + temporal[index * rows + row].astype(F32)
            gated = gated * (gates / (1.0 + jnp.exp(-gates)))
            total = total + jnp.sum(gated * gated, axis=1, keepdims=True)
            kept.append(gated)
        scale = lax.rsqrt(total / inner + EPSILON)
        for index, gated in enumerate(kept):
            at = slice(index * group, (index + 1) * group)
            normed[row * part_len : (row + 1) * part_len, at] = (gated * scale * gains[:, at]).astype(BF16)
    mixed[...] = dot(normed[...], weight[...]).astype(BF16)
    copies = [
        pltpu.make_async_copy(
            mixed.at[pl.ds((row * frames + frame) * part_cols, part_cols), :],
            out.at[frame, row, pl.ds(part * part_cols, part_cols), :],
            sems.at[row * frames + frame],
        )
        for row in range(rows)
        for frame in range(frames)
    ]
    for copy in copies:
        copy.start()
    for copy in copies:
        copy.wait()


def swapped(value, axis, distance):
    count = lax.axis_size(axis)
    return lax.ppermute(value, axis, [(source, source ^ distance) for source in range(count)])


def crossed(value, axis, even, odd):
    count = lax.axis_size(axis)
    pairs = [(source, source ^ (odd if source % 2 else even)) for source in range(count)]
    return lax.ppermute(value, axis, pairs)


def per_device(
    tokens, norm_gain, in_weight, bc_weight, dt_weight, dt_bias, decay_rate, out_gain, out_weight
):
    frames, rows, columns, width = tokens.shape
    heads = decay_rate.shape[1]
    inner = out_weight.shape[0]
    head_dim = inner // heads
    state = bc_weight.shape[1] // 4
    shares = lax.axis_size("tm")
    bands = lax.axis_size("height")
    groups = shares // rows
    group = inner // groups
    per_group = heads // groups
    length = frames * columns
    count = rows * length
    half = state // 2
    chunk_cols = 16
    blocks = parts = 2
    part_len = length // parts
    here = lax.axis_index("tm").astype(jnp.int32).reshape(1)
    band = lax.axis_index("height").astype(jnp.int32).reshape(1)

    packed = (shares, sum(packing(length, group)), group)
    normed, payload, bc_own, logits, params, own, other, band_decays = call(
        functools.partial(entry_kernel, shares, heads, state, blocks),
        "entry",
        [
            shape_of((count, width), BF16),
            shape_of(packed, BF16),
            shape_of((count, 2 * state), BF16),
            shape_of((count, LANES), F32),
            shape_of((16, LANES), F32),
        ]
        + [shape_of((frames * half + TAIL, inner), BF16)] * 2
        + [shape_of((TAIL, inner), BF16)],
        [SCALAR, SCALAR, HBM, WHOLE, WHOLE, WHOLE, HBM, HBM, HBM],
        limit=LARGE,
        outs=[HBM, HBM] + [WHOLE] * 6,
        scratch_shapes=[
            pltpu.VMEM((rows, frames, columns, width), BF16),
            pltpu.VMEM((2 * heads, width), BF16),
            pltpu.VMEM((width, 4 * state), BF16),
            pltpu.VMEM((width, inner), BF16),
            pltpu.VMEM((8, LANES), F32),
            pltpu.VMEM((count, width), BF16),
            pltpu.VMEM(packed, BF16),
            pltpu.SemaphoreType.DMA((rows * frames + 2 + blocks,)),
            pltpu.SemaphoreType.DMA((1 + shares,)),
        ],
    )(here, band, tokens, norm_gain, dt_bias, decay_rate, dt_weight.T, bc_weight, in_weight)

    def sent(parts):
        moved = {d: swapped(parts[d], "tm", d) for d in range(shares - 1, 0, -1)}
        return [parts[0]] + list(moved.values())

    line = [rank_of(device) for device in range(shares)]
    received = lax.all_to_all(
        payload,
        "tm",
        split_axis=0,
        concat_axis=0,
        tiled=True,
        axis_index_groups=[[line.index(rank) for rank in range(shares)]],
    )
    far = swapped(other, "height", 1)
    gate = call(
        functools.partial(gate_kernel, blocks),
        "gate",
        shape_of((count, inner), BF16),
        [ANY, WHOLE, HBM],
        scratch_shapes=[
            pltpu.VMEM((width, inner), BF16),
            pltpu.SemaphoreType.DMA((blocks,)),
        ],
    )(payload, normed, in_weight)

    out_local, reach = call(
        functools.partial(local_kernel, frames, rows, columns, head_dim, groups),
        "spatial_local",
        [shape_of((count, inner), BF16), shape_of((count, LANES), F32)],
        [ANY] + [WHOLE] * 4,
    )(gate, bc_own, logits, params, payload)

    total = call(
        functools.partial(pair_kernel, frames),
        "pair_total",
        shape_of((frames * half + TAIL, inner), BF16),
        [SCALAR, WHOLE, WHOLE],
    )(band, own, far)
    before = []
    distance = 2
    if bands == 8:
        near, far_decays = (swapped(band_decays, "height", distance) for distance in (6, 7))
        first = crossed(total, "height", 2, 4)
        message = call(
            functools.partial(cross_kernel, frames),
            "cross",
            shape_of((frames * half + TAIL, inner), BF16),
            [ANY, SCALAR] + [WHOLE] * 4,
        )(reach, band, total, first, near, far_decays)
        second = crossed(message, "height", 4, 2)
        results = call(
            functools.partial(settle_kernel, frames),
            "settle",
            [shape_of((frames * half, inner), BF16)] * 2,
            [ANY, SCALAR] + [WHOLE] * 6,
        )(reach, band, first, second, near, far_decays, own, far)
        distance = bands
    while distance < bands:
        far_total = swapped(total, "height", distance)
        finish = distance * 2 >= bands
        operands = [reach, band, total, far_total] + before + ([own, far] if finish else [])
        outs = (
            [shape_of((frames * half, inner), BF16)] * 2
            if finish
            else [
                shape_of((frames * half + TAIL, inner), BF16),
                shape_of((frames * half + 8, inner), F32),
            ]
        )
        results = call(
            functools.partial(merge_kernel, frames, distance, finish),
            "merge",
            outs,
            [ANY, SCALAR] + [WHOLE] * (len(operands) - 2),
        )(*operands)
        if not finish:
            total, before = results[0], [results[1]]
        distance *= 2
    keep, give = results
    came = swapped(give, "height", 1)

    spatial_out = call(
        functools.partial(incoming_kernel, frames, rows, columns, head_dim),
        "spatial_incoming",
        shape_of((count, inner), F32),
        [SCALAR] + [WHOLE] * 5,
    )(band, out_local, bc_own, reach, keep, came)

    returned, carried = [], []
    for part in range(parts):
        more = [shape_of((state, group), F32)] if part + 1 < parts else []
        results = call(
            functools.partial(
                temporal_kernel,
                part,
                parts,
                per_group,
                head_dim,
                rows,
                frames,
                columns,
                chunk_cols,
                shares,
                state,
            ),
            "temporal",
            [shape_of((part_len, group), BF16)] * shares + more,
            [SCALAR] + [WHOLE] * (2 + len(carried)) + [ANY] * part,
            scratch_shapes=[
                pltpu.VMEM((shares, part_len, state), BF16),
                pltpu.VMEM((shares, part_len, state), BF16),
                pltpu.VMEM((shares, part_len, LANES), F32),
                pltpu.VMEM((shares, part_len, LANES), F32),
            ],
        )(here, params, received, *carried, *([spatial_out] * part))
        returned.append(sent(results[:shares]))
        carried = results[shares:]

    mixed = []
    for part in range(parts):
        mixed = [
            call(
                functools.partial(exit_kernel, part, parts, shares),
                "exit",
                shape_of(tokens.shape, BF16),
                [SCALAR] + [WHOLE] * (4 + shares) + [HBM] * len(mixed),
                outs=HBM,
                scratch_shapes=[
                    pltpu.VMEM((shares, part_len, group), BF16),
                    pltpu.VMEM((rows * part_len, inner), BF16),
                    pltpu.VMEM((rows * part_len, width), BF16),
                    pltpu.SemaphoreType.DMA((rows * frames,)),
                ],
                input_output_aliases={5 + shares: 0} if mixed else {},
            )(here, spatial_out, gate, out_gain, out_weight, *returned[part], *mixed)
        ]
    return mixed[0]


def solution(mesh):
    in_specs = (P("tm", "height", None, None), P(), P(), P(), P(), P(), P(), P(), P())
    out_specs = P("tm", "height", None, None)
    return jax.shard_map(
        per_device, mesh=mesh, in_specs=in_specs, out_specs=out_specs, check_vma=False
    )
```

```python
import functools
import math

import jax
import jax.numpy as jnp
from jax import lax
from jax.experimental import pallas as pl
from jax.experimental.pallas import tpu as pltpu
from jax.sharding import PartitionSpec as P

EPSILON = 1e-05
LANES = 128
TAIL = 16
LOG2_E = 1.4426950408889634
F32 = jnp.float32
BF16 = jnp.bfloat16
EXACT = lax.Precision.HIGHEST
LARGE = 56 * 1024 * 1024
SMALL = 24 * 1024 * 1024

ANY = pl.BlockSpec(memory_space=pl.ANY)
HBM = pl.BlockSpec(memory_space=pltpu.HBM)
SCALAR = pl.BlockSpec(memory_space=pltpu.SMEM)
WHOLE = pl.BlockSpec(memory_space=pltpu.VMEM)


def call(kernel, name, out_shape, in_specs, limit=SMALL, outs=None, **options):
    return pl.pallas_call(
        kernel,
        out_shape=out_shape,
        in_specs=in_specs,
        out_specs=jax.tree.map(lambda _: WHOLE, out_shape) if outs is None else outs,
        compiler_params=pltpu.CompilerParams(vmem_limit_bytes=limit),
        cost_estimate=pl.CostEstimate(flops=1, bytes_accessed=1, transcendentals=0),
        name=name,
        **options,
    )


def shape_of(shape, dtype):
    return jax.ShapeDtypeStruct(shape, dtype)


def dot(left, right, **options):
    return jnp.dot(left, right, preferred_element_type=F32, **options)


def dot_tn(left, right):
    return lax.dot_general(left, right, (((0,), (0,)), ((), ())), preferred_element_type=F32)


def dot_nt(left, right):
    return lax.dot_general(left, right, (((1,), (1,)), ((), ())), preferred_element_type=F32)


def softplus(values):
    return jnp.maximum(values, 0.0) + jnp.log1p(jnp.exp(-jnp.abs(values)))


def iota(shape, dim):
    return lax.broadcasted_iota(jnp.int32, shape, dim)


def spread_matrix(first_head, width, head_dim):
    return (iota((LANES, width), 0) - first_head == iota((LANES, width), 1) // head_dim).astype(BF16)


def spread(values, matrix):
    high = values.astype(BF16)
    low = (values - high.astype(F32)).astype(BF16)
    return dot(high, matrix) + dot(low, matrix)


def head_mixes(scores, running, running_t, dt_t, x, first_head, heads, head_dim):
    length = scores.shape[0]
    running, running_t = running * LOG2_E, running_t * LOG2_E
    outs = []

    def weights(head):
        spreads = running[:, head : head + 1] - running_t[head : head + 1, :]
        return (scores * jnp.exp2(jnp.minimum(spreads, 0.0)) * dt_t[head : head + 1, :]).astype(BF16)

    head = 0
    while head < heads:
        here = first_head + head
        if head + 1 < heads and 2 * head_dim == LANES:
            both = x[:, head * head_dim : (head + 2) * head_dim]
            first = iota((length, LANES), 1) < head_dim
            zero = jnp.zeros_like(both)
            stacked = jnp.concatenate([jnp.where(first, both, zero), jnp.where(first, zero, both)], axis=0)
            pair = jnp.concatenate([weights(here), weights(here + 1)], axis=1)
            outs.append(dot(pair, stacked))
            head += 2
        else:
            outs.append(dot(weights(here), x[:, head * head_dim : (head + 1) * head_dim]))
            head += 1
    return outs[0] if len(outs) == 1 else jnp.concatenate(outs, axis=1)


def column_copies(weight, scratch, sems, first, offset, blocks):
    width = scratch.shape[1] // blocks
    return [
        pltpu.make_async_copy(
            weight.at[:, pl.ds(offset + index * width, width)],
            scratch.at[:, pl.ds(index * width, width)],
            sems.at[first + index],
        )
        for index in range(blocks)
    ]


def rank_of(device, shares):
    code = device ^ (device >> 1)
    return (shares - code) % shares if isinstance(device, int) else lax.rem(shares - code, shares)


def packing(length, group):
    columns = group // LANES
    rest = -(-(2 * length + TAIL) // columns)
    return length, -(-rest // TAIL) * TAIL


def pack_rest(ref, length, b_proj, c_proj, dt):
    columns, rest = ref.shape[1] // LANES, ref.shape[0] - length
    blank = jnp.zeros((columns * rest - 2 * length - TAIL, LANES), BF16)
    stacked = jnp.concatenate([b_proj, c_proj, dt, blank], axis=0)
    for column in range(columns):
        ref[length:, column * LANES : (column + 1) * LANES] = stacked[column * rest : (column + 1) * rest]


def unpacked_rest(ref, length):
    columns = ref.shape[1] // LANES
    stacked = jnp.concatenate(
        [ref[length:, column * LANES : (column + 1) * LANES] for column in range(columns)], axis=0
    )
    return stacked[:length], stacked[length : 2 * length], stacked[2 * length : 2 * length + TAIL]


def entry_kernel(shares, heads, state, blocks, *refs):
    here_ref, band, tokens, gain, bias, rates, dt_weight, bc_weight, weight = refs[:9]
    normed_out, payload_out, bc_own, logits, params, own_states, other_states, band_decays = refs[9:17]
    held, dt_held, bc_held, held_weight, table, normed, payload, sems, out_sems = refs[17:]
    frames, rows, columns, width = tokens.shape
    length = frames * columns
    count = rows * length
    groups = shares // rows
    per_group = heads // groups
    group = held_weight.shape[1] // groups

    token_copies = [
        pltpu.make_async_copy(tokens.at[frame, row], held.at[row, frame], sems.at[row * frames + frame])
        for row in range(rows)
        for frame in range(frames)
    ]
    for copy in token_copies:
        copy.start()
    first = rows * frames
    dt_copy = pltpu.make_async_copy(dt_weight, dt_held, sems.at[first])
    dt_copy.start()
    bc_copy = pltpu.make_async_copy(bc_weight, bc_held, sems.at[first + 1])
    bc_copy.start()
    copies = column_copies(weight, held_weight, sems, first + 2, 0, blocks)
    for copy in copies:
        copy.start()

    table[...] = jnp.zeros_like(table)
    table[0:1, : 2 * heads] = bias[...].reshape(1, 2 * heads)
    table[1:2, :heads] = rates[0:1, :]
    table[1:2, heads : 2 * heads] = rates[1:2, :]
    first_head = heads + here_ref[0] // rows * per_group
    lane_in, lane_out = iota((LANES, LANES), 0), iota((LANES, LANES), 1)
    own = ((lane_in == lane_out + first_head) & (lane_out < per_group)).astype(F32)
    params[0:8, :] = table[...]
    params[8:16, :] = dot(table[...], own, precision=EXACT)
    logits[...] = jnp.zeros_like(logits)

    gains = gain[...].reshape(1, width)
    for index, copy in enumerate(token_copies):
        copy.wait()
        values = held[index // frames, index % frames].astype(F32)
        mean_square = jnp.mean(values * values, axis=-1, keepdims=True)
        normed[index * columns : (index + 1) * columns, :] = (
            values * lax.rsqrt(mean_square + EPSILON) * gains
        ).astype(BF16)
    outgoing = [pltpu.make_async_copy(normed, normed_out, out_sems.at[0])]
    outgoing[0].start()
    dt_copy.wait()
    logits[:, : 2 * heads] = dot_nt(normed[...], dt_held[...]).astype(BF16).astype(F32)
    dt_heads = jnp.transpose(logits[...]).astype(BF16)[heads : 2 * heads + TAIL]
    bc_copy.wait()
    bc = dot(normed[...], bc_held[...]).astype(BF16)
    bc_own[...] = bc[:, : 2 * state]
    scan = [
        end_factors(frame_of(logits, frame, rows, frames, columns), params, rows * columns)
        for frame in range(frames)
    ]

    block = held_weight.shape[1] // blocks
    for index, copy in enumerate(copies):
        copy.wait()
        at = index * block
        values = dot(normed[...], held_weight[:, at : at + block]).astype(BF16)
        for inside in range(0, block, group):
            part = (at + inside) // group
            for row in range(rows):
                piece = rank_of(part * rows + row, shares)
                here = slice(row * length, (row + 1) * length)
                payload[piece, :length, :] = values[here, inside : inside + group]
                pack_rest(
                    payload.at[piece],
                    length,
                    bc[here, 2 * state : 3 * state],
                    bc[here, 3 * state :],
                    dt_heads[part * per_group : part * per_group + TAIL, here],
                )
                outgoing.append(
                    pltpu.make_async_copy(
                        payload.at[piece], payload_out.at[piece], out_sems.at[1 + piece]
                    )
                )
                outgoing[-1].start()
    half = state // 2
    head_dim = groups * group // heads
    mine = band[0] % 2 == 0
    matrix = spread_matrix(0, groups * group, head_dim)
    factors = dot(jnp.concatenate([factor for factor, _ in scan], axis=0), matrix)
    span = rows * columns
    for frame in range(frames):
        b_proj = frame_of(bc_own, frame, rows, frames, columns)[:, :state]
        values = jnp.concatenate(
            [frame_x(payload, part, frame, rows, columns) for part in range(groups)], axis=1
        )
        scaled = (values.astype(F32) * factors[frame * span : (frame + 1) * span]).astype(BF16)
        fresh = dot_tn(b_proj, scaled).astype(BF16)
        at_rows = slice(frame * half, (frame + 1) * half)
        own_states[at_rows, :] = jnp.where(mine, fresh[:half], fresh[half:])
        other_states[at_rows, :] = jnp.where(mine, fresh[half:], fresh[:half])
    whole = [decay for _, decay in scan] + [jnp.zeros((8 - frames, LANES), F32)]
    decays = spread(jnp.concatenate(whole, axis=0), matrix)
    tail = tail_of(decays)
    own_states[frames * half :, :] = tail
    other_states[frames * half :, :] = tail
    band_decays[...] = tail
    for copy in outgoing:
        copy.wait()


def gate_kernel(blocks, after, normed, weight, out, held_weight, sems):
    inner = held_weight.shape[1]
    copies = column_copies(weight, held_weight, sems, 0, inner, blocks)
    for copy in copies:
        copy.start()
    block = inner // blocks
    for index, copy in enumerate(copies):
        copy.wait()
        at = slice(index * block, (index + 1) * block)
        out[:, at] = dot(normed[...], held_weight[:, at]).astype(BF16)


def frame_of(ref, frame, rows, frames, columns):
    return jnp.concatenate(
        [
            ref[(row * frames + frame) * columns : (row * frames + frame + 1) * columns, :]
            for row in range(rows)
        ],
        axis=0,
    )


def frame_x(payload, part, frame, rows, columns):
    shares = payload.shape[0]
    return jnp.concatenate(
        [
            payload[rank_of(part * rows + row, shares), frame * columns : (frame + 1) * columns, :]
            for row in range(rows)
        ],
        axis=0,
    )


def scan_terms(logits, params, causal):
    dt = softplus(logits + params[0:1, :])
    running = dot(causal.astype(F32), -dt * params[1:2, :], precision=EXACT)
    return dt, running, jnp.min(running, axis=0, keepdims=True)


def end_factors(logits, params, length):
    causal = iota((length, length), 0) >= iota((length, length), 1)
    dt, running, last = scan_terms(logits, params, causal)
    return (jnp.exp(last - running) * dt).astype(BF16), jnp.exp(last)


def local_kernel(frames, rows, columns, head_dim, groups, *refs):
    after, bc, logits, params, x, out, reach, done = refs
    done[...] = jnp.zeros_like(done)
    length = rows * columns
    group = x.shape[2]
    state = bc.shape[1] // 2
    per_group = group // head_dim
    causal = iota((length, length), 0) >= iota((length, length), 1)

    def stored(ref, values, frame, at):
        for row in range(rows):
            to = (row * frames + frame) * columns
            ref[to : to + columns, at] = values[row * columns : (row + 1) * columns]

    for frame in range(frames):
        dt, running, _ = scan_terms(frame_of(logits, frame, rows, frames, columns), params, causal)
        running_t, dt_t = jnp.transpose(running), jnp.transpose(dt)
        bc_rows = frame_of(bc, frame, rows, frames, columns)
        scores = jnp.where(causal, dot_nt(bc_rows[:, state:], bc_rows[:, :state]), 0.0)
        stored(reach, jnp.exp(running), frame, slice(None))
        for piece in range(groups):
            values = frame_x(x, piece, frame, rows, columns)
            mixed = head_mixes(
                scores, running, running_t, dt_t, values, piece * per_group, per_group, head_dim
            )
            stored(out, mixed.astype(BF16), frame, slice(piece * group, (piece + 1) * group))


def tail_of(decays):
    high = decays.astype(BF16)
    return jnp.concatenate([high, (decays - high.astype(F32)).astype(BF16)], axis=0)


def pair_kernel(frames, band, own, far, total):
    rows = (own.shape[0] - TAIL) // frames
    own_decay = own[-TAIL:-8, :].astype(F32) + own[-8:, :].astype(F32)
    far_decay = far[-TAIL:-8, :].astype(F32) + far[-8:, :].astype(F32)
    lower = band[0] % 2 == 0
    through = jnp.where(lower, far_decay, own_decay)
    for frame in range(frames):
        at = slice(frame * rows, (frame + 1) * rows)
        first = jnp.where(lower, own[at, :], far[at, :]).astype(F32)
        second = jnp.where(lower, far[at, :], own[at, :]).astype(F32)
        total[at, :] = (through[frame : frame + 1, :] * first + second).astype(BF16)
    total[frames * rows :, :] = tail_of(own_decay * far_decay)


def merge_kernel(frames, distance, finish, *refs):
    _, band, own, far = refs[:4]
    start = distance == 2
    rest = list(refs[4:])
    before_in = None if start else rest.pop(0)
    band_own, band_far = (rest.pop(0), rest.pop(0)) if finish else (None, None)
    rows = (own.shape[0] - TAIL) // frames
    upper, lower_band = (band[0] // distance) % 2 == 1, band[0] % 2 == 0
    own_decay = own[-TAIL:-8, :].astype(F32) + own[-8:, :].astype(F32)
    far_decay = far[-TAIL:-8, :].astype(F32) + far[-8:, :].astype(F32)
    if start:
        before_decay = jnp.ones_like(own_decay)
    else:
        before_decay = before_in[-8:, :]
    if finish:
        first_decay = jnp.where(
            lower_band,
            band_own[-TAIL:-8, :].astype(F32) + band_own[-8:, :].astype(F32),
            band_far[-TAIL:-8, :].astype(F32) + band_far[-8:, :].astype(F32),
        )
    through = jnp.where(upper, own_decay, far_decay)
    for frame in range(frames):
        at = slice(frame * rows, (frame + 1) * rows)
        row = slice(frame, frame + 1)
        far_state = far[at, :].astype(F32)
        came = before_decay[row, :] * far_state
        if not start:
            came = came + before_in[at, :]
        before = jnp.where(upper, came, 0.0 if start else before_in[at, :])
        if finish:
            keep, give = rest
            first = jnp.where(lower_band, band_own[at, :], band_far[at, :]).astype(F32)
            after = first_decay[row, :] * before + first
            keep[at, :] = jnp.where(lower_band, before, after).astype(BF16)
            give[at, :] = jnp.where(lower_band, after, before).astype(BF16)
        else:
            total, before_out = rest
            own_state = own[at, :].astype(F32)
            early = jnp.where(upper, far_state, own_state)
            late = jnp.where(upper, own_state, far_state)
            total[at, :] = (through[row, :] * early + late).astype(BF16)
            before_out[at, :] = before
    if not finish:
        total[frames * rows :, :] = tail_of(own_decay * far_decay)
        before_out[frames * rows :, :] = jnp.where(upper, before_decay * far_decay, before_decay)


def decays_of(ref):
    return ref[-TAIL:-8, :].astype(F32) + ref[-8:, :].astype(F32)


def places_of(band):
    return band % 2 == 0, (band // 2) % 2 == 1, band // 4 == 1


def cross_kernel(frames, _, band, total, first, near, far, message):
    even, x_high, y_high = places_of(band[0])
    own_decay, first_decay = decays_of(total), decays_of(first)
    diagonal = decays_of(near) * decays_of(far)
    one, zero = jnp.ones_like(own_decay), jnp.zeros_like(own_decay)
    odd_first = jnp.where(y_high, jnp.where(x_high, one, own_decay * diagonal), zero)
    odd_own = jnp.where(x_high & y_high, zero, one)
    of_first = jnp.where(even, jnp.where(x_high, own_decay, one), odd_first)
    of_own = jnp.where(even, jnp.where(x_high, one, first_decay), odd_own)
    rows = (total.shape[0] - TAIL) // frames
    for frame in range(frames):
        at, row = slice(frame * rows, (frame + 1) * rows), slice(frame, frame + 1)
        sent = of_first[row] * first[at, :].astype(F32) + of_own[row] * total[at, :].astype(F32)
        message[at, :] = sent.astype(BF16)
    message[frames * rows :, :] = tail_of(jnp.where(even, own_decay * first_decay, own_decay))


def settle_kernel(frames, _, band, first, second, near, far, band_own, band_far, keep, give):
    even, x_high, y_high = places_of(band[0])
    first_decay, second_decay = decays_of(first), decays_of(second)
    diagonal = decays_of(near) * decays_of(far)
    one, zero = jnp.ones_like(first_decay), jnp.zeros_like(first_decay)
    even_second = jnp.where(y_high, jnp.where(x_high, first_decay, one), zero)
    odd_second = jnp.where(x_high | y_high, one, zero)
    odd_first = jnp.where(y_high, jnp.where(x_high, second_decay, diagonal), zero)
    of_second = jnp.where(even, even_second, odd_second)
    of_first = jnp.where(even, jnp.where(x_high, one, zero), odd_first)
    band_decay = jnp.where(even, decays_of(band_own), decays_of(band_far))
    rows = keep.shape[0] // frames
    for frame in range(frames):
        at, row = slice(frame * rows, (frame + 1) * rows), slice(frame, frame + 1)
        before = of_second[row] * second[at, :].astype(F32) + of_first[row] * first[at, :].astype(F32)
        lower = jnp.where(even, band_own[at, :], band_far[at, :]).astype(F32)
        after = band_decay[row] * before + lower
        keep[at, :] = jnp.where(even, before, after).astype(BF16)
        give[at, :] = jnp.where(even, after, before).astype(BF16)


def incoming_kernel(frames, rows, columns, head_dim, band, out_local, bc, reach, own, other, out):
    state = bc.shape[1] // 2
    half = state // 2
    inner = out.shape[1]
    mine = band[0] % 2 == 0
    matrix = spread_matrix(0, inner, head_dim)
    for frame in range(frames):
        at = slice(frame * half, (frame + 1) * half)
        low = jnp.where(mine, own[at, :], other[at, :])
        high = jnp.where(mine, other[at, :], own[at, :])
        carried = jnp.concatenate([low, high], axis=0)
        for row in range(rows):
            to = (row * frames + frame) * columns
            here = slice(to, to + columns)
            factor = spread(reach[here, :], matrix)
            out[here, :] = out_local[here, :].astype(F32) + factor * dot(bc[here, state:], carried)


def temporal_kernel(
    part, parts, per_group, head_dim, rows, frames, columns, chunk_cols, shares, state, *refs
):
    here_ref, params, payload = refs[:3]
    rest = list(refs[3:])
    carried_in = rest.pop(0) if part > 0 else None
    del rest[:part]
    outs, rest = rest[:shares], rest[shares:]
    carried_out = rest.pop(0) if part + 1 < parts else None
    b_all, c_all, dt_all, decay_all = rest
    here = here_ref[0]
    length = frames * columns
    part_cols = columns // parts
    group = outs[0].shape[1]
    eye = (iota((TAIL, LANES), 0) == iota((TAIL, LANES), 1)) & (iota((TAIL, LANES), 1) < per_group)
    eye = eye.astype(BF16)

    def came(distance):
        return payload.at[rank_of(here ^ distance, shares)]

    for distance in range(shares):
        b_proj, c_proj, logits = unpacked_rest(came(distance), length)
        logits = dot_tn(logits, eye)
        for frame in range(frames):
            at = slice(frame * columns + part * part_cols, frame * columns + (part + 1) * part_cols)
            to = slice(frame * part_cols, (frame + 1) * part_cols)
            b_all[distance, to] = b_proj[at]
            c_all[distance, to] = c_proj[at]
            dt = softplus(logits[at] + params[8:9, :])
            dt_all[distance, to] = dt
            decay_all[distance, to] = -dt * params[9:10, :]

    all_frames = shares * frames
    size = all_frames * chunk_cols

    def order_key(dim):
        index = iota((size, size), dim)
        source = here ^ (index // (frames * chunk_cols))
        frame = source * frames + (index // chunk_cols) % frames
        return (index % chunk_cols) * all_frames + frame

    causal = order_key(0) >= order_key(1)
    order = causal.astype(F32)
    matrix = spread_matrix(0, group, head_dim)
    carried = jnp.zeros((state, group), F32) if part == 0 else carried_in[...]
    places = [(source, frame) for source in range(shares) for frame in range(frames)]
    for chunk in range(part_cols // chunk_cols):

        def gathered(ref_of, pitch=part_cols, offset=0):
            return jnp.concatenate(
                [
                    ref_of(source)[pl.ds(frame * pitch + offset + chunk * chunk_cols, chunk_cols), :]
                    for source, frame in places
                ],
                axis=0,
            )

        values = gathered(came, columns, part * part_cols)
        b_proj = gathered(lambda source: b_all.at[source])
        c_proj = gathered(lambda source: c_all.at[source])
        dt = gathered(lambda source: dt_all.at[source])
        running = dot(order, gathered(lambda source: decay_all.at[source]), precision=EXACT)
        running_t, dt_t = jnp.transpose(running), jnp.transpose(dt)
        scores = jnp.where(causal, dot_nt(c_proj, b_proj), 0.0)
        last = jnp.min(running, axis=0, keepdims=True)
        mixed = head_mixes(scores, running, running_t, dt_t, values, 0, per_group, head_dim)
        ends = jnp.concatenate([running, jnp.broadcast_to(last, (8, LANES))], axis=0)
        to_end = jnp.exp(last - running) * dt
        factors = dot(jnp.concatenate([jnp.exp(ends), to_end], axis=0).astype(BF16), matrix)
        mixed = mixed + factors[:size] * dot(c_proj, carried.astype(BF16))
        scaled = (values.astype(F32) * factors[size + 8 :]).astype(BF16)
        carried = factors[size : size + 1, :] * carried + dot_tn(b_proj, scaled)
        mixed = mixed.astype(BF16)
        for index, (source, frame) in enumerate(places):
            to = frame * part_cols + chunk * chunk_cols
            outs[source][to : to + chunk_cols, :] = mixed[index * chunk_cols : (index + 1) * chunk_cols]
    if carried_out is not None:
        carried_out[...] = carried


def exit_kernel(part, parts, shares, *refs):
    here, spatial, gate, gain, weight = refs[:5]
    out, temporal, normed, mixed, sems = refs[-5:]
    frames, rows, columns, _ = out.shape
    part_cols = columns // parts
    _, part_len, group = temporal.shape
    groups = shares // rows
    inner = groups * group
    for index in range(shares):
        distance = (shares - index) % shares
        temporal[here[0] ^ distance] = refs[5 + index][...]

    def own(ref, row, at):
        return jnp.concatenate(
            [
                ref[pl.ds((row * frames + frame) * columns + part * part_cols, part_cols), at]
                for frame in range(frames)
            ],
            axis=0,
        )

    gains = gain[...].reshape(1, inner)
    for row in range(rows):
        total = jnp.zeros((part_len, 1), F32)
        kept = []
        for index in range(groups):
            at = slice(index * group, (index + 1) * group)
            gates = own(gate, row, at).astype(F32)
            gated = own(spatial, row, at) + temporal[index * rows + row].astype(F32)
            gated = gated * (gates / (1.0 + jnp.exp(-gates)))
            total = total + jnp.sum(gated * gated, axis=1, keepdims=True)
            kept.append(gated)
        scale = lax.rsqrt(total / inner + EPSILON)
        for index, gated in enumerate(kept):
            at = slice(index * group, (index + 1) * group)
            normed[row * part_len : (row + 1) * part_len, at] = (gated * scale * gains[:, at]).astype(BF16)
    mixed[...] = dot(normed[...], weight[...]).astype(BF16)
    copies = [
        pltpu.make_async_copy(
            mixed.at[pl.ds((row * frames + frame) * part_cols, part_cols), :],
            out.at[frame, row, pl.ds(part * part_cols, part_cols), :],
            sems.at[row * frames + frame],
        )
        for row in range(rows)
        for frame in range(frames)
    ]
    for copy in copies:
        copy.start()
    for copy in copies:
        copy.wait()


def swapped(value, axis, distance):
    count = lax.axis_size(axis)
    return lax.ppermute(value, axis, [(source, source ^ distance) for source in range(count)])


def crossed(value, axis, even, odd):
    count = lax.axis_size(axis)
    pairs = [(source, source ^ (odd if source % 2 else even)) for source in range(count)]
    return lax.ppermute(value, axis, pairs)


def per_device(
    tokens, norm_gain, in_weight, bc_weight, dt_weight, dt_bias, decay_rate, out_gain, out_weight
):
    frames, rows, columns, width = tokens.shape
    heads = decay_rate.shape[1]
    inner = out_weight.shape[0]
    head_dim = inner // heads
    state = bc_weight.shape[1] // 4
    shares = lax.axis_size("tm")
    bands = lax.axis_size("height")
    groups = shares // rows
    group = inner // groups
    per_group = heads // groups
    length = frames * columns
    count = rows * length
    half = state // 2
    chunk_cols = 16
    blocks = parts = 2
    part_len = length // parts
    here = lax.axis_index("tm").astype(jnp.int32).reshape(1)
    band = lax.axis_index("height").astype(jnp.int32).reshape(1)

    packed = (shares, sum(packing(length, group)), group)
    normed, payload, bc_own, logits, params, own, other, band_decays = call(
        functools.partial(entry_kernel, shares, heads, state, blocks),
        "entry",
        [
            shape_of((count, width), BF16),
            shape_of(packed, BF16),
            shape_of((count, 2 * state), BF16),
            shape_of((count, LANES), F32),
            shape_of((16, LANES), F32),
        ]
        + [shape_of((frames * half + TAIL, inner), BF16)] * 2
        + [shape_of((TAIL, inner), BF16)],
        [SCALAR, SCALAR, HBM, WHOLE, WHOLE, WHOLE, HBM, HBM, HBM],
        limit=LARGE,
        outs=[HBM, HBM] + [WHOLE] * 6,
        scratch_shapes=[
            pltpu.VMEM((rows, frames, columns, width), BF16),
            pltpu.VMEM((2 * heads, width), BF16),
            pltpu.VMEM((width, 4 * state), BF16),
            pltpu.VMEM((width, inner), BF16),
            pltpu.VMEM((8, LANES), F32),
            pltpu.VMEM((count, width), BF16),
            pltpu.VMEM(packed, BF16),
            pltpu.SemaphoreType.DMA((rows * frames + 2 + blocks,)),
            pltpu.SemaphoreType.DMA((1 + shares,)),
        ],
    )(here, band, tokens, norm_gain, dt_bias, decay_rate, dt_weight.T, bc_weight, in_weight)

    def sent(parts):
        moved = {d: swapped(parts[d], "tm", d) for d in range(shares - 1, 0, -1)}
        return [parts[0]] + list(moved.values())

    line = [rank_of(device, shares) for device in range(shares)]
    received = lax.all_to_all(
        payload,
        "tm",
        split_axis=0,
        concat_axis=0,
        tiled=True,
        axis_index_groups=[[line.index(rank) for rank in range(shares)]],
    )
    far = swapped(other, "height", 1)
    gate = call(
        functools.partial(gate_kernel, blocks),
        "gate",
        shape_of((count, inner), BF16),
        [ANY, WHOLE, HBM],
        scratch_shapes=[
            pltpu.VMEM((width, inner), BF16),
            pltpu.SemaphoreType.DMA((blocks,)),
        ],
    )(payload, normed, in_weight)

    out_local, reach, done = call(
        functools.partial(local_kernel, frames, rows, columns, head_dim, groups),
        "spatial_local",
        [shape_of((count, inner), BF16), shape_of((count, LANES), F32), shape_of((8, LANES), F32)],
        [ANY] + [WHOLE] * 4,
    )(gate, bc_own, logits, params, payload)

    total = call(
        functools.partial(pair_kernel, frames),
        "pair_total",
        shape_of((frames * half + TAIL, inner), BF16),
        [SCALAR, WHOLE, WHOLE],
    )(band, own, far)
    before = []
    distance = 2
    if bands == 8:
        near, far_decays = (swapped(band_decays, "height", distance) for distance in (6, 7))
        first = crossed(total, "height", 2, 4)
        message = call(
            functools.partial(cross_kernel, frames),
            "cross",
            shape_of((frames * half + TAIL, inner), BF16),
            [ANY, SCALAR] + [WHOLE] * 4,
        )(done, band, total, first, near, far_decays)
        second = crossed(message, "height", 4, 2)
        results = call(
            functools.partial(settle_kernel, frames),
            "settle",
            [shape_of((frames * half, inner), BF16)] * 2,
            [ANY, SCALAR] + [WHOLE] * 6,
        )(done, band, first, second, near, far_decays, own, far)
        distance = bands
    while distance < bands:
        far_total = swapped(total, "height", distance)
        finish = distance * 2 >= bands
        operands = [done, band, total, far_total] + before + ([own, far] if finish else [])
        outs = (
            [shape_of((frames * half, inner), BF16)] * 2
            if finish
            else [
                shape_of((frames * half + TAIL, inner), BF16),
                shape_of((frames * half + 8, inner), F32),
            ]
        )
        results = call(
            functools.partial(merge_kernel, frames, distance, finish),
            "merge",
            outs,
            [ANY, SCALAR] + [WHOLE] * (len(operands) - 2),
        )(*operands)
        if not finish:
            total, before = results[0], [results[1]]
        distance *= 2
    keep, give = results
    came = swapped(give, "height", 1)

    spatial_out = call(
        functools.partial(incoming_kernel, frames, rows, columns, head_dim),
        "spatial_incoming",
        shape_of((count, inner), F32),
        [SCALAR] + [WHOLE] * 5,
    )(band, out_local, bc_own, reach, keep, came)

    returned, carried = [], []
    for part in range(parts):
        more = [shape_of((state, group), F32)] if part + 1 < parts else []
        results = call(
            functools.partial(
                temporal_kernel,
                part,
                parts,
                per_group,
                head_dim,
                rows,
                frames,
                columns,
                chunk_cols,
                shares,
                state,
            ),
            "temporal",
            [shape_of((part_len, group), BF16)] * shares + more,
            [SCALAR] + [WHOLE] * (2 + len(carried)) + [ANY] * part,
            scratch_shapes=[
                pltpu.VMEM((shares, part_len, state), BF16),
                pltpu.VMEM((shares, part_len, state), BF16),
                pltpu.VMEM((shares, part_len, LANES), F32),
                pltpu.VMEM((shares, part_len, LANES), F32),
            ],
        )(here, params, received, *carried, *([spatial_out] * part))
        returned.append(sent(results[:shares]))
        carried = results[shares:]

    mixed = []
    for part in range(parts):
        mixed = [
            call(
                functools.partial(exit_kernel, part, parts, shares),
                "exit",
                shape_of(tokens.shape, BF16),
                [SCALAR] + [WHOLE] * (4 + shares) + [HBM] * len(mixed),
                outs=HBM,
                scratch_shapes=[
                    pltpu.VMEM((shares, part_len, group), BF16),
                    pltpu.VMEM((rows * part_len, inner), BF16),
                    pltpu.VMEM((rows * part_len, width), BF16),
                    pltpu.SemaphoreType.DMA((rows * frames,)),
                ],
                input_output_aliases={5 + shares: 0} if mixed else {},
            )(here, spatial_out, gate, out_gain, out_weight, *returned[part], *mixed)
        ]
    return mixed[0]


def solution(mesh):
    in_specs = (P("tm", "height", None, None), P(), P(), P(), P(), P(), P(), P(), P())
    out_specs = P("tm", "height", None, None)
    return jax.shard_map(
        per_device, mesh=mesh, in_specs=in_specs, out_specs=out_specs, check_vma=False
    )
```

```python
import functools
import math

import jax
import jax.numpy as jnp
from jax import lax
from jax.experimental import pallas as pl
from jax.experimental.pallas import tpu as pltpu
from jax.sharding import PartitionSpec as P

EPSILON = 1e-05
LANES = 128
TAIL = 16
LOG2_E = 1.4426950408889634
F32 = jnp.float32
BF16 = jnp.bfloat16
EXACT = lax.Precision.HIGHEST
LARGE = 56 * 1024 * 1024
SMALL = 24 * 1024 * 1024

ANY = pl.BlockSpec(memory_space=pl.ANY)
HBM = pl.BlockSpec(memory_space=pltpu.HBM)
SCALAR = pl.BlockSpec(memory_space=pltpu.SMEM)
WHOLE = pl.BlockSpec(memory_space=pltpu.VMEM)


def call(kernel, name, out_shape, in_specs, limit=SMALL, outs=None, **options):
    return pl.pallas_call(
        kernel,
        out_shape=out_shape,
        in_specs=in_specs,
        out_specs=jax.tree.map(lambda _: WHOLE, out_shape) if outs is None else outs,
        compiler_params=pltpu.CompilerParams(vmem_limit_bytes=limit),
        cost_estimate=pl.CostEstimate(flops=1, bytes_accessed=1, transcendentals=0),
        name=name,
        **options,
    )


def shape_of(shape, dtype):
    return jax.ShapeDtypeStruct(shape, dtype)


def dot(left, right, **options):
    return jnp.dot(left, right, preferred_element_type=F32, **options)


def dot_tn(left, right):
    return lax.dot_general(left, right, (((0,), (0,)), ((), ())), preferred_element_type=F32)


def dot_nt(left, right):
    return lax.dot_general(left, right, (((1,), (1,)), ((), ())), preferred_element_type=F32)


def softplus(values):
    return jnp.maximum(values, 0.0) + jnp.log1p(jnp.exp(-jnp.abs(values)))


def iota(shape, dim):
    return lax.broadcasted_iota(jnp.int32, shape, dim)


def spread_matrix(first_head, width, head_dim):
    return (iota((LANES, width), 0) - first_head == iota((LANES, width), 1) // head_dim).astype(BF16)


def spread(values, matrix):
    high = values.astype(BF16)
    low = (values - high.astype(F32)).astype(BF16)
    return dot(high, matrix) + dot(low, matrix)


def head_mixes(scores, running, running_t, dt_t, x, first_head, heads, head_dim):
    length = scores.shape[0]
    running, running_t = running * LOG2_E, running_t * LOG2_E
    outs = []

    def weights(head):
        spreads = running[:, head : head + 1] - running_t[head : head + 1, :]
        return (scores * jnp.exp2(jnp.minimum(spreads, 0.0)) * dt_t[head : head + 1, :]).astype(BF16)

    head = 0
    while head < heads:
        here = first_head + head
        if head + 1 < heads and 2 * head_dim == LANES:
            both = x[:, head * head_dim : (head + 2) * head_dim]
            first = iota((length, LANES), 1) < head_dim
            zero = jnp.zeros_like(both)
            stacked = jnp.concatenate([jnp.where(first, both, zero), jnp.where(first, zero, both)], axis=0)
            pair = jnp.concatenate([weights(here), weights(here + 1)], axis=1)
            outs.append(dot(pair, stacked))
            head += 2
        else:
            outs.append(dot(weights(here), x[:, head * head_dim : (head + 1) * head_dim]))
            head += 1
    return outs[0] if len(outs) == 1 else jnp.concatenate(outs, axis=1)


def column_copies(weight, scratch, sems, first, offset, blocks):
    width = scratch.shape[1] // blocks
    return [
        pltpu.make_async_copy(
            weight.at[:, pl.ds(offset + index * width, width)],
            scratch.at[:, pl.ds(index * width, width)],
            sems.at[first + index],
        )
        for index in range(blocks)
    ]


def rank_of(device, shares):
    code = device ^ (device >> 1)
    return (shares - code) % shares if isinstance(device, int) else lax.rem(shares - code, shares)


def packing(length, group):
    columns = group // LANES
    rest = -(-(2 * length + TAIL) // columns)
    return length, -(-rest // TAIL) * TAIL


def pack_rest(ref, length, b_proj, c_proj, dt):
    columns, rest = ref.shape[1] // LANES, ref.shape[0] - length
    blank = jnp.zeros((columns * rest - 2 * length - TAIL, LANES), BF16)
    stacked = jnp.concatenate([b_proj, c_proj, dt, blank], axis=0)
    for column in range(columns):
        ref[length:, column * LANES : (column + 1) * LANES] = stacked[column * rest : (column + 1) * rest]


def unpacked_rest(ref, length):
    columns = ref.shape[1] // LANES
    stacked = jnp.concatenate(
        [ref[length:, column * LANES : (column + 1) * LANES] for column in range(columns)], axis=0
    )
    return stacked[:length], stacked[length : 2 * length], stacked[2 * length : 2 * length + TAIL]


def entry_kernel(shares, heads, state, blocks, *refs):
    here_ref, band, tokens, gain, bias, rates, dt_weight, bc_weight, weight = refs[:9]
    normed_out, payload_out, bc_own, logits, params, own_states, other_states, band_decays = refs[9:17]
    held, dt_held, bc_held, held_weight, table, normed, payload, sems, out_sems = refs[17:]
    frames, rows, columns, width = tokens.shape
    length = frames * columns
    count = rows * length
    groups = shares // rows
    per_group = heads // groups
    group = held_weight.shape[1] // groups

    token_copies = [
        pltpu.make_async_copy(tokens.at[frame, row], held.at[row, frame], sems.at[row * frames + frame])
        for row in range(rows)
        for frame in range(frames)
    ]
    for copy in token_copies:
        copy.start()
    first = rows * frames
    dt_copy = pltpu.make_async_copy(dt_weight, dt_held, sems.at[first])
    dt_copy.start()
    copies = column_copies(weight, held_weight, sems, first + 2, 0, blocks)
    for copy in copies:
        copy.start()
    bc_copy = pltpu.make_async_copy(bc_weight, bc_held, sems.at[first + 1])
    bc_copy.start()

    table[...] = jnp.zeros_like(table)
    table[0:1, : 2 * heads] = bias[...].reshape(1, 2 * heads)
    table[1:2, :heads] = rates[0:1, :]
    table[1:2, heads : 2 * heads] = rates[1:2, :]
    first_head = heads + here_ref[0] // rows * per_group
    lane_in, lane_out = iota((LANES, LANES), 0), iota((LANES, LANES), 1)
    own = ((lane_in == lane_out + first_head) & (lane_out < per_group)).astype(F32)
    params[0:8, :] = table[...]
    params[8:16, :] = dot(table[...], own, precision=EXACT)
    logits[...] = jnp.zeros_like(logits)

    gains = gain[...].reshape(1, width)
    for index, copy in enumerate(token_copies):
        copy.wait()
        values = held[index // frames, index % frames].astype(F32)
        mean_square = jnp.mean(values * values, axis=-1, keepdims=True)
        normed[index * columns : (index + 1) * columns, :] = (
            values * lax.rsqrt(mean_square + EPSILON) * gains
        ).astype(BF16)
    outgoing = [pltpu.make_async_copy(normed, normed_out, out_sems.at[0])]
    outgoing[0].start()
    dt_copy.wait()
    logits[:, : 2 * heads] = dot_nt(normed[...], dt_held[...]).astype(BF16).astype(F32)
    dt_heads = jnp.transpose(logits[...]).astype(BF16)[heads : 2 * heads + TAIL]
    scan = [
        end_factors(frame_of(logits, frame, rows, frames, columns), params, rows * columns)
        for frame in range(frames)
    ]

    def leave(piece, at, sem):
        outgoing.append(
            pltpu.make_async_copy(payload.at[piece, at], payload_out.at[piece, at], out_sems.at[sem])
        )
        outgoing[-1].start()

    block = held_weight.shape[1] // blocks
    for index, copy in enumerate(copies):
        copy.wait()
        at = index * block
        values = dot(normed[...], held_weight[:, at : at + block]).astype(BF16)
        for inside in range(0, block, group):
            for row in range(rows):
                piece = rank_of((at + inside) // group * rows + row, shares)
                payload[piece, :length, :] = values[row * length : (row + 1) * length, inside : inside + group]
                leave(piece, pl.ds(0, length), 1 + piece)
    bc_copy.wait()
    bc = dot(normed[...], bc_held[...]).astype(BF16)
    bc_own[...] = bc[:, : 2 * state]
    for part in range(groups):
        for row in range(rows):
            piece = rank_of(part * rows + row, shares)
            here = slice(row * length, (row + 1) * length)
            pack_rest(
                payload.at[piece],
                length,
                bc[here, 2 * state : 3 * state],
                bc[here, 3 * state :],
                dt_heads[part * per_group : part * per_group + TAIL, here],
            )
            leave(piece, pl.ds(length, payload.shape[1] - length), 1 + shares + piece)
    half = state // 2
    head_dim = groups * group // heads
    mine = band[0] % 2 == 0
    matrix = spread_matrix(0, groups * group, head_dim)
    factors = dot(jnp.concatenate([factor for factor, _ in scan], axis=0), matrix)
    span = rows * columns
    for frame in range(frames):
        b_proj = frame_of(bc_own, frame, rows, frames, columns)[:, :state]
        values = jnp.concatenate(
            [frame_x(payload, part, frame, rows, columns) for part in range(groups)], axis=1
        )
        scaled = (values.astype(F32) * factors[frame * span : (frame + 1) * span]).astype(BF16)
        fresh = dot_tn(b_proj, scaled).astype(BF16)
        at_rows = slice(frame * half, (frame + 1) * half)
        own_states[at_rows, :] = jnp.where(mine, fresh[:half], fresh[half:])
        other_states[at_rows, :] = jnp.where(mine, fresh[half:], fresh[:half])
    whole = [decay for _, decay in scan] + [jnp.zeros((8 - frames, LANES), F32)]
    decays = spread(jnp.concatenate(whole, axis=0), matrix)
    tail = tail_of(decays)
    own_states[frames * half :, :] = tail
    other_states[frames * half :, :] = tail
    band_decays[...] = tail
    for copy in outgoing:
        copy.wait()


def gate_kernel(blocks, after, normed, weight, out, held_weight, sems):
    inner = held_weight.shape[1]
    copies = column_copies(weight, held_weight, sems, 0, inner, blocks)
    for copy in copies:
        copy.start()
    block = inner // blocks
    for index, copy in enumerate(copies):
        copy.wait()
        at = slice(index * block, (index + 1) * block)
        out[:, at] = dot(normed[...], held_weight[:, at]).astype(BF16)


def frame_of(ref, frame, rows, frames, columns):
    return jnp.concatenate(
        [
            ref[(row * frames + frame) * columns : (row * frames + frame + 1) * columns, :]
            for row in range(rows)
        ],
        axis=0,
    )


def frame_x(payload, part, frame, rows, columns):
    shares = payload.shape[0]
    return jnp.concatenate(
        [
            payload[rank_of(part * rows + row, shares), frame * columns : (frame + 1) * columns, :]
            for row in range(rows)
        ],
        axis=0,
    )


def scan_terms(logits, params, causal):
    dt = softplus(logits + params[0:1, :])
    running = dot(causal.astype(F32), -dt * params[1:2, :], precision=EXACT)
    return dt, running, jnp.min(running, axis=0, keepdims=True)


def end_factors(logits, params, length):
    causal = iota((length, length), 0) >= iota((length, length), 1)
    dt, running, last = scan_terms(logits, params, causal)
    return (jnp.exp(last - running) * dt).astype(BF16), jnp.exp(last)


def local_kernel(frames, rows, columns, head_dim, groups, *refs):
    after, bc, logits, params, x, out, reach, done = refs
    done[...] = jnp.zeros_like(done)
    length = rows * columns
    group = x.shape[2]
    state = bc.shape[1] // 2
    per_group = group // head_dim
    causal = iota((length, length), 0) >= iota((length, length), 1)

    def stored(ref, values, frame, at):
        for row in range(rows):
            to = (row * frames + frame) * columns
            ref[to : to + columns, at] = values[row * columns : (row + 1) * columns]

    for frame in range(frames):
        dt, running, _ = scan_terms(frame_of(logits, frame, rows, frames, columns), params, causal)
        running_t, dt_t = jnp.transpose(running), jnp.transpose(dt)
        bc_rows = frame_of(bc, frame, rows, frames, columns)
        scores = jnp.where(causal, dot_nt(bc_rows[:, state:], bc_rows[:, :state]), 0.0)
        stored(reach, jnp.exp(running), frame, slice(None))
        for piece in range(groups):
            values = frame_x(x, piece, frame, rows, columns)
            mixed = head_mixes(
                scores, running, running_t, dt_t, values, piece * per_group, per_group, head_dim
            )
            stored(out, mixed.astype(BF16), frame, slice(piece * group, (piece + 1) * group))


def tail_of(decays):
    high = decays.astype(BF16)
    return jnp.concatenate([high, (decays - high.astype(F32)).astype(BF16)], axis=0)


def pair_kernel(frames, band, own, far, total):
    rows = (own.shape[0] - TAIL) // frames
    own_decay = own[-TAIL:-8, :].astype(F32) + own[-8:, :].astype(F32)
    far_decay = far[-TAIL:-8, :].astype(F32) + far[-8:, :].astype(F32)
    lower = band[0] % 2 == 0
    through = jnp.where(lower, far_decay, own_decay)
    for frame in range(frames):
        at = slice(frame * rows, (frame + 1) * rows)
        first = jnp.where(lower, own[at, :], far[at, :]).astype(F32)
        second = jnp.where(lower, far[at, :], own[at, :]).astype(F32)
        total[at, :] = (through[frame : frame + 1, :] * first + second).astype(BF16)
    total[frames * rows :, :] = tail_of(own_decay * far_decay)


def merge_kernel(frames, distance, finish, *refs):
    _, band, own, far = refs[:4]
    start = distance == 2
    rest = list(refs[4:])
    before_in = None if start else rest.pop(0)
    band_own, band_far = (rest.pop(0), rest.pop(0)) if finish else (None, None)
    rows = (own.shape[0] - TAIL) // frames
    upper, lower_band = (band[0] // distance) % 2 == 1, band[0] % 2 == 0
    own_decay = own[-TAIL:-8, :].astype(F32) + own[-8:, :].astype(F32)
    far_decay = far[-TAIL:-8, :].astype(F32) + far[-8:, :].astype(F32)
    if start:
        before_decay = jnp.ones_like(own_decay)
    else:
        before_decay = before_in[-8:, :]
    if finish:
        first_decay = jnp.where(
            lower_band,
            band_own[-TAIL:-8, :].astype(F32) + band_own[-8:, :].astype(F32),
            band_far[-TAIL:-8, :].astype(F32) + band_far[-8:, :].astype(F32),
        )
    through = jnp.where(upper, own_decay, far_decay)
    for frame in range(frames):
        at = slice(frame * rows, (frame + 1) * rows)
        row = slice(frame, frame + 1)
        far_state = far[at, :].astype(F32)
        came = before_decay[row, :] * far_state
        if not start:
            came = came + before_in[at, :]
        before = jnp.where(upper, came, 0.0 if start else before_in[at, :])
        if finish:
            keep, give = rest
            first = jnp.where(lower_band, band_own[at, :], band_far[at, :]).astype(F32)
            after = first_decay[row, :] * before + first
            keep[at, :] = jnp.where(lower_band, before, after).astype(BF16)
            give[at, :] = jnp.where(lower_band, after, before).astype(BF16)
        else:
            total, before_out = rest
            own_state = own[at, :].astype(F32)
            early = jnp.where(upper, far_state, own_state)
            late = jnp.where(upper, own_state, far_state)
            total[at, :] = (through[row, :] * early + late).astype(BF16)
            before_out[at, :] = before
    if not finish:
        total[frames * rows :, :] = tail_of(own_decay * far_decay)
        before_out[frames * rows :, :] = jnp.where(upper, before_decay * far_decay, before_decay)


def decays_of(ref):
    return ref[-TAIL:-8, :].astype(F32) + ref[-8:, :].astype(F32)


def places_of(band):
    return band % 2 == 0, (band // 2) % 2 == 1, band // 4 == 1


def cross_kernel(frames, _, band, total, first, near, far, message):
    even, x_high, y_high = places_of(band[0])
    own_decay, first_decay = decays_of(total), decays_of(first)
    diagonal = decays_of(near) * decays_of(far)
    one, zero = jnp.ones_like(own_decay), jnp.zeros_like(own_decay)
    odd_first = jnp.where(y_high, jnp.where(x_high, one, own_decay * diagonal), zero)
    odd_own = jnp.where(x_high & y_high, zero, one)
    of_first = jnp.where(even, jnp.where(x_high, own_decay, one), odd_first)
    of_own = jnp.where(even, jnp.where(x_high, one, first_decay), odd_own)
    rows = (total.shape[0] - TAIL) // frames
    for frame in range(frames):
        at, row = slice(frame * rows, (frame + 1) * rows), slice(frame, frame + 1)
        sent = of_first[row] * first[at, :].astype(F32) + of_own[row] * total[at, :].astype(F32)
        message[at, :] = sent.astype(BF16)
    message[frames * rows :, :] = tail_of(jnp.where(even, own_decay * first_decay, own_decay))


def settle_kernel(frames, _, band, first, second, near, far, band_own, band_far, keep, give):
    even, x_high, y_high = places_of(band[0])
    first_decay, second_decay = decays_of(first), decays_of(second)
    diagonal = decays_of(near) * decays_of(far)
    one, zero = jnp.ones_like(first_decay), jnp.zeros_like(first_decay)
    even_second = jnp.where(y_high, jnp.where(x_high, first_decay, one), zero)
    odd_second = jnp.where(x_high | y_high, one, zero)
    odd_first = jnp.where(y_high, jnp.where(x_high, second_decay, diagonal), zero)
    of_second = jnp.where(even, even_second, odd_second)
    of_first = jnp.where(even, jnp.where(x_high, one, zero), odd_first)
    band_decay = jnp.where(even, decays_of(band_own), decays_of(band_far))
    rows = keep.shape[0] // frames
    for frame in range(frames):
        at, row = slice(frame * rows, (frame + 1) * rows), slice(frame, frame + 1)
        before = of_second[row] * second[at, :].astype(F32) + of_first[row] * first[at, :].astype(F32)
        lower = jnp.where(even, band_own[at, :], band_far[at, :]).astype(F32)
        after = band_decay[row] * before + lower
        keep[at, :] = jnp.where(even, before, after).astype(BF16)
        give[at, :] = jnp.where(even, after, before).astype(BF16)


def incoming_kernel(frames, rows, columns, head_dim, band, out_local, bc, reach, own, other, out):
    state = bc.shape[1] // 2
    half = state // 2
    inner = out.shape[1]
    mine = band[0] % 2 == 0
    matrix = spread_matrix(0, inner, head_dim)
    for frame in range(frames):
        at = slice(frame * half, (frame + 1) * half)
        low = jnp.where(mine, own[at, :], other[at, :])
        high = jnp.where(mine, other[at, :], own[at, :])
        carried = jnp.concatenate([low, high], axis=0)
        for row in range(rows):
            to = (row * frames + frame) * columns
            here = slice(to, to + columns)
            factor = spread(reach[here, :], matrix)
            out[here, :] = out_local[here, :].astype(F32) + factor * dot(bc[here, state:], carried)


def temporal_kernel(
    part, parts, per_group, head_dim, rows, frames, columns, chunk_cols, shares, state, *refs
):
    here_ref, params, payload = refs[:3]
    rest = list(refs[3:])
    carried_in = rest.pop(0) if part > 0 else None
    del rest[:part]
    outs, rest = rest[:shares], rest[shares:]
    carried_out = rest.pop(0) if part + 1 < parts else None
    b_all, c_all, dt_all, decay_all = rest
    here = here_ref[0]
    length = frames * columns
    part_cols = columns // parts
    group = outs[0].shape[1]
    eye = (iota((TAIL, LANES), 0) == iota((TAIL, LANES), 1)) & (iota((TAIL, LANES), 1) < per_group)
    eye = eye.astype(BF16)

    def came(distance):
        return payload.at[rank_of(here ^ distance, shares)]

    for distance in range(shares):
        b_proj, c_proj, logits = unpacked_rest(came(distance), length)
        logits = dot_tn(logits, eye)
        for frame in range(frames):
            at = slice(frame * columns + part * part_cols, frame * columns + (part + 1) * part_cols)
            to = slice(frame * part_cols, (frame + 1) * part_cols)
            b_all[distance, to] = b_proj[at]
            c_all[distance, to] = c_proj[at]
            dt = softplus(logits[at] + params[8:9, :])
            dt_all[distance, to] = dt
            decay_all[distance, to] = -dt * params[9:10, :]

    all_frames = shares * frames
    size = all_frames * chunk_cols

    def order_key(dim):
        index = iota((size, size), dim)
        source = here ^ (index // (frames * chunk_cols))
        frame = source * frames + (index // chunk_cols) % frames
        return (index % chunk_cols) * all_frames + frame

    causal = order_key(0) >= order_key(1)
    order = causal.astype(F32)
    matrix = spread_matrix(0, group, head_dim)
    carried = jnp.zeros((state, group), F32) if part == 0 else carried_in[...]
    places = [(source, frame) for source in range(shares) for frame in range(frames)]
    for chunk in range(part_cols // chunk_cols):

        def gathered(ref_of, pitch=part_cols, offset=0):
            return jnp.concatenate(
                [
                    ref_of(source)[pl.ds(frame * pitch + offset + chunk * chunk_cols, chunk_cols), :]
                    for source, frame in places
                ],
                axis=0,
            )

        values = gathered(came, columns, part * part_cols)
        b_proj = gathered(lambda source: b_all.at[source])
        c_proj = gathered(lambda source: c_all.at[source])
        dt = gathered(lambda source: dt_all.at[source])
        running = dot(order, gathered(lambda source: decay_all.at[source]), precision=EXACT)
        running_t, dt_t = jnp.transpose(running), jnp.transpose(dt)
        scores = jnp.where(causal, dot_nt(c_proj, b_proj), 0.0)
        last = jnp.min(running, axis=0, keepdims=True)
        mixed = head_mixes(scores, running, running_t, dt_t, values, 0, per_group, head_dim)
        ends = jnp.concatenate([running, jnp.broadcast_to(last, (8, LANES))], axis=0)
        to_end = jnp.exp(last - running) * dt
        factors = dot(jnp.concatenate([jnp.exp(ends), to_end], axis=0).astype(BF16), matrix)
        mixed = mixed + factors[:size] * dot(c_proj, carried.astype(BF16))
        scaled = (values.astype(F32) * factors[size + 8 :]).astype(BF16)
        carried = factors[size : size + 1, :] * carried + dot_tn(b_proj, scaled)
        mixed = mixed.astype(BF16)
        for index, (source, frame) in enumerate(places):
            to = frame * part_cols + chunk * chunk_cols
            outs[source][to : to + chunk_cols, :] = mixed[index * chunk_cols : (index + 1) * chunk_cols]
    if carried_out is not None:
        carried_out[...] = carried


def exit_kernel(part, parts, shares, *refs):
    here, spatial, gate, gain, weight = refs[:5]
    out, temporal, normed, mixed, sems = refs[-5:]
    frames, rows, columns, _ = out.shape
    part_cols = columns // parts
    _, part_len, group = temporal.shape
    groups = shares // rows
    inner = groups * group
    for index in range(shares):
        distance = (shares - index) % shares
        temporal[here[0] ^ distance] = refs[5 + index][...]

    def own(ref, row, at):
        return jnp.concatenate(
            [
                ref[pl.ds((row * frames + frame) * columns + part * part_cols, part_cols), at]
                for frame in range(frames)
            ],
            axis=0,
        )

    gains = gain[...].reshape(1, inner)
    for row in range(rows):
        total = jnp.zeros((part_len, 1), F32)
        kept = []
        for index in range(groups):
            at = slice(index * group, (index + 1) * group)
            gates = own(gate, row, at).astype(F32)
            gated = own(spatial, row, at) + temporal[index * rows + row].astype(F32)
            gated = gated * (gates / (1.0 + jnp.exp(-gates)))
            total = total + jnp.sum(gated * gated, axis=1, keepdims=True)
            kept.append(gated)
        scale = lax.rsqrt(total / inner + EPSILON)
        for index, gated in enumerate(kept):
            at = slice(index * group, (index + 1) * group)
            normed[row * part_len : (row + 1) * part_len, at] = (gated * scale * gains[:, at]).astype(BF16)
    mixed[...] = dot(normed[...], weight[...]).astype(BF16)
    copies = [
        pltpu.make_async_copy(
            mixed.at[pl.ds((row * frames + frame) * part_cols, part_cols), :],
            out.at[frame, row, pl.ds(part * part_cols, part_cols), :],
            sems.at[row * frames + frame],
        )
        for row in range(rows)
        for frame in range(frames)
    ]
    for copy in copies:
        copy.start()
    for copy in copies:
        copy.wait()


def swapped(value, axis, distance):
    count = lax.axis_size(axis)
    return lax.ppermute(value, axis, [(source, source ^ distance) for source in range(count)])


def crossed(value, axis, even, odd):
    count = lax.axis_size(axis)
    pairs = [(source, source ^ (odd if source % 2 else even)) for source in range(count)]
    return lax.ppermute(value, axis, pairs)


def per_device(
    tokens, norm_gain, in_weight, bc_weight, dt_weight, dt_bias, decay_rate, out_gain, out_weight
):
    frames, rows, columns, width = tokens.shape
    heads = decay_rate.shape[1]
    inner = out_weight.shape[0]
    head_dim = inner // heads
    state = bc_weight.shape[1] // 4
    shares = lax.axis_size("tm")
    bands = lax.axis_size("height")
    groups = shares // rows
    group = inner // groups
    per_group = heads // groups
    length = frames * columns
    count = rows * length
    half = state // 2
    chunk_cols = 16
    blocks = parts = 2
    part_len = length // parts
    here = lax.axis_index("tm").astype(jnp.int32).reshape(1)
    band = lax.axis_index("height").astype(jnp.int32).reshape(1)

    packed = (shares, sum(packing(length, group)), group)
    normed, payload, bc_own, logits, params, own, other, band_decays = call(
        functools.partial(entry_kernel, shares, heads, state, blocks),
        "entry",
        [
            shape_of((count, width), BF16),
            shape_of(packed, BF16),
            shape_of((count, 2 * state), BF16),
            shape_of((count, LANES), F32),
            shape_of((16, LANES), F32),
        ]
        + [shape_of((frames * half + TAIL, inner), BF16)] * 2
        + [shape_of((TAIL, inner), BF16)],
        [SCALAR, SCALAR, HBM, WHOLE, WHOLE, WHOLE, HBM, HBM, HBM],
        limit=LARGE,
        outs=[HBM, HBM] + [WHOLE] * 6,
        scratch_shapes=[
            pltpu.VMEM((rows, frames, columns, width), BF16),
            pltpu.VMEM((2 * heads, width), BF16),
            pltpu.VMEM((width, 4 * state), BF16),
            pltpu.VMEM((width, inner), BF16),
            pltpu.VMEM((8, LANES), F32),
            pltpu.VMEM((count, width), BF16),
            pltpu.VMEM(packed, BF16),
            pltpu.SemaphoreType.DMA((rows * frames + 2 + blocks,)),
            pltpu.SemaphoreType.DMA((1 + 2 * shares,)),
        ],
    )(here, band, tokens, norm_gain, dt_bias, decay_rate, dt_weight.T, bc_weight, in_weight)

    def sent(parts):
        moved = {d: swapped(parts[d], "tm", d) for d in range(shares - 1, 0, -1)}
        return [parts[0]] + list(moved.values())

    line = [rank_of(device, shares) for device in range(shares)]
    received = lax.all_to_all(
        payload,
        "tm",
        split_axis=0,
        concat_axis=0,
        tiled=True,
        axis_index_groups=[[line.index(rank) for rank in range(shares)]],
    )
    far = swapped(other, "height", 1)
    gate = call(
        functools.partial(gate_kernel, blocks),
        "gate",
        shape_of((count, inner), BF16),
        [ANY, WHOLE, HBM],
        scratch_shapes=[
            pltpu.VMEM((width, inner), BF16),
            pltpu.SemaphoreType.DMA((blocks,)),
        ],
    )(payload, normed, in_weight)

    out_local, reach, done = call(
        functools.partial(local_kernel, frames, rows, columns, head_dim, groups),
        "spatial_local",
        [shape_of((count, inner), BF16), shape_of((count, LANES), F32), shape_of((8, LANES), F32)],
        [ANY] + [WHOLE] * 4,
    )(gate, bc_own, logits, params, payload)

    total = call(
        functools.partial(pair_kernel, frames),
        "pair_total",
        shape_of((frames * half + TAIL, inner), BF16),
        [SCALAR, WHOLE, WHOLE],
    )(band, own, far)
    before = []
    distance = 2
    if bands == 8:
        near, far_decays = (swapped(band_decays, "height", distance) for distance in (6, 7))
        first = crossed(total, "height", 2, 4)
        message = call(
            functools.partial(cross_kernel, frames),
            "cross",
            shape_of((frames * half + TAIL, inner), BF16),
            [ANY, SCALAR] + [WHOLE] * 4,
        )(done, band, total, first, near, far_decays)
        second = crossed(message, "height", 4, 2)
        results = call(
            functools.partial(settle_kernel, frames),
            "settle",
            [shape_of((frames * half, inner), BF16)] * 2,
            [ANY, SCALAR] + [WHOLE] * 6,
        )(done, band, first, second, near, far_decays, own, far)
        distance = bands
    while distance < bands:
        far_total = swapped(total, "height", distance)
        finish = distance * 2 >= bands
        operands = [done, band, total, far_total] + before + ([own, far] if finish else [])
        outs = (
            [shape_of((frames * half, inner), BF16)] * 2
            if finish
            else [
                shape_of((frames * half + TAIL, inner), BF16),
                shape_of((frames * half + 8, inner), F32),
            ]
        )
        results = call(
            functools.partial(merge_kernel, frames, distance, finish),
            "merge",
            outs,
            [ANY, SCALAR] + [WHOLE] * (len(operands) - 2),
        )(*operands)
        if not finish:
            total, before = results[0], [results[1]]
        distance *= 2
    keep, give = results
    came = swapped(give, "height", 1)

    spatial_out = call(
        functools.partial(incoming_kernel, frames, rows, columns, head_dim),
        "spatial_incoming",
        shape_of((count, inner), F32),
        [SCALAR] + [WHOLE] * 5,
    )(band, out_local, bc_own, reach, keep, came)

    returned, carried = [], []
    for part in range(parts):
        more = [shape_of((state, group), F32)] if part + 1 < parts else []
        results = call(
            functools.partial(
                temporal_kernel,
                part,
                parts,
                per_group,
                head_dim,
                rows,
                frames,
                columns,
                chunk_cols,
                shares,
                state,
            ),
            "temporal",
            [shape_of((part_len, group), BF16)] * shares + more,
            [SCALAR] + [WHOLE] * (2 + len(carried)) + [ANY] * part,
            scratch_shapes=[
                pltpu.VMEM((shares, part_len, state), BF16),
                pltpu.VMEM((shares, part_len, state), BF16),
                pltpu.VMEM((shares, part_len, LANES), F32),
                pltpu.VMEM((shares, part_len, LANES), F32),
            ],
        )(here, params, received, *carried, *([spatial_out] * part))
        returned.append(sent(results[:shares]))
        carried = results[shares:]

    mixed = []
    for part in range(parts):
        mixed = [
            call(
                functools.partial(exit_kernel, part, parts, shares),
                "exit",
                shape_of(tokens.shape, BF16),
                [SCALAR] + [WHOLE] * (4 + shares) + [HBM] * len(mixed),
                outs=HBM,
                scratch_shapes=[
                    pltpu.VMEM((shares, part_len, group), BF16),
                    pltpu.VMEM((rows * part_len, inner), BF16),
                    pltpu.VMEM((rows * part_len, width), BF16),
                    pltpu.SemaphoreType.DMA((rows * frames,)),
                ],
                input_output_aliases={5 + shares: 0} if mixed else {},
            )(here, spatial_out, gate, out_gain, out_weight, *returned[part], *mixed)
        ]
    return mixed[0]


def solution(mesh):
    in_specs = (P("tm", "height", None, None), P(), P(), P(), P(), P(), P(), P(), P())
    out_specs = P("tm", "height", None, None)
    return jax.shard_map(
        per_device, mesh=mesh, in_specs=in_specs, out_specs=out_specs, check_vma=False
    )
```

```python
import functools
import math

import jax
import jax.numpy as jnp
from jax import lax
from jax.experimental import pallas as pl
from jax.experimental.pallas import tpu as pltpu
from jax.sharding import PartitionSpec as P

EPSILON = 1e-05
LANES = 128
TAIL = 16
LOG2_E = 1.4426950408889634
F32 = jnp.float32
BF16 = jnp.bfloat16
EXACT = lax.Precision.HIGHEST
LARGE = 56 * 1024 * 1024
SMALL = 24 * 1024 * 1024

ANY = pl.BlockSpec(memory_space=pl.ANY)
HBM = pl.BlockSpec(memory_space=pltpu.HBM)
SCALAR = pl.BlockSpec(memory_space=pltpu.SMEM)
WHOLE = pl.BlockSpec(memory_space=pltpu.VMEM)


def call(kernel, name, out_shape, in_specs, limit=SMALL, outs=None, **options):
    return pl.pallas_call(
        kernel,
        out_shape=out_shape,
        in_specs=in_specs,
        out_specs=jax.tree.map(lambda _: WHOLE, out_shape) if outs is None else outs,
        compiler_params=pltpu.CompilerParams(vmem_limit_bytes=limit),
        cost_estimate=pl.CostEstimate(flops=1, bytes_accessed=1, transcendentals=0),
        name=name,
        **options,
    )


def shape_of(shape, dtype):
    return jax.ShapeDtypeStruct(shape, dtype)


def dot(left, right, **options):
    return jnp.dot(left, right, preferred_element_type=F32, **options)


def dot_tn(left, right):
    return lax.dot_general(left, right, (((0,), (0,)), ((), ())), preferred_element_type=F32)


def dot_nt(left, right):
    return lax.dot_general(left, right, (((1,), (1,)), ((), ())), preferred_element_type=F32)


def softplus(values):
    return jnp.maximum(values, 0.0) + jnp.log1p(jnp.exp(-jnp.abs(values)))


def iota(shape, dim):
    return lax.broadcasted_iota(jnp.int32, shape, dim)


def spread_matrix(first_head, width, head_dim):
    return (iota((LANES, width), 0) - first_head == iota((LANES, width), 1) // head_dim).astype(BF16)


def spread(values, matrix):
    high = values.astype(BF16)
    low = (values - high.astype(F32)).astype(BF16)
    return dot(high, matrix) + dot(low, matrix)


def head_mixes(scores, running, running_t, dt_t, x, first_head, heads, head_dim):
    length = scores.shape[0]
    running, running_t = running * LOG2_E, running_t * LOG2_E
    outs = []

    def weights(head):
        spreads = running[:, head : head + 1] - running_t[head : head + 1, :]
        return (scores * jnp.exp2(jnp.minimum(spreads, 0.0)) * dt_t[head : head + 1, :]).astype(BF16)

    head = 0
    while head < heads:
        here = first_head + head
        if head + 1 < heads and 2 * head_dim == LANES:
            both = x[:, head * head_dim : (head + 2) * head_dim]
            first = iota((length, LANES), 1) < head_dim
            zero = jnp.zeros_like(both)
            stacked = jnp.concatenate([jnp.where(first, both, zero), jnp.where(first, zero, both)], axis=0)
            pair = jnp.concatenate([weights(here), weights(here + 1)], axis=1)
            outs.append(dot(pair, stacked))
            head += 2
        else:
            outs.append(dot(weights(here), x[:, head * head_dim : (head + 1) * head_dim]))
            head += 1
    return outs[0] if len(outs) == 1 else jnp.concatenate(outs, axis=1)


def column_copies(weight, scratch, sems, first, offset, blocks):
    width = scratch.shape[1] // blocks
    return [
        pltpu.make_async_copy(
            weight.at[:, pl.ds(offset + index * width, width)],
            scratch.at[:, pl.ds(index * width, width)],
            sems.at[first + index],
        )
        for index in range(blocks)
    ]


def rank_of(device):
    return device ^ (device >> 1)


def packing(length, group):
    columns = group // LANES
    rest = -(-(2 * length + TAIL) // columns)
    return length, -(-rest // TAIL) * TAIL


def pack_rest(ref, length, b_proj, c_proj, dt):
    columns, rest = ref.shape[1] // LANES, ref.shape[0] - length
    blank = jnp.zeros((columns * rest - 2 * length - TAIL, LANES), BF16)
    stacked = jnp.concatenate([b_proj, c_proj, dt, blank], axis=0)
    for column in range(columns):
        ref[length:, column * LANES : (column + 1) * LANES] = stacked[column * rest : (column + 1) * rest]


def unpacked_rest(ref, length):
    columns = ref.shape[1] // LANES
    stacked = jnp.concatenate(
        [ref[length:, column * LANES : (column + 1) * LANES] for column in range(columns)], axis=0
    )
    return stacked[:length], stacked[length : 2 * length], stacked[2 * length : 2 * length + TAIL]


def entry_kernel(shares, heads, state, blocks, *refs):
    here_ref, band, tokens, gain, bias, rates, dt_weight, bc_weight, weight = refs[:9]
    normed_out, payload_out, bc_own, logits, params, own_states, other_states, band_decays = refs[9:17]
    held, dt_held, bc_held, held_weight, table, normed, payload, sems, out_sems = refs[17:]
    frames, rows, columns, width = tokens.shape
    length = frames * columns
    count = rows * length
    groups = shares // rows
    per_group = heads // groups
    group = held_weight.shape[1] // groups

    token_copies = [
        pltpu.make_async_copy(tokens.at[frame, row], held.at[row, frame], sems.at[row * frames + frame])
        for row in range(rows)
        for frame in range(frames)
    ]
    for copy in token_copies:
        copy.start()
    first = rows * frames
    dt_copy = pltpu.make_async_copy(dt_weight, dt_held, sems.at[first])
    dt_copy.start()
    bc_copy = pltpu.make_async_copy(bc_weight, bc_held, sems.at[first + 1])
    bc_copy.start()
    copies = column_copies(weight, held_weight, sems, first + 2, 0, blocks)
    for copy in copies:
        copy.start()

    table[...] = jnp.zeros_like(table)
    table[0:1, : 2 * heads] = bias[...].reshape(1, 2 * heads)
    table[1:2, :heads] = rates[0:1, :]
    table[1:2, heads : 2 * heads] = rates[1:2, :]
    first_head = heads + here_ref[0] // rows * per_group
    lane_in, lane_out = iota((LANES, LANES), 0), iota((LANES, LANES), 1)
    own = ((lane_in == lane_out + first_head) & (lane_out < per_group)).astype(F32)
    params[0:8, :] = table[...]
    params[8:16, :] = dot(table[...], own, precision=EXACT)
    logits[...] = jnp.zeros_like(logits)

    gains = gain[...].reshape(1, width)
    for index, copy in enumerate(token_copies):
        copy.wait()
        values = held[index // frames, index % frames].astype(F32)
        mean_square = jnp.mean(values * values, axis=-1, keepdims=True)
        normed[index * columns : (index + 1) * columns, :] = (
            values * lax.rsqrt(mean_square + EPSILON) * gains
        ).astype(BF16)
    outgoing = [pltpu.make_async_copy(normed, normed_out, out_sems.at[0])]
    outgoing[0].start()
    dt_copy.wait()
    logits[:, : 2 * heads] = dot_nt(normed[...], dt_held[...]).astype(BF16).astype(F32)
    dt_heads = jnp.transpose(logits[...]).astype(BF16)[heads : 2 * heads + TAIL]
    bc_copy.wait()
    bc = dot(normed[...], bc_held[...]).astype(BF16)
    bc_own[...] = bc[:, : 2 * state]
    scan = [
        end_factors(frame_of(logits, frame, rows, frames, columns), params, rows * columns)
        for frame in range(frames)
    ]

    block = held_weight.shape[1] // blocks
    for index, copy in enumerate(copies):
        copy.wait()
        at = index * block
        values = dot(normed[...], held_weight[:, at : at + block]).astype(BF16)
        for inside in range(0, block, group):
            part = (at + inside) // group
            for row in range(rows):
                piece = rank_of(part * rows + row)
                here = slice(row * length, (row + 1) * length)
                payload[piece, :length, :] = values[here, inside : inside + group]
                pack_rest(
                    payload.at[piece],
                    length,
                    bc[here, 2 * state : 3 * state],
                    bc[here, 3 * state :],
                    dt_heads[part * per_group : part * per_group + TAIL, here],
                )
                outgoing.append(
                    pltpu.make_async_copy(
                        payload.at[piece], payload_out.at[piece], out_sems.at[1 + piece]
                    )
                )
                outgoing[-1].start()
    half = state // 2
    head_dim = groups * group // heads
    mine = band[0] % 2 == 0
    matrix = spread_matrix(0, groups * group, head_dim)
    factors = dot(jnp.concatenate([factor for factor, _ in scan], axis=0), matrix)
    span = rows * columns
    for frame in range(frames):
        b_proj = frame_of(bc_own, frame, rows, frames, columns)[:, :state]
        values = jnp.concatenate(
            [frame_x(payload, part, frame, rows, columns) for part in range(groups)], axis=1
        )
        scaled = (values.astype(F32) * factors[frame * span : (frame + 1) * span]).astype(BF16)
        fresh = dot_tn(b_proj, scaled).astype(BF16)
        at_rows = slice(frame * half, (frame + 1) * half)
        own_states[at_rows, :] = jnp.where(mine, fresh[:half], fresh[half:])
        other_states[at_rows, :] = jnp.where(mine, fresh[half:], fresh[:half])
    whole = [decay for _, decay in scan] + [jnp.zeros((8 - frames, LANES), F32)]
    decays = spread(jnp.concatenate(whole, axis=0), matrix)
    tail = tail_of(decays)
    own_states[frames * half :, :] = tail
    other_states[frames * half :, :] = tail
    band_decays[...] = tail
    for copy in outgoing:
        copy.wait()


def gate_kernel(blocks, after, normed, weight, out, held_weight, sems):
    inner = held_weight.shape[1]
    copies = column_copies(weight, held_weight, sems, 0, inner, blocks)
    for copy in copies:
        copy.start()
    block = inner // blocks
    for index, copy in enumerate(copies):
        copy.wait()
        at = slice(index * block, (index + 1) * block)
        gates = dot(normed[...], held_weight[:, at]).astype(BF16).astype(F32)
        out[:, at] = (gates / (1.0 + jnp.exp(-gates))).astype(BF16)


def frame_of(ref, frame, rows, frames, columns):
    return jnp.concatenate(
        [
            ref[(row * frames + frame) * columns : (row * frames + frame + 1) * columns, :]
            for row in range(rows)
        ],
        axis=0,
    )


def frame_x(payload, part, frame, rows, columns):
    return jnp.concatenate(
        [
            payload[rank_of(part * rows + row), frame * columns : (frame + 1) * columns, :]
            for row in range(rows)
        ],
        axis=0,
    )


def scan_terms(logits, params, causal):
    dt = softplus(logits + params[0:1, :])
    running = dot(causal.astype(F32), -dt * params[1:2, :], precision=EXACT)
    return dt, running, jnp.min(running, axis=0, keepdims=True)


def end_factors(logits, params, length):
    causal = iota((length, length), 0) >= iota((length, length), 1)
    dt, running, last = scan_terms(logits, params, causal)
    return (jnp.exp(last - running) * dt).astype(BF16), jnp.exp(last)


def local_kernel(frames, rows, columns, head_dim, groups, *refs):
    after, bc, logits, params, x, out, reach = refs
    length = rows * columns
    group = x.shape[2]
    state = bc.shape[1] // 2
    per_group = group // head_dim
    causal = iota((length, length), 0) >= iota((length, length), 1)

    def stored(ref, values, frame, at):
        for row in range(rows):
            to = (row * frames + frame) * columns
            ref[to : to + columns, at] = values[row * columns : (row + 1) * columns]

    for frame in range(frames):
        dt, running, _ = scan_terms(frame_of(logits, frame, rows, frames, columns), params, causal)
        running_t, dt_t = jnp.transpose(running), jnp.transpose(dt)
        bc_rows = frame_of(bc, frame, rows, frames, columns)
        scores = jnp.where(causal, dot_nt(bc_rows[:, state:], bc_rows[:, :state]), 0.0)
        stored(reach, jnp.exp(running), frame, slice(None))
        for piece in range(groups):
            values = frame_x(x, piece, frame, rows, columns)
            mixed = head_mixes(
                scores, running, running_t, dt_t, values, piece * per_group, per_group, head_dim
            )
            stored(out, mixed.astype(BF16), frame, slice(piece * group, (piece + 1) * group))


def tail_of(decays):
    high = decays.astype(BF16)
    return jnp.concatenate([high, (decays - high.astype(F32)).astype(BF16)], axis=0)


def pair_kernel(frames, band, own, far, total):
    rows = (own.shape[0] - TAIL) // frames
    own_decay = own[-TAIL:-8, :].astype(F32) + own[-8:, :].astype(F32)
    far_decay = far[-TAIL:-8, :].astype(F32) + far[-8:, :].astype(F32)
    lower = band[0] % 2 == 0
    through = jnp.where(lower, far_decay, own_decay)
    for frame in range(frames):
        at = slice(frame * rows, (frame + 1) * rows)
        first = jnp.where(lower, own[at, :], far[at, :]).astype(F32)
        second = jnp.where(lower, far[at, :], own[at, :]).astype(F32)
        total[at, :] = (through[frame : frame + 1, :] * first + second).astype(BF16)
    total[frames * rows :, :] = tail_of(own_decay * far_decay)


def merge_kernel(frames, distance, finish, *refs):
    _, band, own, far = refs[:4]
    start = distance == 2
    rest = list(refs[4:])
    before_in = None if start else rest.pop(0)
    band_own, band_far = (rest.pop(0), rest.pop(0)) if finish else (None, None)
    rows = (own.shape[0] - TAIL) // frames
    upper, lower_band = (band[0] // distance) % 2 == 1, band[0] % 2 == 0
    own_decay = own[-TAIL:-8, :].astype(F32) + own[-8:, :].astype(F32)
    far_decay = far[-TAIL:-8, :].astype(F32) + far[-8:, :].astype(F32)
    if start:
        before_decay = jnp.ones_like(own_decay)
    else:
        before_decay = before_in[-8:, :]
    if finish:
        first_decay = jnp.where(
            lower_band,
            band_own[-TAIL:-8, :].astype(F32) + band_own[-8:, :].astype(F32),
            band_far[-TAIL:-8, :].astype(F32) + band_far[-8:, :].astype(F32),
        )
    through = jnp.where(upper, own_decay, far_decay)
    for frame in range(frames):
        at = slice(frame * rows, (frame + 1) * rows)
        row = slice(frame, frame + 1)
        far_state = far[at, :].astype(F32)
        came = before_decay[row, :] * far_state
        if not start:
            came = came + before_in[at, :]
        before = jnp.where(upper, came, 0.0 if start else before_in[at, :])
        if finish:
            keep, give = rest
            first = jnp.where(lower_band, band_own[at, :], band_far[at, :]).astype(F32)
            after = first_decay[row, :] * before + first
            keep[at, :] = jnp.where(lower_band, before, after).astype(BF16)
            give[at, :] = jnp.where(lower_band, after, before).astype(BF16)
        else:
            total, before_out = rest
            own_state = own[at, :].astype(F32)
            early = jnp.where(upper, far_state, own_state)
            late = jnp.where(upper, own_state, far_state)
            total[at, :] = (through[row, :] * early + late).astype(BF16)
            before_out[at, :] = before
    if not finish:
        total[frames * rows :, :] = tail_of(own_decay * far_decay)
        before_out[frames * rows :, :] = jnp.where(upper, before_decay * far_decay, before_decay)


def decays_of(ref):
    return ref[-TAIL:-8, :].astype(F32) + ref[-8:, :].astype(F32)


def places_of(band):
    return band % 2 == 0, (band // 2) % 2 == 1, band // 4 == 1


def cross_kernel(frames, _, band, total, first, near, far, message):
    even, x_high, y_high = places_of(band[0])
    own_decay, first_decay = decays_of(total), decays_of(first)
    diagonal = decays_of(near) * decays_of(far)
    one, zero = jnp.ones_like(own_decay), jnp.zeros_like(own_decay)
    odd_first = jnp.where(y_high, jnp.where(x_high, one, own_decay * diagonal), zero)
    odd_own = jnp.where(x_high & y_high, zero, one)
    of_first = jnp.where(even, jnp.where(x_high, own_decay, one), odd_first)
    of_own = jnp.where(even, jnp.where(x_high, one, first_decay), odd_own)
    rows = (total.shape[0] - TAIL) // frames
    for frame in range(frames):
        at, row = slice(frame * rows, (frame + 1) * rows), slice(frame, frame + 1)
        sent = of_first[row] * first[at, :].astype(F32) + of_own[row] * total[at, :].astype(F32)
        message[at, :] = sent.astype(BF16)
    message[frames * rows :, :] = tail_of(jnp.where(even, own_decay * first_decay, own_decay))


def settle_kernel(frames, _, band, first, second, near, far, band_own, band_far, keep, give):
    even, x_high, y_high = places_of(band[0])
    first_decay, second_decay = decays_of(first), decays_of(second)
    diagonal = decays_of(near) * decays_of(far)
    one, zero = jnp.ones_like(first_decay), jnp.zeros_like(first_decay)
    even_second = jnp.where(y_high, jnp.where(x_high, first_decay, one), zero)
    odd_second = jnp.where(x_high | y_high, one, zero)
    odd_first = jnp.where(y_high, jnp.where(x_high, second_decay, diagonal), zero)
    of_second = jnp.where(even, even_second, odd_second)
    of_first = jnp.where(even, jnp.where(x_high, one, zero), odd_first)
    band_decay = jnp.where(even, decays_of(band_own), decays_of(band_far))
    rows = keep.shape[0] // frames
    for frame in range(frames):
        at, row = slice(frame * rows, (frame + 1) * rows), slice(frame, frame + 1)
        before = of_second[row] * second[at, :].astype(F32) + of_first[row] * first[at, :].astype(F32)
        lower = jnp.where(even, band_own[at, :], band_far[at, :]).astype(F32)
        after = band_decay[row] * before + lower
        keep[at, :] = jnp.where(even, before, after).astype(BF16)
        give[at, :] = jnp.where(even, after, before).astype(BF16)


def incoming_kernel(frames, rows, columns, head_dim, band, out_local, bc, reach, own, other, out):
    state = bc.shape[1] // 2
    half = state // 2
    inner = out.shape[1]
    mine = band[0] % 2 == 0
    matrix = spread_matrix(0, inner, head_dim)
    for frame in range(frames):
        at = slice(frame * half, (frame + 1) * half)
        low = jnp.where(mine, own[at, :], other[at, :])
        high = jnp.where(mine, other[at, :], own[at, :])
        carried = jnp.concatenate([low, high], axis=0)
        for row in range(rows):
            to = (row * frames + frame) * columns
            here = slice(to, to + columns)
            factor = spread(reach[here, :], matrix)
            out[here, :] = out_local[here, :].astype(F32) + factor * dot(bc[here, state:], carried)


def temporal_kernel(
    part, parts, per_group, head_dim, rows, frames, columns, chunk_cols, shares, state, *refs
):
    here_ref, params, payload = refs[:3]
    rest = list(refs[3:])
    carried_in = rest.pop(0) if part > 0 else None
    del rest[:part]
    outs, rest = rest[:shares], rest[shares:]
    carried_out = rest.pop(0) if part + 1 < parts else None
    b_all, c_all, dt_all, decay_all = rest
    here = here_ref[0]
    length = frames * columns
    part_cols = columns // parts
    group = outs[0].shape[1]
    eye = (iota((TAIL, LANES), 0) == iota((TAIL, LANES), 1)) & (iota((TAIL, LANES), 1) < per_group)
    eye = eye.astype(BF16)

    def came(distance):
        return payload.at[rank_of(here ^ distance)]

    for distance in range(shares):
        b_proj, c_proj, logits = unpacked_rest(came(distance), length)
        logits = dot_tn(logits, eye)
        for frame in range(frames):
            at = slice(frame * columns + part * part_cols, frame * columns + (part + 1) * part_cols)
            to = slice(frame * part_cols, (frame + 1) * part_cols)
            b_all[distance, to] = b_proj[at]
            c_all[distance, to] = c_proj[at]
            dt = softplus(logits[at] + params[8:9, :])
            dt_all[distance, to] = dt
            decay_all[distance, to] = -dt * params[9:10, :]

    all_frames = shares * frames
    size = all_frames * chunk_cols

    def order_key(dim):
        index = iota((size, size), dim)
        source = here ^ (index // (frames * chunk_cols))
        frame = source * frames + (index // chunk_cols) % frames
        return (index % chunk_cols) * all_frames + frame

    causal = order_key(0) >= order_key(1)
    order = causal.astype(F32)
    matrix = spread_matrix(0, group, head_dim)
    carried = jnp.zeros((state, group), F32) if part == 0 else carried_in[...]
    places = [(source, frame) for source in range(shares) for frame in range(frames)]
    for chunk in range(part_cols // chunk_cols):

        def gathered(ref_of, pitch=part_cols, offset=0):
            return jnp.concatenate(
                [
                    ref_of(source)[pl.ds(frame * pitch + offset + chunk * chunk_cols, chunk_cols), :]
                    for source, frame in places
                ],
                axis=0,
            )

        values = gathered(came, columns, part * part_cols)
        b_proj = gathered(lambda source: b_all.at[source])
        c_proj = gathered(lambda source: c_all.at[source])
        dt = gathered(lambda source: dt_all.at[source])
        running = dot(order, gathered(lambda source: decay_all.at[source]), precision=EXACT)
        running_t, dt_t = jnp.transpose(running), jnp.transpose(dt)
        scores = jnp.where(causal, dot_nt(c_proj, b_proj), 0.0)
        last = jnp.min(running, axis=0, keepdims=True)
        mixed = head_mixes(scores, running, running_t, dt_t, values, 0, per_group, head_dim)
        ends = jnp.concatenate([running, jnp.broadcast_to(last, (8, LANES))], axis=0)
        to_end = jnp.exp(last - running) * dt
        factors = dot(jnp.concatenate([jnp.exp(ends), to_end], axis=0).astype(BF16), matrix)
        mixed = mixed + factors[:size] * dot(c_proj, carried.astype(BF16))
        scaled = (values.astype(F32) * factors[size + 8 :]).astype(BF16)
        carried = factors[size : size + 1, :] * carried + dot_tn(b_proj, scaled)
        mixed = mixed.astype(BF16)
        for index, (source, frame) in enumerate(places):
            to = frame * part_cols + chunk * chunk_cols
            outs[source][to : to + chunk_cols, :] = mixed[index * chunk_cols : (index + 1) * chunk_cols]
    if carried_out is not None:
        carried_out[...] = carried


def exit_kernel(part, parts, shares, *refs):
    here, spatial, gate, gain, weight = refs[:5]
    out, temporal, normed, mixed, sems = refs[-5:]
    frames, rows, columns, _ = out.shape
    part_cols = columns // parts
    _, part_len, group = temporal.shape
    groups = shares // rows
    inner = groups * group
    for index in range(shares):
        distance = (shares - index) % shares
        temporal[here[0] ^ distance] = refs[5 + index][...]

    def own(ref, row, at):
        return jnp.concatenate(
            [
                ref[pl.ds((row * frames + frame) * columns + part * part_cols, part_cols), at]
                for frame in range(frames)
            ],
            axis=0,
        )

    gains = gain[...].reshape(1, inner)
    for row in range(rows):
        total = jnp.zeros((part_len, 1), F32)
        kept = []
        for index in range(groups):
            at = slice(index * group, (index + 1) * group)
            gated = own(spatial, row, at) + temporal[index * rows + row].astype(F32)
            gated = gated * own(gate, row, at).astype(F32)
            total = total + jnp.sum(gated * gated, axis=1, keepdims=True)
            kept.append(gated)
        scale = lax.rsqrt(total / inner + EPSILON)
        for index, gated in enumerate(kept):
            at = slice(index * group, (index + 1) * group)
            normed[row * part_len : (row + 1) * part_len, at] = (gated * scale * gains[:, at]).astype(BF16)
    copies = []
    width = mixed.shape[1] // 2
    for side in range(2):
        cols = pl.ds(side * width, width)
        mixed[:, side * width : (side + 1) * width] = dot(
            normed[...], weight[:, side * width : (side + 1) * width]
        ).astype(BF16)
        for row in range(rows):
            for frame in range(frames):
                copies.append(
                    pltpu.make_async_copy(
                        mixed.at[pl.ds((row * frames + frame) * part_cols, part_cols), cols],
                        out.at[frame, row, pl.ds(part * part_cols, part_cols), cols],
                        sems.at[len(copies)],
                    )
                )
                copies[-1].start()
    for copy in copies:
        copy.wait()


def swapped(value, axis, distance):
    count = lax.axis_size(axis)
    return lax.ppermute(value, axis, [(source, source ^ distance) for source in range(count)])


def crossed(value, axis, even, odd):
    count = lax.axis_size(axis)
    pairs = [(source, source ^ (odd if source % 2 else even)) for source in range(count)]
    return lax.ppermute(value, axis, pairs)


def per_device(
    tokens, norm_gain, in_weight, bc_weight, dt_weight, dt_bias, decay_rate, out_gain, out_weight
):
    frames, rows, columns, width = tokens.shape
    heads = decay_rate.shape[1]
    inner = out_weight.shape[0]
    head_dim = inner // heads
    state = bc_weight.shape[1] // 4
    shares = lax.axis_size("tm")
    bands = lax.axis_size("height")
    groups = shares // rows
    group = inner // groups
    per_group = heads // groups
    length = frames * columns
    count = rows * length
    half = state // 2
    chunk_cols = 16
    blocks = parts = 2
    part_len = length // parts
    here = lax.axis_index("tm").astype(jnp.int32).reshape(1)
    band = lax.axis_index("height").astype(jnp.int32).reshape(1)

    packed = (shares, sum(packing(length, group)), group)
    normed, payload, bc_own, logits, params, own, other, band_decays = call(
        functools.partial(entry_kernel, shares, heads, state, blocks),
        "entry",
        [
            shape_of((count, width), BF16),
            shape_of(packed, BF16),
            shape_of((count, 2 * state), BF16),
            shape_of((count, LANES), F32),
            shape_of((16, LANES), F32),
        ]
        + [shape_of((frames * half + TAIL, inner), BF16)] * 2
        + [shape_of((TAIL, inner), BF16)],
        [SCALAR, SCALAR, HBM, WHOLE, WHOLE, WHOLE, HBM, HBM, HBM],
        limit=LARGE,
        outs=[HBM, HBM] + [WHOLE] * 6,
        scratch_shapes=[
            pltpu.VMEM((rows, frames, columns, width), BF16),
            pltpu.VMEM((2 * heads, width), BF16),
            pltpu.VMEM((width, 4 * state), BF16),
            pltpu.VMEM((width, inner), BF16),
            pltpu.VMEM((8, LANES), F32),
            pltpu.VMEM((count, width), BF16),
            pltpu.VMEM(packed, BF16),
            pltpu.SemaphoreType.DMA((rows * frames + 2 + blocks,)),
            pltpu.SemaphoreType.DMA((1 + shares,)),
        ],
    )(here, band, tokens, norm_gain, dt_bias, decay_rate, dt_weight.T, bc_weight, in_weight)

    def sent(parts):
        moved = {d: swapped(parts[d], "tm", d) for d in range(shares - 1, 0, -1)}
        return [parts[0]] + list(moved.values())

    line = [rank_of(device) for device in range(shares)]
    received = lax.all_to_all(
        payload,
        "tm",
        split_axis=0,
        concat_axis=0,
        tiled=True,
        axis_index_groups=[[line.index(rank) for rank in range(shares)]],
    )
    far = swapped(other, "height", 1)
    gate = call(
        functools.partial(gate_kernel, blocks),
        "gate",
        shape_of((count, inner), BF16),
        [ANY, WHOLE, HBM],
        scratch_shapes=[
            pltpu.VMEM((width, inner), BF16),
            pltpu.SemaphoreType.DMA((blocks,)),
        ],
    )(payload, normed, in_weight)

    out_local, reach = call(
        functools.partial(local_kernel, frames, rows, columns, head_dim, groups),
        "spatial_local",
        [shape_of((count, inner), BF16), shape_of((count, LANES), F32)],
        [ANY] + [WHOLE] * 4,
    )(gate, bc_own, logits, params, payload)

    total = call(
        functools.partial(pair_kernel, frames),
        "pair_total",
        shape_of((frames * half + TAIL, inner), BF16),
        [SCALAR, WHOLE, WHOLE],
    )(band, own, far)
    before = []
    distance = 2
    if bands == 8:
        near, far_decays = (swapped(band_decays, "height", distance) for distance in (6, 7))
        first = crossed(total, "height", 2, 4)
        message = call(
            functools.partial(cross_kernel, frames),
            "cross",
            shape_of((frames * half + TAIL, inner), BF16),
            [ANY, SCALAR] + [WHOLE] * 4,
        )(reach, band, total, first, near, far_decays)
        second = crossed(message, "height", 4, 2)
        results = call(
            functools.partial(settle_kernel, frames),
            "settle",
            [shape_of((frames * half, inner), BF16)] * 2,
            [ANY, SCALAR] + [WHOLE] * 6,
        )(reach, band, first, second, near, far_decays, own, far)
        distance = bands
    while distance < bands:
        far_total = swapped(total, "height", distance)
        finish = distance * 2 >= bands
        operands = [reach, band, total, far_total] + before + ([own, far] if finish else [])
        outs = (
            [shape_of((frames * half, inner), BF16)] * 2
            if finish
            else [
                shape_of((frames * half + TAIL, inner), BF16),
                shape_of((frames * half + 8, inner), F32),
            ]
        )
        results = call(
            functools.partial(merge_kernel, frames, distance, finish),
            "merge",
            outs,
            [ANY, SCALAR] + [WHOLE] * (len(operands) - 2),
        )(*operands)
        if not finish:
            total, before = results[0], [results[1]]
        distance *= 2
    keep, give = results
    came = swapped(give, "height", 1)

    spatial_out = call(
        functools.partial(incoming_kernel, frames, rows, columns, head_dim),
        "spatial_incoming",
        shape_of((count, inner), F32),
        [SCALAR] + [WHOLE] * 5,
    )(band, out_local, bc_own, reach, keep, came)

    returned, carried = [], []
    for part in range(parts):
        more = [shape_of((state, group), F32)] if part + 1 < parts else []
        results = call(
            functools.partial(
                temporal_kernel,
                part,
                parts,
                per_group,
                head_dim,
                rows,
                frames,
                columns,
                chunk_cols,
                shares,
                state,
            ),
            "temporal",
            [shape_of((part_len, group), BF16)] * shares + more,
            [SCALAR] + [WHOLE] * (2 + len(carried)) + [ANY] * part,
            scratch_shapes=[
                pltpu.VMEM((shares, part_len, state), BF16),
                pltpu.VMEM((shares, part_len, state), BF16),
                pltpu.VMEM((shares, part_len, LANES), F32),
                pltpu.VMEM((shares, part_len, LANES), F32),
            ],
        )(here, params, received, *carried, *([spatial_out] * part))
        returned.append(sent(results[:shares]))
        carried = results[shares:]

    mixed = []
    for part in range(parts):
        mixed = [
            call(
                functools.partial(exit_kernel, part, parts, shares),
                "exit",
                shape_of(tokens.shape, BF16),
                [SCALAR] + [WHOLE] * (4 + shares) + [HBM] * len(mixed),
                outs=HBM,
                scratch_shapes=[
                    pltpu.VMEM((shares, part_len, group), BF16),
                    pltpu.VMEM((rows * part_len, inner), BF16),
                    pltpu.VMEM((rows * part_len, width), BF16),
                    pltpu.SemaphoreType.DMA((2 * rows * frames,)),
                ],
                input_output_aliases={5 + shares: 0} if mixed else {},
            )(here, spatial_out, gate, out_gain, out_weight, *returned[part], *mixed)
        ]
    return mixed[0]


def solution(mesh):
    in_specs = (P("tm", "height", None, None), P(), P(), P(), P(), P(), P(), P(), P())
    out_specs = P("tm", "height", None, None)
    return jax.shard_map(
        per_device, mesh=mesh, in_specs=in_specs, out_specs=out_specs, check_vma=False
    )
```

```python
import functools
import math

import jax
import jax.numpy as jnp
from jax import lax
from jax.experimental import pallas as pl
from jax.experimental.pallas import tpu as pltpu
from jax.sharding import PartitionSpec as P

EPSILON = 1e-05
LANES = 128
TAIL = 16
LOG2_E = 1.4426950408889634
F32 = jnp.float32
BF16 = jnp.bfloat16
EXACT = lax.Precision.HIGHEST
LARGE = 56 * 1024 * 1024
SMALL = 24 * 1024 * 1024

ANY = pl.BlockSpec(memory_space=pl.ANY)
HBM = pl.BlockSpec(memory_space=pltpu.HBM)
SCALAR = pl.BlockSpec(memory_space=pltpu.SMEM)
WHOLE = pl.BlockSpec(memory_space=pltpu.VMEM)


def call(kernel, name, out_shape, in_specs, limit=SMALL, outs=None, **options):
    return pl.pallas_call(
        kernel,
        out_shape=out_shape,
        in_specs=in_specs,
        out_specs=jax.tree.map(lambda _: WHOLE, out_shape) if outs is None else outs,
        compiler_params=pltpu.CompilerParams(vmem_limit_bytes=limit),
        cost_estimate=pl.CostEstimate(flops=1, bytes_accessed=1, transcendentals=0),
        name=name,
        **options,
    )


def shape_of(shape, dtype):
    return jax.ShapeDtypeStruct(shape, dtype)


def dot(left, right, **options):
    return jnp.dot(left, right, preferred_element_type=F32, **options)


def dot_tn(left, right):
    return lax.dot_general(left, right, (((0,), (0,)), ((), ())), preferred_element_type=F32)


def dot_nt(left, right):
    return lax.dot_general(left, right, (((1,), (1,)), ((), ())), preferred_element_type=F32)


def softplus(values):
    return jnp.maximum(values, 0.0) + jnp.log1p(jnp.exp(-jnp.abs(values)))


def iota(shape, dim):
    return lax.broadcasted_iota(jnp.int32, shape, dim)


def spread_matrix(first_head, width, head_dim):
    return (iota((LANES, width), 0) - first_head == iota((LANES, width), 1) // head_dim).astype(BF16)


def spread(values, matrix):
    high = values.astype(BF16)
    low = (values - high.astype(F32)).astype(BF16)
    return dot(high, matrix) + dot(low, matrix)


def head_mixes(scores, running, running_t, dt_t, x, first_head, heads, head_dim):
    length = scores.shape[0]
    running, running_t = running * LOG2_E, running_t * LOG2_E
    outs = []

    def weights(head):
        spreads = running[:, head : head + 1] - running_t[head : head + 1, :]
        return (scores * jnp.exp2(jnp.minimum(spreads, 0.0)) * dt_t[head : head + 1, :]).astype(BF16)

    head = 0
    while head < heads:
        here = first_head + head
        if head + 1 < heads and 2 * head_dim == LANES:
            both = x[:, head * head_dim : (head + 2) * head_dim]
            first = iota((length, LANES), 1) < head_dim
            zero = jnp.zeros_like(both)
            stacked = jnp.concatenate([jnp.where(first, both, zero), jnp.where(first, zero, both)], axis=0)
            pair = jnp.concatenate([weights(here), weights(here + 1)], axis=1)
            outs.append(dot(pair, stacked))
            head += 2
        else:
            outs.append(dot(weights(here), x[:, head * head_dim : (head + 1) * head_dim]))
            head += 1
    return outs[0] if len(outs) == 1 else jnp.concatenate(outs, axis=1)


def column_copies(weight, scratch, sems, first, offset, blocks):
    width = scratch.shape[1] // blocks
    return [
        pltpu.make_async_copy(
            weight.at[:, pl.ds(offset + index * width, width)],
            scratch.at[:, pl.ds(index * width, width)],
            sems.at[first + index],
        )
        for index in range(blocks)
    ]


def rank_of(device):
    return device ^ (device >> 1)


def packing(length, group):
    columns = group // LANES
    rest = -(-(2 * length + TAIL) // columns)
    return length, -(-rest // TAIL) * TAIL


def pack_rest(ref, length, b_proj, c_proj, dt):
    columns, rest = ref.shape[1] // LANES, ref.shape[0] - length
    blank = jnp.zeros((columns * rest - 2 * length - TAIL, LANES), BF16)
    stacked = jnp.concatenate([b_proj, c_proj, dt, blank], axis=0)
    for column in range(columns):
        ref[length:, column * LANES : (column + 1) * LANES] = stacked[column * rest : (column + 1) * rest]


def unpacked_rest(ref, length):
    columns = ref.shape[1] // LANES
    stacked = jnp.concatenate(
        [ref[length:, column * LANES : (column + 1) * LANES] for column in range(columns)], axis=0
    )
    return stacked[:length], stacked[length : 2 * length], stacked[2 * length : 2 * length + TAIL]


def entry_kernel(shares, heads, state, blocks, *refs):
    here_ref, band, tokens, gain, bias, rates, dt_weight, bc_weight, weight = refs[:9]
    normed_out, payload_out, bc_own, logits, params, own_states, other_states, band_decays = refs[9:17]
    held, dt_held, bc_held, held_weight, table, normed, payload, sems, out_sems = refs[17:]
    frames, rows, columns, width = tokens.shape
    length = frames * columns
    count = rows * length
    groups = shares // rows
    per_group = heads // groups
    group = held_weight.shape[1] // groups

    token_copies = [
        pltpu.make_async_copy(tokens.at[frame, row], held.at[row, frame], sems.at[row * frames + frame])
        for row in range(rows)
        for frame in range(frames)
    ]
    for copy in token_copies:
        copy.start()
    first = rows * frames
    dt_copy = pltpu.make_async_copy(dt_weight, dt_held, sems.at[first])
    dt_copy.start()
    bc_copy = pltpu.make_async_copy(bc_weight, bc_held, sems.at[first + 1])
    bc_copy.start()
    copies = column_copies(weight, held_weight, sems, first + 2, 0, blocks)
    for copy in copies:
        copy.start()

    table[...] = jnp.zeros_like(table)
    table[0:1, : 2 * heads] = bias[...].reshape(1, 2 * heads)
    table[1:2, :heads] = rates[0:1, :]
    table[1:2, heads : 2 * heads] = rates[1:2, :]
    first_head = heads + here_ref[0] // rows * per_group
    lane_in, lane_out = iota((LANES, LANES), 0), iota((LANES, LANES), 1)
    own = ((lane_in == lane_out + first_head) & (lane_out < per_group)).astype(F32)
    params[0:8, :] = table[...]
    params[8:16, :] = dot(table[...], own, precision=EXACT)
    logits[...] = jnp.zeros_like(logits)

    gains = gain[...].reshape(1, width)
    for index, copy in enumerate(token_copies):
        copy.wait()
        values = held[index // frames, index % frames].astype(F32)
        mean_square = jnp.mean(values * values, axis=-1, keepdims=True)
        normed[index * columns : (index + 1) * columns, :] = (
            values * lax.rsqrt(mean_square + EPSILON) * gains
        ).astype(BF16)
    outgoing = [pltpu.make_async_copy(normed, normed_out, out_sems.at[0])]
    outgoing[0].start()
    dt_copy.wait()
    logits[:, : 2 * heads] = dot_nt(normed[...], dt_held[...]).astype(BF16).astype(F32)
    dt_heads = jnp.transpose(logits[...]).astype(BF16)[heads : 2 * heads + TAIL]
    bc_copy.wait()
    bc = dot(normed[...], bc_held[...]).astype(BF16)
    bc_own[...] = bc[:, : 2 * state]
    scan = [
        end_factors(frame_of(logits, frame, rows, frames, columns), params, rows * columns)
        for frame in range(frames)
    ]

    block = held_weight.shape[1] // blocks
    for index, copy in enumerate(copies):
        copy.wait()
        at = index * block
        values = dot(normed[...], held_weight[:, at : at + block]).astype(BF16)
        for inside in range(0, block, group):
            part = (at + inside) // group
            for row in range(rows):
                piece = rank_of(part * rows + row)
                here = slice(row * length, (row + 1) * length)
                payload[piece, :length, :] = values[here, inside : inside + group]
                pack_rest(
                    payload.at[piece],
                    length,
                    bc[here, 2 * state : 3 * state],
                    bc[here, 3 * state :],
                    dt_heads[part * per_group : part * per_group + TAIL, here],
                )
                outgoing.append(
                    pltpu.make_async_copy(
                        payload.at[piece], payload_out.at[piece], out_sems.at[1 + piece]
                    )
                )
                outgoing[-1].start()
    half = state // 2
    head_dim = groups * group // heads
    mine = band[0] % 2 == 0
    matrix = spread_matrix(0, groups * group, head_dim)
    factors = dot(jnp.concatenate([factor for factor, _ in scan], axis=0), matrix)
    span = rows * columns
    for frame in range(frames):
        b_proj = frame_of(bc_own, frame, rows, frames, columns)[:, :state]
        values = jnp.concatenate(
            [frame_x(payload, part, frame, rows, columns) for part in range(groups)], axis=1
        )
        scaled = (values.astype(F32) * factors[frame * span : (frame + 1) * span]).astype(BF16)
        fresh = dot_tn(b_proj, scaled).astype(BF16)
        at_rows = slice(frame * half, (frame + 1) * half)
        own_states[at_rows, :] = jnp.where(mine, fresh[:half], fresh[half:])
        other_states[at_rows, :] = jnp.where(mine, fresh[half:], fresh[:half])
    whole = [decay for _, decay in scan] + [jnp.zeros((8 - frames, LANES), F32)]
    decays = spread(jnp.concatenate(whole, axis=0), matrix)
    tail = tail_of(decays)
    own_states[frames * half :, :] = tail
    other_states[frames * half :, :] = tail
    band_decays[...] = tail
    for copy in outgoing:
        copy.wait()


def gate_kernel(blocks, after, normed, weight, out, held_weight, sems):
    inner = held_weight.shape[1]
    copies = column_copies(weight, held_weight, sems, 0, inner, blocks)
    for copy in copies:
        copy.start()
    block = inner // blocks
    for index, copy in enumerate(copies):
        copy.wait()
        at = slice(index * block, (index + 1) * block)
        gates = dot(normed[...], held_weight[:, at]).astype(BF16).astype(F32)
        out[:, at] = (gates / (1.0 + jnp.exp(-gates))).astype(BF16)


def frame_of(ref, frame, rows, frames, columns):
    return jnp.concatenate(
        [
            ref[(row * frames + frame) * columns : (row * frames + frame + 1) * columns, :]
            for row in range(rows)
        ],
        axis=0,
    )


def frame_x(payload, part, frame, rows, columns):
    return jnp.concatenate(
        [
            payload[rank_of(part * rows + row), frame * columns : (frame + 1) * columns, :]
            for row in range(rows)
        ],
        axis=0,
    )


def scan_terms(logits, params, causal):
    dt = softplus(logits + params[0:1, :])
    running = dot(causal.astype(F32), -dt * params[1:2, :], precision=EXACT)
    return dt, running, jnp.min(running, axis=0, keepdims=True)


def end_factors(logits, params, length):
    causal = iota((length, length), 0) >= iota((length, length), 1)
    dt, running, last = scan_terms(logits, params, causal)
    return (jnp.exp(last - running) * dt).astype(BF16), jnp.exp(last)


def local_kernel(frames, rows, columns, head_dim, groups, *refs):
    after, bc, logits, params, x, out, reach = refs
    length = rows * columns
    group = x.shape[2]
    state = bc.shape[1] // 2
    per_group = group // head_dim
    causal = iota((length, length), 0) >= iota((length, length), 1)

    def stored(ref, values, frame, at):
        for row in range(rows):
            to = (row * frames + frame) * columns
            ref[to : to + columns, at] = values[row * columns : (row + 1) * columns]

    for frame in range(frames):
        dt, running, _ = scan_terms(frame_of(logits, frame, rows, frames, columns), params, causal)
        running_t, dt_t = jnp.transpose(running), jnp.transpose(dt)
        bc_rows = frame_of(bc, frame, rows, frames, columns)
        scores = jnp.where(causal, dot_nt(bc_rows[:, state:], bc_rows[:, :state]), 0.0)
        stored(reach, jnp.exp(running), frame, slice(None))
        for piece in range(groups):
            values = frame_x(x, piece, frame, rows, columns)
            mixed = head_mixes(
                scores, running, running_t, dt_t, values, piece * per_group, per_group, head_dim
            )
            stored(out, mixed.astype(BF16), frame, slice(piece * group, (piece + 1) * group))


def tail_of(decays):
    high = decays.astype(BF16)
    return jnp.concatenate([high, (decays - high.astype(F32)).astype(BF16)], axis=0)


def pair_kernel(frames, band, own, far, total):
    rows = (own.shape[0] - TAIL) // frames
    own_decay = own[-TAIL:-8, :].astype(F32) + own[-8:, :].astype(F32)
    far_decay = far[-TAIL:-8, :].astype(F32) + far[-8:, :].astype(F32)
    lower = band[0] % 2 == 0
    through = jnp.where(lower, far_decay, own_decay)
    for frame in range(frames):
        at = slice(frame * rows, (frame + 1) * rows)
        first = jnp.where(lower, own[at, :], far[at, :]).astype(F32)
        second = jnp.where(lower, far[at, :], own[at, :]).astype(F32)
        total[at, :] = (through[frame : frame + 1, :] * first + second).astype(BF16)
    total[frames * rows :, :] = tail_of(own_decay * far_decay)


def merge_kernel(frames, distance, finish, *refs):
    _, band, own, far = refs[:4]
    start = distance == 2
    rest = list(refs[4:])
    before_in = None if start else rest.pop(0)
    band_own, band_far = (rest.pop(0), rest.pop(0)) if finish else (None, None)
    rows = (own.shape[0] - TAIL) // frames
    upper, lower_band = (band[0] // distance) % 2 == 1, band[0] % 2 == 0
    own_decay = own[-TAIL:-8, :].astype(F32) + own[-8:, :].astype(F32)
    far_decay = far[-TAIL:-8, :].astype(F32) + far[-8:, :].astype(F32)
    if start:
        before_decay = jnp.ones_like(own_decay)
    else:
        before_decay = before_in[-8:, :]
    if finish:
        first_decay = jnp.where(
            lower_band,
            band_own[-TAIL:-8, :].astype(F32) + band_own[-8:, :].astype(F32),
            band_far[-TAIL:-8, :].astype(F32) + band_far[-8:, :].astype(F32),
        )
    through = jnp.where(upper, own_decay, far_decay)
    for frame in range(frames):
        at = slice(frame * rows, (frame + 1) * rows)
        row = slice(frame, frame + 1)
        far_state = far[at, :].astype(F32)
        came = before_decay[row, :] * far_state
        if not start:
            came = came + before_in[at, :]
        before = jnp.where(upper, came, 0.0 if start else before_in[at, :])
        if finish:
            keep, give = rest
            first = jnp.where(lower_band, band_own[at, :], band_far[at, :]).astype(F32)
            after = first_decay[row, :] * before + first
            keep[at, :] = jnp.where(lower_band, before, after).astype(BF16)
            give[at, :] = jnp.where(lower_band, after, before).astype(BF16)
        else:
            total, before_out = rest
            own_state = own[at, :].astype(F32)
            early = jnp.where(upper, far_state, own_state)
            late = jnp.where(upper, own_state, far_state)
            total[at, :] = (through[row, :] * early + late).astype(BF16)
            before_out[at, :] = before
    if not finish:
        total[frames * rows :, :] = tail_of(own_decay * far_decay)
        before_out[frames * rows :, :] = jnp.where(upper, before_decay * far_decay, before_decay)


def decays_of(ref):
    return ref[-TAIL:-8, :].astype(F32) + ref[-8:, :].astype(F32)


def places_of(band):
    return band % 2 == 0, (band // 2) % 2 == 1, band // 4 == 1


def cross_kernel(frames, _, band, total, first, near, far, message):
    even, x_high, y_high = places_of(band[0])
    own_decay, first_decay = decays_of(total), decays_of(first)
    diagonal = decays_of(near) * decays_of(far)
    one, zero = jnp.ones_like(own_decay), jnp.zeros_like(own_decay)
    odd_first = jnp.where(y_high, jnp.where(x_high, one, own_decay * diagonal), zero)
    odd_own = jnp.where(x_high & y_high, zero, one)
    of_first = jnp.where(even, jnp.where(x_high, own_decay, one), odd_first)
    of_own = jnp.where(even, jnp.where(x_high, one, first_decay), odd_own)
    rows = (total.shape[0] - TAIL) // frames
    for frame in range(frames):
        at, row = slice(frame * rows, (frame + 1) * rows), slice(frame, frame + 1)
        sent = of_first[row] * first[at, :].astype(F32) + of_own[row] * total[at, :].astype(F32)
        message[at, :] = sent.astype(BF16)
    message[frames * rows :, :] = tail_of(jnp.where(even, own_decay * first_decay, own_decay))


def settle_kernel(frames, _, band, first, second, near, far, band_own, band_far, keep, give):
    even, x_high, y_high = places_of(band[0])
    first_decay, second_decay = decays_of(first), decays_of(second)
    diagonal = decays_of(near) * decays_of(far)
    one, zero = jnp.ones_like(first_decay), jnp.zeros_like(first_decay)
    even_second = jnp.where(y_high, jnp.where(x_high, first_decay, one), zero)
    odd_second = jnp.where(x_high | y_high, one, zero)
    odd_first = jnp.where(y_high, jnp.where(x_high, second_decay, diagonal), zero)
    of_second = jnp.where(even, even_second, odd_second)
    of_first = jnp.where(even, jnp.where(x_high, one, zero), odd_first)
    band_decay = jnp.where(even, decays_of(band_own), decays_of(band_far))
    rows = keep.shape[0] // frames
    for frame in range(frames):
        at, row = slice(frame * rows, (frame + 1) * rows), slice(frame, frame + 1)
        before = of_second[row] * second[at, :].astype(F32) + of_first[row] * first[at, :].astype(F32)
        lower = jnp.where(even, band_own[at, :], band_far[at, :]).astype(F32)
        after = band_decay[row] * before + lower
        keep[at, :] = jnp.where(even, before, after).astype(BF16)
        give[at, :] = jnp.where(even, after, before).astype(BF16)


def incoming_kernel(frames, rows, columns, head_dim, band, out_local, bc, reach, own, other, out):
    state = bc.shape[1] // 2
    half = state // 2
    inner = out.shape[1]
    mine = band[0] % 2 == 0
    matrix = spread_matrix(0, inner, head_dim)
    for frame in range(frames):
        at = slice(frame * half, (frame + 1) * half)
        low = jnp.where(mine, own[at, :], other[at, :])
        high = jnp.where(mine, other[at, :], own[at, :])
        carried = jnp.concatenate([low, high], axis=0)
        for row in range(rows):
            to = (row * frames + frame) * columns
            here = slice(to, to + columns)
            factor = spread(reach[here, :], matrix)
            out[here, :] = out_local[here, :].astype(F32) + factor * dot(bc[here, state:], carried)


def temporal_kernel(
    part, parts, per_group, head_dim, rows, frames, columns, chunk_cols, shares, state, *refs
):
    here_ref, params, payload = refs[:3]
    rest = list(refs[3:])
    carried_in = rest.pop(0) if part > 0 else None
    del rest[:part]
    outs, rest = rest[:shares], rest[shares:]
    carried_out = rest.pop(0) if part + 1 < parts else None
    b_all, c_all, dt_all, decay_all = rest
    here = here_ref[0]
    length = frames * columns
    part_cols = columns // parts
    group = outs[0].shape[1]
    eye = (iota((TAIL, LANES), 0) == iota((TAIL, LANES), 1)) & (iota((TAIL, LANES), 1) < per_group)
    eye = eye.astype(BF16)

    def came(distance):
        return payload.at[rank_of(here ^ distance)]

    for distance in range(shares):
        b_proj, c_proj, logits = unpacked_rest(came(distance), length)
        logits = dot_tn(logits, eye)
        for frame in range(frames):
            at = slice(frame * columns + part * part_cols, frame * columns + (part + 1) * part_cols)
            to = slice(frame * part_cols, (frame + 1) * part_cols)
            b_all[distance, to] = b_proj[at]
            c_all[distance, to] = c_proj[at]
            dt = softplus(logits[at] + params[8:9, :])
            dt_all[distance, to] = dt
            decay_all[distance, to] = -dt * params[9:10, :]

    all_frames = shares * frames
    size = all_frames * chunk_cols

    def order_key(dim):
        index = iota((size, size), dim)
        source = here ^ (index // (frames * chunk_cols))
        frame = source * frames + (index // chunk_cols) % frames
        return (index % chunk_cols) * all_frames + frame

    causal = order_key(0) >= order_key(1)
    order = causal.astype(F32)
    matrix = spread_matrix(0, group, head_dim)
    carried = jnp.zeros((state, group), F32) if part == 0 else carried_in[...]
    places = [(source, frame) for source in range(shares) for frame in range(frames)]
    for chunk in range(part_cols // chunk_cols):

        def gathered(ref_of, pitch=part_cols, offset=0):
            return jnp.concatenate(
                [
                    ref_of(source)[pl.ds(frame * pitch + offset + chunk * chunk_cols, chunk_cols), :]
                    for source, frame in places
                ],
                axis=0,
            )

        values = gathered(came, columns, part * part_cols)
        b_proj = gathered(lambda source: b_all.at[source])
        c_proj = gathered(lambda source: c_all.at[source])
        dt = gathered(lambda source: dt_all.at[source])
        running = dot(order, gathered(lambda source: decay_all.at[source]), precision=EXACT)
        running_t, dt_t = jnp.transpose(running), jnp.transpose(dt)
        scores = jnp.where(causal, dot_nt(c_proj, b_proj), 0.0)
        last = jnp.min(running, axis=0, keepdims=True)
        mixed = head_mixes(scores, running, running_t, dt_t, values, 0, per_group, head_dim)
        ends = jnp.concatenate([running, jnp.broadcast_to(last, (8, LANES))], axis=0)
        to_end = jnp.exp(last - running) * dt
        factors = dot(jnp.concatenate([jnp.exp(ends), to_end], axis=0).astype(BF16), matrix)
        mixed = mixed + factors[:size] * dot(c_proj, carried.astype(BF16))
        scaled = (values.astype(F32) * factors[size + 8 :]).astype(BF16)
        carried = factors[size : size + 1, :] * carried + dot_tn(b_proj, scaled)
        mixed = mixed.astype(BF16)
        for index, (source, frame) in enumerate(places):
            to = frame * part_cols + chunk * chunk_cols
            outs[source][to : to + chunk_cols, :] = mixed[index * chunk_cols : (index + 1) * chunk_cols]
    if carried_out is not None:
        carried_out[...] = carried


def exit_kernel(part, parts, shares, *refs):
    here, spatial, gate, gain, weight = refs[:5]
    out, temporal, normed, mixed, sems = refs[-5:]
    frames, rows, columns, _ = out.shape
    part_cols = columns // parts
    _, part_len, group = temporal.shape
    groups = shares // rows
    inner = groups * group
    for index in range(shares):
        distance = (shares - index) % shares
        temporal[here[0] ^ distance] = refs[5 + index][...]

    def own(ref, row, at):
        return jnp.concatenate(
            [
                ref[pl.ds((row * frames + frame) * columns + part * part_cols, part_cols), at]
                for frame in range(frames)
            ],
            axis=0,
        )

    gains = gain[...].reshape(1, inner)
    for row in range(rows):
        total = jnp.zeros((part_len, 1), F32)
        kept = []
        for index in range(groups):
            at = slice(index * group, (index + 1) * group)
            gated = own(spatial, row, at) + temporal[index * rows + row].astype(F32)
            gated = gated * own(gate, row, at).astype(F32)
            total = total + jnp.sum(gated * gated, axis=1, keepdims=True)
            kept.append(gated)
        scale = lax.rsqrt(total / inner + EPSILON)
        for index, gated in enumerate(kept):
            at = slice(index * group, (index + 1) * group)
            normed[row * part_len : (row + 1) * part_len, at] = (gated * scale * gains[:, at]).astype(BF16)
    copies = []
    width = mixed.shape[1] // 2
    for side in range(2):
        cols = pl.ds(side * width, width)
        mixed[:, side * width : (side + 1) * width] = dot(
            normed[...], weight[:, side * width : (side + 1) * width]
        ).astype(BF16)
        for row in range(rows):
            for frame in range(frames):
                copies.append(
                    pltpu.make_async_copy(
                        mixed.at[pl.ds((row * frames + frame) * part_cols, part_cols), cols],
                        out.at[frame, row, pl.ds(part * part_cols, part_cols), cols],
                        sems.at[len(copies)],
                    )
                )
                copies[-1].start()
    for copy in copies:
        copy.wait()


def swapped(value, axis, distance):
    count = lax.axis_size(axis)
    return lax.ppermute(value, axis, [(source, source ^ distance) for source in range(count)])


def crossed(value, axis, even, odd):
    count = lax.axis_size(axis)
    pairs = [(source, source ^ (odd if source % 2 else even)) for source in range(count)]
    return lax.ppermute(value, axis, pairs)


def per_device(
    tokens, norm_gain, in_weight, bc_weight, dt_weight, dt_bias, decay_rate, out_gain, out_weight
):
    frames, rows, columns, width = tokens.shape
    heads = decay_rate.shape[1]
    inner = out_weight.shape[0]
    head_dim = inner // heads
    state = bc_weight.shape[1] // 4
    shares = lax.axis_size("tm")
    bands = lax.axis_size("height")
    groups = shares // rows
    group = inner // groups
    per_group = heads // groups
    length = frames * columns
    count = rows * length
    half = state // 2
    chunk_cols = 16
    blocks = parts = 2
    part_len = length // parts
    here = lax.axis_index("tm").astype(jnp.int32).reshape(1)
    band = lax.axis_index("height").astype(jnp.int32).reshape(1)

    packed = (shares, sum(packing(length, group)), group)
    normed, payload, bc_own, logits, params, own, other, band_decays = call(
        functools.partial(entry_kernel, shares, heads, state, blocks),
        "entry",
        [
            shape_of((count, width), BF16),
            shape_of(packed, BF16),
            shape_of((count, 2 * state), BF16),
            shape_of((count, LANES), F32),
            shape_of((16, LANES), F32),
        ]
        + [shape_of((frames * half + TAIL, inner), BF16)] * 2
        + [shape_of((TAIL, inner), BF16)],
        [SCALAR, SCALAR, HBM, WHOLE, WHOLE, WHOLE, HBM, HBM, HBM],
        limit=LARGE,
        outs=[HBM, HBM] + [WHOLE] * 6,
        scratch_shapes=[
            pltpu.VMEM((rows, frames, columns, width), BF16),
            pltpu.VMEM((2 * heads, width), BF16),
            pltpu.VMEM((width, 4 * state), BF16),
            pltpu.VMEM((width, inner), BF16),
            pltpu.VMEM((8, LANES), F32),
            pltpu.VMEM((count, width), BF16),
            pltpu.VMEM(packed, BF16),
            pltpu.SemaphoreType.DMA((rows * frames + 2 + blocks,)),
            pltpu.SemaphoreType.DMA((1 + shares,)),
        ],
    )(here, band, tokens, norm_gain, dt_bias, decay_rate, dt_weight.T, bc_weight, in_weight)

    def sent(parts):
        moved = {d: swapped(parts[d], "tm", d) for d in range(shares - 1, 0, -1)}
        return [parts[0]] + list(moved.values())

    line = [rank_of(device) for device in range(shares)]
    received = lax.all_to_all(
        payload,
        "tm",
        split_axis=0,
        concat_axis=0,
        tiled=True,
        axis_index_groups=[[line.index(rank) for rank in range(shares)]],
    )
    far = swapped(other, "height", 1)
    gate = call(
        functools.partial(gate_kernel, blocks),
        "gate",
        shape_of((count, inner), BF16),
        [ANY, WHOLE, HBM],
        scratch_shapes=[
            pltpu.VMEM((width, inner), BF16),
            pltpu.SemaphoreType.DMA((blocks,)),
        ],
    )(payload, normed, in_weight)

    out_local, reach = call(
        functools.partial(local_kernel, frames, rows, columns, head_dim, groups),
        "spatial_local",
        [shape_of((count, inner), BF16), shape_of((count, LANES), F32)],
        [ANY] + [WHOLE] * 4,
    )(gate, bc_own, logits, params, payload)

    total = call(
        functools.partial(pair_kernel, frames),
        "pair_total",
        shape_of((frames * half + TAIL, inner), BF16),
        [SCALAR, WHOLE, WHOLE],
    )(band, own, far)
    before = []
    distance = 2
    if bands == 8:
        near, far_decays = (swapped(band_decays, "height", distance) for distance in (6, 7))
        first = crossed(total, "height", 2, 4)
        message = call(
            functools.partial(cross_kernel, frames),
            "cross",
            shape_of((frames * half + TAIL, inner), BF16),
            [ANY, SCALAR] + [WHOLE] * 4,
        )(reach, band, total, first, near, far_decays)
        second = crossed(message, "height", 4, 2)
        results = call(
            functools.partial(settle_kernel, frames),
            "settle",
            [shape_of((frames * half, inner), BF16)] * 2,
            [ANY, SCALAR] + [WHOLE] * 6,
        )(reach, band, first, second, near, far_decays, own, far)
        distance = bands
    while distance < bands:
        far_total = swapped(total, "height", distance)
        finish = distance * 2 >= bands
        operands = [reach, band, total, far_total] + before + ([own, far] if finish else [])
        outs = (
            [shape_of((frames * half, inner), BF16)] * 2
            if finish
            else [
                shape_of((frames * half + TAIL, inner), BF16),
                shape_of((frames * half + 8, inner), F32),
            ]
        )
        results = call(
            functools.partial(merge_kernel, frames, distance, finish),
            "merge",
            outs,
            [ANY, SCALAR] + [WHOLE] * (len(operands) - 2),
        )(*operands)
        if not finish:
            total, before = results[0], [results[1]]
        distance *= 2
    keep, give = results
    came = swapped(give, "height", 1)

    spatial_out = call(
        functools.partial(incoming_kernel, frames, rows, columns, head_dim),
        "spatial_incoming",
        shape_of((count, inner), F32),
        [SCALAR] + [WHOLE] * 5,
    )(band, out_local, bc_own, reach, keep, came)

    returned, carried = [], []
    for part in range(parts):
        more = [shape_of((state, group), F32)] if part + 1 < parts else []
        results = call(
            functools.partial(
                temporal_kernel,
                part,
                parts,
                per_group,
                head_dim,
                rows,
                frames,
                columns,
                chunk_cols,
                shares,
                state,
            ),
            "temporal",
            [shape_of((part_len, group), BF16)] * shares + more,
            [SCALAR] + [WHOLE] * (2 + len(carried)) + [ANY] * part,
            scratch_shapes=[
                pltpu.VMEM((shares, part_len, state), BF16),
                pltpu.VMEM((shares, part_len, state), BF16),
                pltpu.VMEM((shares, part_len, LANES), F32),
                pltpu.VMEM((shares, part_len, LANES), F32),
            ],
        )(here, params, received, *carried, *([came] * part))
        returned.append(sent(results[:shares]))
        carried = results[shares:]

    mixed = []
    for part in range(parts):
        mixed = [
            call(
                functools.partial(exit_kernel, part, parts, shares),
                "exit",
                shape_of(tokens.shape, BF16),
                [SCALAR] + [WHOLE] * (4 + shares) + [HBM] * len(mixed),
                outs=HBM,
                scratch_shapes=[
                    pltpu.VMEM((shares, part_len, group), BF16),
                    pltpu.VMEM((rows * part_len, inner), BF16),
                    pltpu.VMEM((rows * part_len, width), BF16),
                    pltpu.SemaphoreType.DMA((2 * rows * frames,)),
                ],
                input_output_aliases={5 + shares: 0} if mixed else {},
            )(here, spatial_out, gate, out_gain, out_weight, *returned[part], *mixed)
        ]
    return mixed[0]


def solution(mesh):
    in_specs = (P("tm", "height", None, None), P(), P(), P(), P(), P(), P(), P(), P())
    out_specs = P("tm", "height", None, None)
    return jax.shard_map(
        per_device, mesh=mesh, in_specs=in_specs, out_specs=out_specs, check_vma=False
    )
```
